32 devices in a mesh: section: 4 (over y, x), dp: 8 (over z, core).
Axes of the slice: x: 2, y: 2, z: 4, core: 2. Of those that a mesh axis runs over, the one named last changes fastest.
Arguments:
- lidar: bfloat16 [4, 8, 16, 16, 256], P('section', 'dp'), may hold values from -6 to 6
- context: bfloat16 [4, 8, 128, 80], P('section', 'dp'), may hold values from -60 to 60
- depth_logits: bfloat16 [4, 8, 128, 118], P('section', 'dp'), may hold values from -9 to 9
- cell_index: int32 [4, 8, 128, 118], P('section', 'dp'), may hold values from 0 to 255
- unite_weight: bfloat16 [9, 336, 256], replicated, may hold values from -0.109375 to 0.109375
- unite_gain: float32 [256], replicated, may hold values from 0.5 to 1.5
- unite_bias: float32 [256], replicated, may hold values from -3 to 3
- first_weight: bfloat16 [4, 9, 256, 256], P('section'), may hold values from -0.125 to 0.125
- second_weight: bfloat16 [4, 9, 256, 256], P('section'), may hold values from -0.125 to 0.125
- first_gain: float32 [4, 256], P('section'), may hold values from 0.5 to 1.5
- first_bias: float32 [4, 256], P('section'), may hold values from -3 to 3
- second_gain: float32 [4, 256], P('section'), may hold values from 0.5 to 1.5
- second_bias: float32 [4, 256], P('section'), may hold values from -3 to 3
- cotangent: bfloat16 [4, 8, 16, 16, 256], P(None, 'dp'), may hold values from -6 to 6
Outputs:
- activations: float32 [4, 8, 16, 16, 256], P('section', 'dp')
- grad_lidar: float32 [4, 8, 16, 16, 256], P('section', 'dp')
- grad_context: float32 [4, 8, 128, 80], P('section', 'dp')
- grad_depth_logits: float32 [4, 8, 128, 118], P('section', 'dp')
- grad_unite_weight: float32 [9, 336, 256], replicated
- grad_unite_gain: float32 [256], replicated
- grad_unite_bias: float32 [256], replicated
- grad_first_weight: float32 [4, 9, 256, 256], P('section')
- grad_second_weight: float32 [4, 9, 256, 256], P('section')
- grad_first_gain: float32 [4, 256], P('section')
- grad_first_bias: float32 [4, 256], P('section')
- grad_second_gain: float32 [4, 256], P('section')
- grad_second_bias: float32 [4, 256], P('section')
The draws below stay inside these ranges and needn't reach their ends.
Inputs may be any that keep to these rules, and one draw needn't show every extreme that they name: `cell_index`: row-major index of a cell of the 16 x 16 grid.
All inputs are finite; a program needn't handle non-finite values.
Results may differ from the reference program's by a relative error of at most 0.03.
Values may be sent and summed in bfloat16 or wider, within the bound.
A program may use at most 192 MiB of HBM per device.

```python
import jax
import jax.numpy as jnp
from jax import lax

BEV_CH = 256
LIDAR_CH = 256
CAM_CH = 80
BINS = 118
UNITED_IN = 336
GRID = 16
PIX = 128
MICRO = 4
BATCH = 8
N_SECTION = 4


def with_ends(array, stream_key, least, top_value):
    longest = array.shape.index(max(array.shape))
    spots = []
    for shift in (0, 1):
        where = [jax.random.randint(jax.random.fold_in(stream_key, axis), (), 0, length) for axis, length in enumerate(array.shape)]
        where[longest] = (where[longest] + shift) % array.shape[longest]
        spots.append(tuple(where))
    return array.at[spots[0]].set(least).at[spots[1]].set(top_value)


def levels(key, shape, shards, smallest, high):
    def one(dim, blocks):
        draws = jax.random.uniform(jax.random.fold_in(jax.random.fold_in(key, 6), dim), (blocks,), jnp.float32, smallest / len(shards), high / len(shards))
        return jnp.repeat(jnp.exp(draws), shape[dim] // blocks).reshape((-1,) + (1,) * (len(shape) - dim - 1))

    factor_of = one(*shards[0])
    for cut in shards[1:]:
        factor_of = factor_of * one(*cut)
    return factor_of


def scatter_about(key, extent, scale, limit, split=(), held_as=jnp.bfloat16):
    values = jax.random.normal(key, extent, jnp.float32) * scale
    if len(split) > 0:
        values = levels(key, extent, split, -0.22, 0.18) * values
    return jnp.clip(values, min=-limit, max=limit).astype(held_as)


def setup_inputs(seed: int = 0) -> dict:
    keys = jax.random.split(jax.random.key(seed), 15)
    return {
        "lidar": scatter_about(keys[0], (MICRO, BATCH, GRID, GRID, LIDAR_CH), 1.0, 6.0, ((0, 4), (1, 8))),
        "context": scatter_about(keys[1], (MICRO, BATCH, PIX, CAM_CH), 10.0, 60.0, ((0, 4), (1, 8))),
        "depth_logits": scatter_about(keys[2], (MICRO, BATCH, PIX, BINS), 1.5, 9.0, ((0, 4), (1, 8))),
        "cell_index": with_ends(jax.random.randint(keys[3], (MICRO, BATCH, PIX, BINS), 0, GRID * GRID), jax.random.fold_in(keys[3], 1), 0, (GRID * GRID) - 1).astype(jnp.int32),
        "unite_weight": scatter_about(keys[4], (9, UNITED_IN, BEV_CH), (9 * UNITED_IN) ** -0.5, 0.109375),
        "unite_gain": jnp.clip(1.0 + 0.1 * jax.random.normal(keys[5], (BEV_CH,), jnp.float32), 0.5, 1.5),
        "unite_bias": scatter_about(keys[6], (BEV_CH,), 0.5, 3.0, (), jnp.float32),
        "first_weight": scatter_about(keys[7], (N_SECTION, 9, BEV_CH, BEV_CH), (9 * BEV_CH) ** -0.5, 0.125, ((0, 4),)),
        "second_weight": scatter_about(keys[8], (N_SECTION, 9, BEV_CH, BEV_CH), (9 * BEV_CH) ** -0.5, 0.125, ((0, 4),)),
        "first_gain": jnp.clip(1.0 + 0.1 * jax.random.normal(keys[9], (N_SECTION, BEV_CH), jnp.float32), 0.5, 1.5),
        "first_bias": scatter_about(keys[10], (N_SECTION, BEV_CH), 0.5, 3.0, ((0, 4),), jnp.float32),
        "second_gain": jnp.clip(1.0 + 0.1 * jax.random.normal(keys[11], (N_SECTION, BEV_CH), jnp.float32), 0.5, 1.5),
        "second_bias": scatter_about(keys[12], (N_SECTION, BEV_CH), 0.5, 3.0, ((0, 4),), jnp.float32),
        "cotangent": scatter_about(keys[13], (MICRO, BATCH, GRID, GRID, BEV_CH), 1.0, 6.0, ((1, 8),)),
    }


eps = 1e-05

@jax.custom_vjp
def low(v):
    return lax.optimization_barrier(v.astype(jnp.bfloat16)).astype(jnp.float32)

@jax.custom_vjp
def low_back(v):
    return v

def low_keep(v):
    return (low(v), None)

def low_pass(kept, grad):
    return (grad,)

def back_keep(v):
    return (v, None)

def back_low(kept, grad):
    return (low(grad),)
low.defvjp(low_keep, low_pass)
low_back.defvjp(back_keep, back_low)

def conv_apply(inputs, kernel):
    padded = jnp.pad(inputs, ((0, 0), (1, 1), (1, 1), (0, 0)))
    total = None
    for stencil in range(9):
        vertical, lateral = divmod(stencil, 3)
        window = padded[:, vertical:vertical + GRID, lateral:lateral + GRID]
        term = jnp.einsum('nhwc,cd->nhwd', window, kernel[stencil], precision=lax.Precision.HIGHEST)
        total = term if total is None else total + term
    return total

def batch_norm(activ, gain, bias):
    center = lax.optimization_barrier(jnp.mean(activ, axis=(0, 1, 2)))
    spread = lax.optimization_barrier(jnp.mean((activ - center) ** 2, axis=(0, 1, 2)))
    return gain * (activ - center) * lax.rsqrt(spread + eps) + bias

def lift_sample(pieces):
    context, logits, cells = pieces
    probability = jax.nn.softmax(logits, axis=-1)
    points = low(probability[:, :, None] * context[:, None, :])
    pooled = jax.ops.segment_sum(points.reshape(-1, CAM_CH), cells.reshape(-1), num_segments=GRID * GRID)
    return pooled.reshape(GRID, GRID, CAM_CH)

def micro_batch(params, pieces):
    lidar, context, logits, cells = pieces
    unite_weight, unite_gain, unite_bias, first_weight, second_weight, first_gain, first_bias, second_gain, second_bias = params
    pooled = lax.map(jax.checkpoint(lift_sample), (context, logits, cells))
    joined = jnp.concatenate([lidar, low(pooled)], axis=-1)
    activ = low_back(conv_apply(joined, unite_weight))
    current = low(low_back(jax.nn.silu(batch_norm(activ, unite_gain, unite_bias))))
    for section in range(N_SECTION):
        first = low_back(conv_apply(current, first_weight[section]))
        hidden = low(jax.nn.silu(batch_norm(first, first_gain[section], first_bias[section])))
        second = low_back(conv_apply(hidden, second_weight[section]))
        result = current + jax.nn.silu(batch_norm(second, second_gain[section], second_bias[section]))
        current = low(low_back(result)) if section + 1 < N_SECTION else result
    return current

def reference(lidar, context, depth_logits, cell_index, unite_weight, unite_gain, unite_bias, first_weight, second_weight, first_gain, first_bias, second_gain, second_bias, cotangent):
    primals = tuple((value.astype(jnp.float32) for value in (lidar, context, depth_logits, unite_weight, unite_gain, unite_bias, first_weight, second_weight, first_gain, first_bias, second_gain, second_bias)))

    def forward(lidar_in, context_in, logits_in, *params):

        def per_micro(pieces):
            return micro_batch(params, pieces)
        return lax.map(jax.checkpoint(per_micro), (lidar_in, context_in, logits_in, cell_index))
    result, pullback = jax.vjp(forward, *primals)
    grads = pullback(cotangent.astype(jnp.float32))
    return (result, grads[0], grads[1], grads[2], grads[3], grads[4], grads[5], grads[6], grads[7], grads[8], grads[9], grads[10], grads[11])
```

```python
import functools

import jax
import jax.numpy as jnp
from jax import lax
from jax.experimental import pallas as pl
from jax.experimental.pallas import tpu as pltpu
from jax.sharding import PartitionSpec as P

eps = 1e-05
f32, bf16 = jnp.float32, jnp.bfloat16
MESH = pl.DeviceIdType.MESH
side = 16
cells = side * side
transposed_rhs = (((1,), (1,)), ((), ()))
transposed_lhs = (((0,), (0,)), ((), ()))


def sigmoid(value):
    return 0.5 * jnp.tanh(0.5 * value) + 0.5


def slope(value):
    gate = sigmoid(value)
    return gate * (1.0 + value * (1.0 - gate))


def put_shifted(buffer, value, stride, offset=0):
    column = lax.broadcasted_iota(jnp.int32, (cells, 1), 0) % side
    width = value.shape[1]
    before = jnp.where(column == 0, 0.0, pltpu.roll(value, 1, 0))
    after = jnp.where(column == side - 1, 0.0, pltpu.roll(value, cells - 1, 0))
    for group, shifted in enumerate((before, value, after)):
        start = group * stride + offset
        buffer[side : side + cells, start : start + width] = shifted.astype(bf16)


def total_of(terms):
    total = None
    for term in terms:
        total = term if total is None else total + term
    return total


def conv(buffer, weight):
    return total_of(
        jnp.dot(buffer[side * i : side * i + cells, :], weight(i), preferred_element_type=f32) for i in range(3)
    )


def conv_transposed(buffer, weight, width):
    return total_of(
        lax.dot_general(
            buffer[side * (2 - i) : side * (2 - i) + cells, width * (2 - j) : width * (3 - j)],
            weight(3 * i + j),
            transposed_rhs,
            preferred_element_type=f32,
        )
        for i in range(3)
        for j in range(3)
    )


def kernel(
    peers,
    lidar_ref, context_ref, logit_ref, cell_ref, unite_ref, unite_gain, unite_bias, first_ref, second_ref,
    first_gain, first_bias, second_gain, second_bias, cotangent_ref,
    act_ref, lidar_grad, context_grad, logit_grad, unite_grad, first_grad, second_grad, sums_ref,
    joined, shifted, current, kept, normed, scales, held, mine, slots, probability, cell_wide, turned, histogram,
    send_sem, recv_sem,
):
    me = lax.axis_index("dp")
    blocks = first_ref.shape[0]
    channels = current.shape[1]
    bins = logit_ref.shape[1]
    cam = context_ref.shape[1]
    united_in = channels + cam
    count = float(peers * cells)

    barrier = pltpu.get_barrier_semaphore()
    for step in range(1, peers):
        pl.semaphore_signal(barrier, inc=1, device_id={"dp": lax.rem(me + step, peers)}, device_id_type=MESH)
    pl.semaphore_wait(barrier, peers - 1)

    def copy_stats(stage, step):
        return pltpu.make_async_remote_copy(
            src_ref=mine.at[stage], dst_ref=slots.at[stage, me], send_sem=send_sem.at[stage], recv_sem=recv_sem.at[stage],
            device_id={"dp": lax.rem(me + step, peers)}, device_id_type=MESH,
        )

    def send_stats(stage, first, second):
        mine[stage, 0:1] = first
        mine[stage, 1:2] = second
        slots[stage, me] = mine[stage]
        for step in range(1, peers):
            copy_stats(stage, step).start()

    def wait_peers(stage, semaphore):
        part = slots.at[stage, pl.ds(0, peers - 1)]
        pltpu.make_async_copy(part, part, semaphore.at[stage]).wait()

    def take_stats(stage):
        wait_peers(stage, recv_sem)
        return slots[stage, :, 0, :], slots[stage, :, 1, :]

    def local_moments(activ):
        center = jnp.sum(activ, axis=0, keepdims=True) * (1.0 / cells)
        offsets = activ - center
        return center, jnp.sum(offsets * offsets, axis=0, keepdims=True)

    def whole_moments(stage):
        centers, squares = take_stats(stage)
        center = jnp.sum(centers, axis=0, keepdims=True) * (1.0 / peers)
        apart = centers - center
        spread = jnp.sum(squares, axis=0, keepdims=True) + cells * jnp.sum(apart * apart, axis=0, keepdims=True)
        return center, lax.rsqrt(spread * (1.0 / count) + eps)

    def normalise(stage, activ, meanwhile):
        center, square = local_moments(activ)
        held[...] = activ
        send_stats(stage, center, square)
        meanwhile()
        center, scale = whole_moments(stage)
        value = (held[...] - center) * scale
        normed[stage] = value
        scales[stage] = scale
        return value

    def silu_of(value, gain, bias):
        pre = gain * value + bias
        return pre * sigmoid(pre)

    joined[...] = jnp.zeros_like(joined)
    shifted[...] = jnp.zeros_like(shifted)
    probability[...] = jnp.zeros_like(probability)
    cell_wide[...] = jnp.zeros_like(cell_wide)

    logits = logit_ref[...].astype(f32)
    raised = jnp.exp(logits - jnp.max(logits, axis=-1, keepdims=True))
    probability[:, 0:bins] = raised / jnp.sum(raised, axis=-1, keepdims=True)
    cell_wide[:, 0:bins] = cell_ref[...]
    turned[0] = probability[...].T
    turned[1] = cell_wide[...].astype(f32).T
    address = lax.broadcasted_iota(jnp.int32, (cells, 128), 0).astype(f32)

    def add_bin(number, total):
        return total + jnp.where(turned[1, pl.ds(number, 1)] == address, turned[0, pl.ds(number, 1)], 0.0)

    counted = lax.fori_loop(0, bins, add_bin, jnp.zeros((cells, 128), f32)).astype(bf16)
    histogram[...] = counted
    pooled = jnp.dot(counted, context_ref[...], preferred_element_type=f32)

    lidar = lidar_ref[...].astype(f32)
    put_shifted(joined, lidar, 384)
    put_shifted(joined, pooled, 384, channels)
    united = total_of(
        jnp.dot(
            joined[side * i : side * i + cells, 384 * j : 384 * j + united_in],
            unite_ref[united_in * (3 * i + j) : united_in * (3 * i + j + 1), :],
            preferred_element_type=f32,
        )
        for i in range(3)
        for j in range(3)
    )

    def keep_joined():
        kept[0, 0:channels] = lidar_ref[...].astype(f32).T.astype(bf16)
        wide = jnp.concatenate([pooled, jnp.zeros((cells, 128 - cam), f32)], axis=1)
        kept[0, channels : channels + 128] = wide.T.astype(bf16)

    value = normalise(0, united, keep_joined)
    entering = silu_of(value, unite_gain[...], unite_bias[...]).astype(bf16)
    current[...] = entering.astype(f32)

    def block(s, unused):
        stage = 2 * s + 1
        inputs = current[...]
        put_shifted(shifted, inputs, channels)
        activ = conv(shifted, lambda i: first_ref[s, 3 * channels * i : 3 * channels * (i + 1), :])

        def keep_inputs():
            kept[stage, 0:channels] = current[...].T.astype(bf16)

        value = normalise(stage, activ, keep_inputs)
        hidden = silu_of(value, first_gain[pl.ds(s, 1)], first_bias[pl.ds(s, 1)]).astype(bf16).astype(f32)
        put_shifted(shifted, hidden, channels)
        activ = conv(shifted, lambda i: second_ref[s, 3 * channels * i : 3 * channels * (i + 1), :])

        def keep_hidden():
            kept[stage + 1, 0:channels] = shifted[side : side + cells, channels : 2 * channels].astype(f32).T.astype(bf16)

        value = normalise(stage + 1, activ, keep_hidden)
        output = current[...] + silu_of(value, second_gain[pl.ds(s, 1)], second_bias[pl.ds(s, 1)])
        act_ref[...] = output
        current[...] = output.astype(bf16).astype(f32)
        return 0

    lax.fori_loop(0, blocks, block, 0)

    stages = 2 * blocks + 1

    def through_norm(stage, upstream, gain, bias, meanwhile):
        value = normed[stage]
        grads = upstream * slope(gain * value + bias)
        held[...] = grads
        send_stats(stages + stage, jnp.sum(grads, axis=0, keepdims=True), jnp.sum(grads * value, axis=0, keepdims=True))
        meanwhile()
        first, second = take_stats(stages + stage)
        first = jnp.sum(first, axis=0, keepdims=True)
        second = jnp.sum(second, axis=0, keepdims=True)
        sums_ref[stage, 0:1] = first
        sums_ref[stage, 1:2] = second
        result = (gain * scales[stage]) * (held[...] - first * (1.0 / count) - normed[stage] * (second * (1.0 / count)))
        put_shifted(shifted, result.astype(bf16).astype(f32), channels)

    def weight_grad(stage, store):
        for i in range(3):
            rows = shifted[side * (2 - i) : side * (2 - i) + cells, :]
            taps = jnp.dot(kept[stage, 0:channels], rows, preferred_element_type=f32).astype(bf16)
            for j in range(3):
                store(3 * i + j, taps[:, channels * (2 - j) : channels * (3 - j)])

    def store_first(s):
        def store(tap, value):
            first_grad[s, channels * tap : channels * (tap + 1), :] = value
        return store

    def store_second(s):
        def store(tap, value):
            second_grad[s, channels * tap : channels * (tap + 1), :] = value
        return store

    current[...] = cotangent_ref[...].astype(f32)

    def block_back(back, unused):
        s = blocks - 1 - back
        stage = 2 * s + 1

        def previous():
            @pl.when(back > 0)
            def _():
                weight_grad(stage + 2, store_first(s + 1))

        through_norm(stage + 1, current[...], second_gain[pl.ds(s, 1)], second_bias[pl.ds(s, 1)], previous)
        upstream = conv_transposed(
            shifted, lambda tap: second_ref[s, channels * tap : channels * (tap + 1), :], channels
        )
        through_norm(
            stage, upstream, first_gain[pl.ds(s, 1)], first_bias[pl.ds(s, 1)],
            lambda: weight_grad(stage + 1, store_second(s)),
        )
        passed = conv_transposed(
            shifted, lambda tap: first_ref[s, channels * tap : channels * (tap + 1), :], channels
        )
        current[...] = (current[...] + passed).astype(bf16).astype(f32)
        return 0

    lax.fori_loop(0, blocks, block_back, 0)

    through_norm(0, current[...], unite_gain[...], unite_bias[...], lambda: weight_grad(1, store_first(0)))
    lidar_grad[...] = conv_transposed(
        shifted, lambda tap: unite_ref[united_in * tap : united_in * tap + channels, :], channels
    )
    pooled_grad = conv_transposed(
        shifted, lambda tap: unite_ref[united_in * tap + channels : united_in * (tap + 1), :], channels
    ).astype(bf16)
    for i in range(3):
        rows = shifted[side * (2 - i) : side * (2 - i) + cells, :]
        taps = jnp.dot(kept[0, 0:united_in], rows, preferred_element_type=f32).astype(bf16)
        for j in range(3):
            tap = 3 * i + j
            unite_grad[united_in * tap : united_in * (tap + 1), :] = taps[:, channels * (2 - j) : channels * (3 - j)]

    context_grad[...] = lax.dot_general(histogram[...], pooled_grad, transposed_lhs, preferred_element_type=f32)
    table = lax.dot_general(context_ref[...], pooled_grad, transposed_rhs, preferred_element_type=f32)
    places = cell_wide[...]
    within = lax.rem(places, 128)
    low = jnp.take_along_axis(table[:, 0:128], within, axis=1)
    high = jnp.take_along_axis(table[:, 128:256], within, axis=1)
    chance = probability[...]
    chance_grad = jnp.where(places < 128, low, high)
    logits_grad = chance * (chance_grad - jnp.sum(chance_grad * chance, axis=-1, keepdims=True))
    logit_grad[...] = logits_grad[:, 0:bins]

    def drain(number, unused):
        wait_peers(number, send_sem)
        return 0

    lax.fori_loop(0, 2 * stages, drain, 0)


def body(
    lidar, context, depth_logits, cell_index, unite_weight, unite_gain, unite_bias, first_weight, second_weight,
    first_gain, first_bias, second_gain, second_bias, cotangent,
):
    peers = lax.axis_size("dp")
    section = lax.axis_index("section")
    channels = cotangent.shape[-1]
    pixels, bins = depth_logits.shape[2:]
    cam = context.shape[-1]
    united_in = unite_weight.shape[1]

    def gathered(array):
        return lax.all_gather(array, "section", axis=0, tiled=True)

    first_all = gathered(first_weight).reshape(-1, 9 * channels, channels)
    second_all = gathered(second_weight).reshape(-1, 9 * channels, channels)
    vectors = gathered(jnp.stack([first_gain, first_bias, second_gain, second_bias], axis=1))
    blocks = first_all.shape[0]
    stages = 2 * blocks + 1
    cot = lax.dynamic_index_in_dim(cotangent, section, 0, keepdims=False)

    vmem = pl.BlockSpec(memory_space=pltpu.VMEM)
    shape = jax.ShapeDtypeStruct
    act, lidar_grad, context_grad, logit_grad, unite_grad, first_grad, second_grad, sums = pl.pallas_call(
        functools.partial(kernel, peers),
        out_shape=(
            shape((cells, channels), f32),
            shape((cells, channels), f32),
            shape((pixels, cam), f32),
            shape((pixels, bins), f32),
            shape((9 * united_in, channels), bf16),
            shape((blocks, 9 * channels, channels), bf16),
            shape((blocks, 9 * channels, channels), bf16),
            shape((stages, 2, channels), f32),
        ),
        in_specs=[vmem] * 14,
        out_specs=[vmem] * 8,
        scratch_shapes=[
            pltpu.VMEM((cells + 2 * side, 3 * 384), bf16),
            pltpu.VMEM((cells + 2 * side, 3 * channels), bf16),
            pltpu.VMEM((cells, channels), f32),
            pltpu.VMEM((stages, 384, cells), bf16),
            pltpu.VMEM((stages, cells, channels), f32),
            pltpu.VMEM((stages, 1, channels), f32),
            pltpu.VMEM((cells, channels), f32),
            pltpu.VMEM((2 * stages, 2, channels), f32),
            pltpu.VMEM((2 * stages, peers, 2, channels), f32),
            pltpu.VMEM((128, 128), f32),
            pltpu.VMEM((128, 128), jnp.int32),
            pltpu.VMEM((2, 128, 128), f32),
            pltpu.VMEM((cells, 128), bf16),
            pltpu.SemaphoreType.DMA((2 * stages,)),
            pltpu.SemaphoreType.DMA((2 * stages,)),
        ],
        compiler_params=pltpu.CompilerParams(
            collective_id=0, has_side_effects=True, vmem_limit_bytes=60 << 20
        ),
    )(
        lidar.reshape(cells, channels), context.reshape(pixels, cam), depth_logits.reshape(pixels, bins),
        cell_index.reshape(pixels, bins), unite_weight.reshape(-1, channels),
        unite_gain[None], unite_bias[None], first_all, second_all,
        vectors[:, 0], vectors[:, 1], vectors[:, 2], vectors[:, 3], cot.reshape(cells, channels),
    )

    whole = lax.psum(unite_grad.astype(f32), ("section", "dp"))
    first_whole = lax.psum(lax.psum_scatter(first_grad.astype(f32), "section", scatter_dimension=0, tiled=True), "dp")
    second_whole = lax.psum(lax.psum_scatter(second_grad.astype(f32), "section", scatter_dimension=0, tiled=True), "dp")
    sums = lax.psum(sums, "section")
    own = lax.dynamic_slice_in_dim(sums[1:].reshape(blocks, 2, 2, channels), section, 1, 0)
    return (
        act.reshape(lidar.shape),
        lidar_grad.reshape(lidar.shape),
        context_grad.reshape(context.shape),
        logit_grad.reshape(depth_logits.shape),
        whole.reshape(unite_weight.shape),
        sums[0, 1],
        sums[0, 0],
        first_whole.reshape(first_weight.shape),
        second_whole.reshape(second_weight.shape),
        own[:, 0, 1],
        own[:, 0, 0],
        own[:, 1, 1],
        own[:, 1, 0],
    )


def solution(mesh):
    split, by_dp = P("section"), P("section", "dp")
    in_specs = (by_dp, by_dp, by_dp, by_dp, P(), P(), P(), split, split, split, split, split, split, P(None, "dp"))
    out_specs = (by_dp, by_dp, by_dp, by_dp, P(), P(), P(), split, split, split, split, split, split)
    return jax.shard_map(body, mesh=mesh, in_specs=in_specs, out_specs=out_specs, check_vma=False)
```

```python
import functools

import jax
import jax.numpy as jnp
from jax import lax
from jax.experimental import pallas as pl
from jax.experimental.pallas import tpu as pltpu
from jax.sharding import PartitionSpec as P

eps = 1e-05
f32, bf16 = jnp.float32, jnp.bfloat16
MESH = pl.DeviceIdType.MESH
side = 16
cells = side * side
wide = 384
chips = 4
half = 128
flat_rows = 768
transposed_rhs = (((1,), (1,)), ((), ()))
transposed_lhs = (((0,), (0,)), ((), ()))


def sigmoid(value):
    return 0.5 * jnp.tanh(0.5 * value) + 0.5


def slope(value):
    gate = sigmoid(value)
    return gate * (1.0 + value * (1.0 - gate))


def silu(value):
    return value * sigmoid(value)


def put_shifted(buffer, value, stride, offset=0):
    column = lax.broadcasted_iota(jnp.int32, (cells, 1), 0) % side
    width = value.shape[1]
    before = jnp.where(column == 0, 0.0, pltpu.roll(value, 1, 0))
    after = jnp.where(column == side - 1, 0.0, pltpu.roll(value, cells - 1, 0))
    for group, shifted in enumerate((before, value, after)):
        start = group * stride + offset
        buffer[side : side + cells, start : start + width] = shifted.astype(bf16)


def total_of(terms):
    total = None
    for term in terms:
        total = term if total is None else total + term
    return total


def conv(buffer, weight):
    return total_of(
        jnp.dot(buffer[side * i : side * i + cells, :], weight(i), preferred_element_type=f32) for i in range(3)
    )


def conv_transposed(buffer, weight, width):
    return total_of(
        lax.dot_general(
            buffer[side * (2 - i) : side * (2 - i) + cells, width * (2 - j) : width * (3 - j)],
            weight(3 * i + j),
            transposed_rhs,
            preferred_element_type=f32,
        )
        for i in range(3)
        for j in range(3)
    )


def kernel(
    peers, sections,
    lidar_ref, context_ref, logit_ref, cell_ref, unite_ref, unite_gain, unite_bias, first_ref, second_ref,
    first_gain, first_bias, second_gain, second_bias, cotangent_ref,
    act_ref, lidar_grad, context_grad, logit_grad, unite_out, camera_out, first_out, second_out, sums_out,
    weights, unite_weight, vectors, joined, shifted, current, kept, normed, scales, held, gathered, upstream,
    lidars, cameras, mine, slots, unite_mine, unite_slots, probability, cell_wide, turned, histogram,
    partial, core_part, own_part, section_part, whole, flat, flat_core, flat_own, flat_section, flat_whole,
    totals, group_part, flat_group,
    local_sem, unite_send, unite_recv, stat_send, stat_recv, raw_send, raw_recv, cot_send, cot_recv,
    lidar_send, lidar_recv, camera_send, camera_recv, weight_send, weight_recv, relay_send, pass_send, pass_recv,
    vector_send, vector_recv, grad_send, grad_recv, total_send, total_recv, group_send, group_recv,
):
    me = lax.axis_index("dp")
    section = lax.axis_index("section")
    core = lax.rem(me, 2)
    chip = lax.rem(lax.div(me, 2), chips)
    group = lax.div(me, 2 * chips)
    groups = peers // (2 * chips)
    blocks = sections
    stages = 2 * blocks + 1
    channels = vectors.shape[-1]
    bins = logit_ref.shape[1]
    cam = context_ref.shape[1]
    united_in = channels + cam
    taken = 9 * channels
    row_half = lax.div(chip, 2)
    lane_half = lax.rem(chip, 2)
    count = float(peers * cells)

    def at(other_section=None, other=None):
        return (section if other_section is None else other_section, me if other is None else other)

    def chip_peer(step):
        return group * (2 * chips) + lax.rem(chip + step, chips) * 2 + core

    sibling = me + 1 - 2 * core

    def remote(source, target, send, recv, device):
        return pltpu.make_async_remote_copy(
            src_ref=source, dst_ref=target, send_sem=send, recv_sem=recv, device_id=device, device_id_type=MESH
        )

    def wait_for(part, semaphore):
        pltpu.make_async_copy(part, part, semaphore).wait()

    barrier = pltpu.get_barrier_semaphore()
    for step in range(1, sections):
        pl.semaphore_signal(
            barrier, inc=1, device_id=at(other_section=lax.rem(section + step, sections)), device_id_type=MESH
        )

    def greet(step, unused):
        pl.semaphore_signal(barrier, inc=1, device_id=at(other=lax.rem(me + step, peers)), device_id_type=MESH)
        return 0

    lax.fori_loop(1, peers, greet, 0)

    unite_copy = pltpu.make_async_copy(unite_ref, unite_weight, local_sem.at[0])
    own_first = pltpu.make_async_copy(first_ref, weights.at[2 * section], local_sem.at[1])
    own_second = pltpu.make_async_copy(second_ref, weights.at[2 * section + 1], local_sem.at[2])
    own_cot = pltpu.make_async_copy(cotangent_ref.at[section], upstream.at[chip], local_sem.at[3])
    own_lidar = pltpu.make_async_copy(lidar_ref, lidars.at[chip], local_sem.at[4])
    own_lidar.start()
    unite_copy.start()
    own_first.start()
    own_second.start()
    own_cot.start()
    for number, part in enumerate((first_gain, first_bias, second_gain, second_bias)):
        vectors[section, number : number + 1] = part[...]
    joined[...] = jnp.zeros_like(joined)
    probability[...] = jnp.zeros_like(probability)
    cell_wide[...] = jnp.zeros_like(cell_wide)
    cameras[chip] = jnp.zeros((cells, half), bf16)
    pl.semaphore_wait(barrier, peers - 1 + sections - 1)

    beside = section + 1 - 2 * lax.rem(section, 2)
    across = lax.rem(section + 2, sections)
    near = beside + core * (across - beside)
    far = across + core * (beside - across)
    part_rows = taken // 2
    part = pl.ds(pl.multiple_of(core * part_rows, part_rows), part_rows)
    sources = (first_ref, second_ref)

    def offer(which, target, number):
        index = 2 * section + which
        remote(
            sources[which].at[part], weights.at[index, part], weight_send.at[number], weight_recv.at[index],
            at(other_section=target),
        ).start()

    def arrived(index):
        wait_for(weights.at[index, part], weight_recv.at[index])

    def pass_on(index):
        remote(
            weights.at[index, part], weights.at[index, part], pass_send.at[index], pass_recv.at[index],
            at(other=sibling),
        ).start()

    def relay(block, which):
        index = 2 * block + which

        @pl.when(near == block)
        def _():
            arrived(index)
            remote(
                weights.at[index, part], weights.at[index, part], relay_send.at[which], weight_recv.at[index],
                at(other_section=far),
            ).start()
            pass_on(index)

    def arrive(block, which):
        index = 2 * block + which

        @pl.when((section != block) & (near != block))
        def _():
            arrived(index)
            pass_on(index)

    def ready(block, which):
        index = 2 * block + which
        rest = pl.ds(pl.multiple_of((1 - core) * part_rows, part_rows), part_rows)

        @pl.when(section != block)
        def _():
            wait_for(weights.at[index, rest], pass_recv.at[index])

        @pl.when(section == block)
        def _():
            (own_second if which else own_first).wait()

    offer(0, near, 0)
    for step in range(1, sections):
        remote(
            vectors.at[section], vectors.at[section], vector_send, vector_recv,
            at(other_section=lax.rem(section + step, sections)),
        ).start()

    logits = logit_ref[...].astype(f32)
    raised = jnp.exp(logits - jnp.max(logits, axis=-1, keepdims=True))
    probability[:, 0:bins] = raised / jnp.sum(raised, axis=-1, keepdims=True)
    cell_wide[:, 0:bins] = cell_ref[...]
    turned[0] = probability[...].T
    turned[1] = cell_wide[...].astype(f32).T
    address = lax.broadcasted_iota(jnp.int32, (cells, half), 0).astype(f32)

    def add_bin(number, total):
        return total + jnp.where(turned[1, pl.ds(number, 1)] == address, turned[0, pl.ds(number, 1)], 0.0)

    counted = lax.fori_loop(0, bins, add_bin, jnp.zeros((cells, half), f32)).astype(bf16)
    histogram[...] = counted
    pooled = jnp.dot(counted, context_ref[...], preferred_element_type=f32)
    cameras[chip, :, 0:cam] = pooled.astype(bf16)

    own_lidar.wait()
    put_shifted(joined, lidars[chip].astype(f32), wide)
    put_shifted(joined, pooled, wide, channels)
    unite_copy.wait()
    united = total_of(
        jnp.dot(
            joined[side * i : side * i + cells, wide * j : wide * j + united_in],
            unite_weight[united_in * (3 * i + j) : united_in * (3 * i + j + 1), :],
            preferred_element_type=f32,
        )
        for i in range(3)
        for j in range(3)
    )
    gathered[chip] = united.astype(bf16)
    for step in range(1, chips):
        remote(
            gathered.at[chip], gathered.at[chip], raw_send.at[step], raw_recv.at[step], at(other=chip_peer(step))
        ).start()
    center = jnp.sum(united, axis=0, keepdims=True) * (1.0 / cells)
    offsets = united - center
    unite_mine[0:1] = center
    unite_mine[1:2] = jnp.sum(offsets * offsets, axis=0, keepdims=True)
    unite_slots[me] = unite_mine[...]

    def send_unite(step, unused):
        remote(
            unite_mine, unite_slots.at[me], unite_send, unite_recv, at(other=lax.rem(me + step, peers))
        ).start()
        return 0

    lax.fori_loop(1, peers, send_unite, 0)

    @pl.when(section == 0)
    def _():
        offer(0, far, 1)
        offer(1, near, 2)

    shifted[...] = jnp.zeros_like(shifted)
    flat[9 * cam :, :] = jnp.zeros((flat_rows - 9 * cam, half), bf16)

    def merged(centers, squares, each):
        parts = centers.shape[0]
        center = jnp.sum(centers, axis=0, keepdims=True) * (1.0 / parts)
        apart = centers - center
        square = jnp.sum(squares, axis=0, keepdims=True) + each * jnp.sum(apart * apart, axis=0, keepdims=True)
        return center, square

    wait_for(unite_slots.at[pl.ds(0, peers - 1)], unite_recv)
    center, square = merged(unite_slots[:, 0, :], unite_slots[:, 1, :], cells)
    scales[0] = lax.rsqrt(square * (1.0 / count) + eps)
    scales[stages] = center
    relay(0, 0)

    @pl.when(section != 0)
    def _():
        offer(0, far, 1)

    def enter(number):
        value = (gathered[number].astype(f32) - scales[stages]) * scales[0]
        normed[0, number] = value
        entering = silu(unite_gain[...] * value + unite_bias[...])
        current[number] = entering.astype(bf16)
        kept[0, number] = entering.astype(bf16)
        put_shifted(shifted.at[number], entering, channels)

    enter(chip)
    for step in (1, 3, 2):
        wait_for(gathered.at[0], raw_recv.at[step])
        enter(lax.rem(chip - step + chips, chips))
        if step == 1:
            relay(1, 0)

            @pl.when(section == 0)
            def _():
                offer(1, far, 3)

    own_cot.wait()
    for step in range(1, chips):
        peer = at(other=chip_peer(step))
        remote(upstream.at[chip], upstream.at[chip], cot_send.at[step], cot_recv.at[step], peer).start()
    for step in range(1, chips):
        peer = at(other=chip_peer(step))
        remote(lidars.at[chip], lidars.at[chip], lidar_send.at[step], lidar_recv.at[step], peer).start()
        remote(cameras.at[chip], cameras.at[chip], camera_send.at[step], camera_recv.at[step], peer).start()

    arrive(0, 0)
    relay(0, 1)

    @pl.when(section != 0)
    def _():
        offer(1, near, 2)

    wait_for(vectors.at[pl.ds(0, sections - 1)], vector_recv)

    members = 2 * groups
    place = group * 2 + core

    def copy_stats(event, step):
        to = lax.rem(place + step, members)
        return remote(
            mine.at[event], slots.at[event, place], stat_send.at[event], stat_recv.at[event],
            at(other=lax.div(to, 2) * (2 * chips) + chip * 2 + lax.rem(to, 2)),
        )

    def send_stats(event, first, second):
        mine[event, 0:1] = first
        mine[event, 1:2] = second
        slots[event, place] = mine[event]
        for step in range(1, members):
            copy_stats(event, step).start()

    def take_stats(event):
        wait_for(slots.at[event, pl.ds(0, members - 1)], stat_recv.at[event])
        return slots[event, :, 0, :], slots[event, :, 1, :]

    def forward_stage(stage, weight, meanwhile, use):
        centers, squares = [], []
        for number in range(chips):
            activ = conv(shifted.at[number], weight)
            held[number] = activ
            center = jnp.sum(activ, axis=0, keepdims=True) * (1.0 / cells)
            offsets = activ - center
            centers.append(center)
            squares.append(jnp.sum(offsets * offsets, axis=0, keepdims=True))
        center, square = merged(jnp.concatenate(centers, axis=0), jnp.concatenate(squares, axis=0), cells)
        send_stats(stage - 1, center, square)
        meanwhile()
        centers, squares = take_stats(stage - 1)
        center, square = merged(centers, squares, chips * cells)
        scale = lax.rsqrt(square * (1.0 / count) + eps)
        scales[stage] = scale
        for number in range(chips):
            value = (held[number] - center) * scale
            normed[stage, number] = value
            use(number, value)

    def block(s, unused):
        stage = 2 * s + 1

        def vector(number):
            return vectors[s, number : number + 1]

        def during_first():
            @pl.when(s == 0)
            def _():
                relay(2, 0)

                @pl.when(section != 0)
                def _():
                    offer(1, far, 3)

            @pl.when(s == 1)
            def _():
                relay(2, 1)

            arrive(s, 1)

        def during_second():
            @pl.when(s == 0)
            def _():
                relay(3, 0)
                relay(1, 1)

            @pl.when(s == 1)
            def _():
                relay(3, 1)

            @pl.when(s < blocks - 1)
            def _():
                arrive(s + 1, 0)

        def use_first(number, value):
            hidden = silu(vector(0) * value + vector(1))
            kept[stage, number] = hidden.astype(bf16)
            put_shifted(shifted.at[number], hidden, channels)

        def use_second(number, value):
            output = current[number].astype(f32) + silu(vector(2) * value + vector(3))
            held[number] = output
            current[number] = output.astype(bf16)

            @pl.when(s < blocks - 1)
            def _():
                kept[stage + 1, number] = output.astype(bf16)
                put_shifted(shifted.at[number], output, channels)

        ready(s, 0)
        forward_stage(
            stage, lambda i: weights[2 * s, 3 * channels * i : 3 * channels * (i + 1), :], during_first, use_first
        )
        ready(s, 1)
        forward_stage(
            stage + 1, lambda i: weights[2 * s + 1, 3 * channels * i : 3 * channels * (i + 1), :],
            during_second, use_second,
        )
        return 0

    lax.fori_loop(0, blocks, block, 0)
    act_ref[...] = held[chip]

    rows16 = pl.ds(pl.multiple_of(section * 16, 16), 16)
    lanes = pl.ds(pl.multiple_of(lane_half * half, half), half)
    flat48 = pl.ds(pl.multiple_of(section * 48, 16), 48)

    def lateral(j):
        return pl.ds(pl.multiple_of(channels * (2 - j) + lane_half * half, half), half)

    def weight_grad(stage, inputs):
        columns = pl.ds(pl.multiple_of(row_half * half, half), half)
        values = [inputs[number, :, columns] for number in range(chips)]
        for i in range(3):
            for j in range(3):
                taps = total_of(
                    lax.dot_general(
                        values[number],
                        shifted[number, side * (2 - i) : side * (2 - i) + cells, lateral(j)],
                        transposed_lhs,
                        preferred_element_type=f32,
                    )
                    for number in range(chips)
                ).astype(bf16)
                partial[stage, 3 * i + j, 0] = taps[0:64]
                partial[stage, 3 * i + j, 1] = taps[64:128]
        to_sibling(stage)

    def to_sibling(k):
        remote(
            partial.at[k, :, 1 - core], core_part.at[k], grad_send.at[0, k], grad_recv.at[0, k], at(other=sibling)
        ).start()

    def to_sections(k):
        wait_for(core_part.at[k], grad_recv.at[0, k])
        for tap in range(9):
            own_part[k, tap] = (partial[k, tap, core].astype(f32) + core_part[k, tap].astype(f32)).astype(bf16)
        section_part[k, section] = own_part[k, :, rows16]
        for step in range(1, sections):
            other = lax.rem(section + step, sections)
            remote(
                own_part.at[k, :, pl.ds(pl.multiple_of(other * 16, 16), 16)], section_part.at[k, section],
                grad_send.at[1, k], grad_recv.at[1, k], at(other_section=other),
            ).start()

    def over_groups(k, value, buffer, number):
        if groups == 1:
            return value
        buffer[k, group] = value
        for step in range(1, groups):
            to = lax.rem(group + step, groups) * (2 * chips) + chip * 2 + core
            remote(
                buffer.at[k, group], buffer.at[k, group], group_send.at[number], group_recv.at[number], at(other=to)
            ).start()
        wait_for(buffer.at[k, pl.ds(0, groups - 1)], group_recv.at[number])
        return jnp.sum(buffer[k].astype(f32), axis=0).astype(bf16)

    def to_column(k):
        wait_for(section_part.at[k, pl.ds(0, sections - 1)], grad_recv.at[1, k])
        piece = total_of(section_part[k, number].astype(f32) for number in range(sections)).astype(bf16)
        place = whole.at[k, :, row_half, core, rows16, lanes]
        place[...] = over_groups(k, piece, group_part, k)
        for step in range(1, chips):
            remote(place, place, grad_send.at[2, k], grad_recv.at[2, k], at(other=chip_peer(step))).start()

    def column_arrived(k):
        wait_for(whole.at[k, :, 0, 0, pl.ds(0, 16 * (chips - 1)), pl.ds(0, half)], grad_recv.at[2, k])

    def to_owner(k, block):
        column_arrived(k)
        place = whole.at[k, :, :, core, rows16]

        @pl.when(section != block)
        def _():
            remote(place, place, grad_send.at[3, k], grad_recv.at[3, k], at(other_section=block)).start()

    def to_all(k):
        column_arrived(k)
        place = whole.at[k, :, :, core, rows16]
        for step in range(1, sections):
            other = lax.rem(section + step, sections)
            remote(place, place, grad_send.at[3, k], grad_recv.at[3, k], at(other_section=other)).start()

    def share(k):
        wait_for(whole.at[k, :, :, 0, pl.ds(0, 16 * (sections - 1))], grad_recv.at[3, k])
        place = whole.at[k, :, :, core]
        remote(place, place, grad_send.at[4, k], grad_recv.at[4, k], at(other=sibling)).start()

    def owner_share(k, block):
        @pl.when(section == block)
        def _():
            share(k)

    def shared(k):
        wait_for(whole.at[k, :, :, 0], grad_recv.at[4, k])

    def block_of(k):
        return lax.div(k - 1, 2)

    def advance(slot):
        due = ((2, to_sections), (4, to_column), (6, lambda k: to_owner(k, block_of(k))),
               (8, lambda k: owner_share(k, block_of(k))))
        for ahead, act in due:
            @pl.when(slot + ahead <= stages - 1)
            def _():
                act(slot + ahead)

    def backward_stage(stage, gain, bias, gradient, meanwhile):
        event = stages - 1 + stage
        firsts, seconds = None, None
        for number in range(chips):
            value = normed[stage, number]
            grads = gradient(number) * slope(gain * value + bias)
            held[number] = grads
            first = jnp.sum(grads, axis=0, keepdims=True)
            second = jnp.sum(grads * value, axis=0, keepdims=True)
            firsts = first if firsts is None else firsts + first
            seconds = second if seconds is None else seconds + second
        send_stats(event, firsts, seconds)
        meanwhile()
        first, second = take_stats(event)
        first = jnp.sum(first, axis=0, keepdims=True)
        second = jnp.sum(second, axis=0, keepdims=True)
        totals[section, stage, 0:1] = first
        totals[section, stage, 1:2] = second
        first = first * (1.0 / count)
        second = second * (1.0 / count)
        factor = gain * scales[stage]
        for number in range(chips):
            put_shifted(
                shifted.at[number], factor * (held[number] - first - normed[stage, number] * second), channels
            )

    for step in range(1, chips):
        wait_for(upstream.at[0], cot_recv.at[step])
        wait_for(upstream.at[0], cot_send.at[step])

    def block_back(back, unused):
        s = blocks - 1 - back
        stage = 2 * s + 1

        def vector(number):
            return vectors[s, number : number + 1]

        def during_second():
            @pl.when(back > 0)
            def _():
                weight_grad(stage + 2, kept.at[stage + 1])
            advance(stage + 1)

        def during_first():
            weight_grad(stage + 1, kept.at[stage])
            advance(stage)

        backward_stage(stage + 1, vector(2), vector(3), lambda number: upstream[number].astype(f32), during_second)
        for number in range(chips):
            held[number] = conv_transposed(
                shifted.at[number], lambda tap: weights[2 * s + 1, channels * tap : channels * (tap + 1), :], channels
            )
        backward_stage(stage, vector(0), vector(1), lambda number: held[number], during_first)
        for number in range(chips):
            passed = conv_transposed(
                shifted.at[number], lambda tap: weights[2 * s, channels * tap : channels * (tap + 1), :], channels
            )
            upstream[number] = (upstream[number].astype(f32) + passed).astype(bf16)
        return 0

    lax.fori_loop(0, blocks, block_back, 0)

    def during_unite():
        weight_grad(1, kept.at[0])
        advance(0)

    backward_stage(
        0, unite_gain[...], unite_bias[...], lambda number: upstream[number].astype(f32), during_unite
    )
    for step in range(1, sections):
        remote(
            totals.at[section], totals.at[section], total_send, total_recv,
            at(other_section=lax.rem(section + step, sections)),
        ).start()
    for step in range(1, chips):
        wait_for(lidars.at[0], lidar_recv.at[step])
        wait_for(cameras.at[0], camera_recv.at[step])
    weight_grad(0, lidars)
    held_cameras = [cameras[number] for number in range(chips)]
    for i in range(3):
        for j in range(3):
            taps = total_of(
                lax.dot_general(
                    held_cameras[number],
                    shifted[number, side * (2 - i) : side * (2 - i) + cells, lateral(j)],
                    transposed_lhs,
                    preferred_element_type=f32,
                )
                for number in range(chips)
            ).astype(bf16)
            flat[cam * (3 * i + j) : cam * (3 * i + j + 1)] = taps[0:cam]
    quarter = flat_rows // 4
    kept_rows = pl.ds(pl.multiple_of(row_half * (2 * quarter) + core * quarter, 16), quarter)
    sent_rows = pl.ds(pl.multiple_of(row_half * (2 * quarter) + (1 - core) * quarter, 16), quarter)
    extra = stages
    remote(
        flat.at[sent_rows], flat_core, grad_send.at[0, extra], grad_recv.at[0, extra], at(other=sibling)
    ).start()
    advance(-1)
    own = shifted.at[chip]
    lidar_grad[...] = conv_transposed(
        own, lambda tap: unite_weight[united_in * tap : united_in * tap + channels, :], channels
    )
    pooled_grad = conv_transposed(
        own, lambda tap: unite_weight[united_in * tap + channels : united_in * (tap + 1), :], channels
    ).astype(bf16)

    wait_for(flat_core, grad_recv.at[0, extra])
    flat_own[...] = (flat[kept_rows].astype(f32) + flat_core[...].astype(f32)).astype(bf16)
    flat_section[section] = flat_own[flat48]
    for step in range(1, sections):
        other = lax.rem(section + step, sections)
        remote(
            flat_own.at[pl.ds(pl.multiple_of(other * 48, 16), 48)], flat_section.at[section],
            grad_send.at[1, extra], grad_recv.at[1, extra], at(other_section=other),
        ).start()
    advance(-2)

    context_grad[...] = lax.dot_general(histogram[...], pooled_grad, transposed_lhs, preferred_element_type=f32)
    table = lax.dot_general(context_ref[...], pooled_grad, transposed_rhs, preferred_element_type=f32)
    places = cell_wide[...]
    within = lax.rem(places, half)
    low = jnp.take_along_axis(table[:, 0:half], within, axis=1)
    high = jnp.take_along_axis(table[:, half : 2 * half], within, axis=1)
    chance = probability[...]
    chance_grad = jnp.where(places < half, low, high)
    logits_grad = chance * (chance_grad - jnp.sum(chance_grad * chance, axis=-1, keepdims=True))
    logit_grad[...] = logits_grad[:, 0:bins]

    to_column(1)
    to_owner(3, 1)
    owner_share(5, 2)
    to_column(0)
    wait_for(flat_section.at[pl.ds(0, sections - 1)], grad_recv.at[1, extra])
    piece = total_of(flat_section[number].astype(f32) for number in range(sections)).astype(bf16)
    flat_place = flat_whole.at[row_half, core, flat48, lanes]
    flat_place[...] = over_groups(0, piece, flat_group, extra)
    for step in range(1, chips):
        remote(
            flat_place, flat_place, grad_send.at[2, extra], grad_recv.at[2, extra], at(other=chip_peer(step))
        ).start()
    to_owner(2, 0)
    owner_share(4, 1)
    to_owner(1, 0)
    owner_share(3, 1)
    to_all(0)
    wait_for(flat_whole.at[0, 0, pl.ds(0, 48 * (chips - 1)), pl.ds(0, half)], grad_recv.at[2, extra])
    flat_rows_place = flat_whole.at[:, core, flat48]
    for step in range(1, sections):
        other = lax.rem(section + step, sections)
        remote(
            flat_rows_place, flat_rows_place, grad_send.at[3, extra], grad_recv.at[3, extra],
            at(other_section=other),
        ).start()
    owner_share(2, 0)
    owner_share(1, 0)
    share(0)
    wait_for(flat_whole.at[:, 0, pl.ds(0, 48 * (sections - 1))], grad_recv.at[3, extra])
    flat_half = flat_whole.at[:, core]
    remote(flat_half, flat_half, grad_send.at[4, extra], grad_recv.at[4, extra], at(other=sibling)).start()

    wait_for(totals.at[pl.ds(0, sections - 1)], total_recv)
    sums_out[...] = total_of(totals[number] for number in range(sections))
    shared(2 * section + 1)
    shared(2 * section + 2)
    first_copy = pltpu.make_async_copy(whole.at[2 * section + 1], first_out, local_sem.at[5])
    second_copy = pltpu.make_async_copy(whole.at[2 * section + 2], second_out, local_sem.at[6])
    first_copy.start()
    second_copy.start()
    shared(0)
    unite_done = pltpu.make_async_copy(whole.at[0], unite_out, local_sem.at[7])
    unite_done.start()
    wait_for(flat_whole.at[:, 0], grad_recv.at[4, extra])
    camera_done = pltpu.make_async_copy(flat_whole, camera_out, local_sem.at[8])
    camera_done.start()

    wait_for(unite_slots.at[pl.ds(0, peers - 1)], unite_send)
    for step in range(1, chips):
        wait_for(gathered.at[0], raw_send.at[step])
        wait_for(lidars.at[0], lidar_send.at[step])
        wait_for(cameras.at[0], camera_send.at[step])
    for number in range(4):
        wait_for(weights.at[0, part], weight_send.at[number])
    for number in range(2):
        wait_for(weights.at[0, part], relay_send.at[number])
    wait_for(vectors.at[pl.ds(0, sections - 1)], vector_send)
    wait_for(totals.at[pl.ds(0, sections - 1)], total_send)

    def drain_stats(event, unused):
        wait_for(slots.at[event, pl.ds(0, members - 1)], stat_send.at[event])
        return 0

    lax.fori_loop(0, 2 * stages - 1, drain_stats, 0)

    def drain_weights(index, unused):
        @pl.when(section != lax.div(index, 2))
        def _():
            wait_for(weights.at[index, part], pass_send.at[index])
        return 0

    lax.fori_loop(0, 2 * blocks, drain_weights, 0)

    def drain_grads(k, unused):
        wait_for(core_part.at[k], grad_send.at[0, k])
        wait_for(section_part.at[k, pl.ds(0, sections - 1)], grad_send.at[1, k])
        wait_for(whole.at[k, :, 0, 0, pl.ds(0, 16 * (chips - 1)), pl.ds(0, half)], grad_send.at[2, k])
        if groups > 1:
            wait_for(group_part.at[k, pl.ds(0, groups - 1)], group_send.at[k])

        @pl.when((k > 0) & (section != block_of(k)))
        def _():
            wait_for(whole.at[k, :, :, 0, pl.ds(0, 16)], grad_send.at[3, k])

        @pl.when((k > 0) & (section == block_of(k)))
        def _():
            wait_for(whole.at[k, :, :, 0], grad_send.at[4, k])
        return 0

    lax.fori_loop(0, stages, drain_grads, 0)
    wait_for(whole.at[0, :, :, 0, pl.ds(0, 16 * (sections - 1))], grad_send.at[3, 0])
    wait_for(whole.at[0, :, :, 0], grad_send.at[4, 0])
    wait_for(flat_core, grad_send.at[0, extra])
    wait_for(flat_section.at[pl.ds(0, sections - 1)], grad_send.at[1, extra])
    wait_for(flat_whole.at[0, 0, pl.ds(0, 48 * (chips - 1)), pl.ds(0, half)], grad_send.at[2, extra])
    wait_for(flat_whole.at[:, 0, pl.ds(0, 48 * (sections - 1))], grad_send.at[3, extra])
    wait_for(flat_whole.at[:, 0], grad_send.at[4, extra])
    if groups > 1:
        wait_for(flat_group.at[0, pl.ds(0, groups - 1)], group_send.at[extra])
    first_copy.wait()
    second_copy.wait()
    unite_done.wait()
    camera_done.wait()


def body(
    lidar, context, depth_logits, cell_index, unite_weight, unite_gain, unite_bias, first_weight, second_weight,
    first_gain, first_bias, second_gain, second_bias, cotangent,
):
    peers = lax.axis_size("dp")
    sections = lax.axis_size("section")
    section = lax.axis_index("section")
    channels = cotangent.shape[-1]
    pixels, bins = depth_logits.shape[2:]
    cam = context.shape[-1]
    united_in = unite_weight.shape[1]
    blocks = sections
    stages = 2 * blocks + 1
    events = 2 * stages - 1
    groups = peers // (2 * chips)
    taken = 9 * channels

    vmem = pl.BlockSpec(memory_space=pltpu.VMEM)
    hbm = pl.BlockSpec(memory_space=pl.ANY)
    shape = jax.ShapeDtypeStruct
    dma = pltpu.SemaphoreType.DMA
    act, lidar_grad, context_grad, logit_grad, unite_grad, camera_grad, first_grad, second_grad, sums = pl.pallas_call(
        functools.partial(kernel, peers, sections),
        out_shape=(
            shape((cells, channels), f32),
            shape((cells, channels), f32),
            shape((pixels, cam), f32),
            shape((pixels, bins), f32),
            shape((9, 2, 2, 64, channels), bf16),
            shape((2, 2, flat_rows // 4, channels), bf16),
            shape((9, 2, 2, 64, channels), bf16),
            shape((9, 2, 2, 64, channels), bf16),
            shape((stages, 2, channels), f32),
        ),
        in_specs=[hbm, vmem, vmem, vmem, hbm, vmem, vmem, hbm, hbm, vmem, vmem, vmem, vmem, hbm],
        out_specs=[vmem, vmem, vmem, vmem, hbm, hbm, hbm, hbm, vmem],
        scratch_shapes=[
            pltpu.VMEM((2 * blocks, taken, channels), bf16),
            pltpu.VMEM((9 * united_in, channels), bf16),
            pltpu.VMEM((blocks, 4, channels), f32),
            pltpu.VMEM((cells + 2 * side, 3 * wide), bf16),
            pltpu.VMEM((chips, cells + 2 * side, 3 * channels), bf16),
            pltpu.VMEM((chips, cells, channels), bf16),
            pltpu.VMEM((2 * blocks, chips, cells, channels), bf16),
            pltpu.VMEM((stages, chips, cells, channels), f32),
            pltpu.VMEM((stages + 1, 1, channels), f32),
            pltpu.VMEM((chips, cells, channels), f32),
            pltpu.VMEM((chips, cells, channels), bf16),
            pltpu.VMEM((chips, cells, channels), bf16),
            pltpu.VMEM((chips, cells, channels), bf16),
            pltpu.VMEM((chips, cells, half), bf16),
            pltpu.VMEM((events, 2, channels), f32),
            pltpu.VMEM((events, 2 * groups, 2, channels), f32),
            pltpu.VMEM((2, channels), f32),
            pltpu.VMEM((peers, 2, channels), f32),
            pltpu.VMEM((pixels, half), f32),
            pltpu.VMEM((pixels, half), jnp.int32),
            pltpu.VMEM((2, half, pixels), f32),
            pltpu.VMEM((cells, pixels), bf16),
            pltpu.VMEM((stages, 9, 2, 64, half), bf16),
            pltpu.VMEM((stages, 9, 64, half), bf16),
            pltpu.VMEM((stages, 9, 64, half), bf16),
            pltpu.VMEM((stages, sections, 9, 16, half), bf16),
            pltpu.VMEM((stages, 9, 2, 2, 64, channels), bf16),
            pltpu.VMEM((flat_rows, half), bf16),
            pltpu.VMEM((flat_rows // 4, half), bf16),
            pltpu.VMEM((flat_rows // 4, half), bf16),
            pltpu.VMEM((sections, 48, half), bf16),
            pltpu.VMEM((2, 2, flat_rows // 4, channels), bf16),
            pltpu.VMEM((sections, stages, 2, channels), f32),
            pltpu.VMEM((stages if groups > 1 else 1, groups, 9, 16, half), bf16),
            pltpu.VMEM((1, groups, 48, half), bf16),
            dma((9,)), dma, dma, dma((events,)), dma((events,)), dma((chips,)), dma((chips,)), dma((chips,)),
            dma((chips,)), dma((chips,)), dma((chips,)), dma((chips,)), dma((chips,)), dma((4,)),
            dma((2 * blocks,)), dma((2,)), dma((2 * blocks,)), dma((2 * blocks,)), dma, dma,
            dma((5, stages + 1)), dma((5, stages + 1)), dma, dma, dma((stages + 1,)), dma((stages + 1,)),
        ],
        compiler_params=pltpu.CompilerParams(
            collective_id=0, has_side_effects=True, vmem_limit_bytes=56 << 20
        ),
    )(
        lidar.reshape(cells, channels), context.reshape(pixels, cam), depth_logits.reshape(pixels, bins),
        cell_index.reshape(pixels, bins), unite_weight.reshape(-1, channels),
        unite_gain[None], unite_bias[None], first_weight.reshape(taken, channels),
        second_weight.reshape(taken, channels), first_gain, first_bias, second_gain, second_bias,
        cotangent.reshape(-1, cells, channels),
    )

    camera_rows = camera_grad.reshape(-1, channels)[: 9 * cam].reshape(9, cam, channels)
    unite_whole = jnp.concatenate(
        [unite_grad.reshape(9, channels, channels).astype(f32), camera_rows.astype(f32)], axis=1
    )
    own = lax.dynamic_slice_in_dim(sums[1:].reshape(blocks, 2, 2, channels), section, 1, 0)
    return (
        act.reshape(lidar.shape),
        lidar_grad.reshape(lidar.shape),
        context_grad.reshape(context.shape),
        logit_grad.reshape(depth_logits.shape),
        unite_whole,
        sums[0, 1],
        sums[0, 0],
        first_grad.reshape(first_weight.shape).astype(f32),
        second_grad.reshape(second_weight.shape).astype(f32),
        own[:, 0, 1],
        own[:, 0, 0],
        own[:, 1, 1],
        own[:, 1, 0],
    )


def solution(mesh):
    split, by_dp = P("section"), P("section", "dp")
    in_specs = (by_dp, by_dp, by_dp, by_dp, P(), P(), P(), split, split, split, split, split, split, P(None, "dp"))
    out_specs = (by_dp, by_dp, by_dp, by_dp, P(), P(), P(), split, split, split, split, split, split)
    return jax.shard_map(body, mesh=mesh, in_specs=in_specs, out_specs=out_specs, check_vma=False)
```

```python
import functools

import jax
import jax.numpy as jnp
from jax import lax
from jax.experimental import pallas as pl
from jax.experimental.pallas import tpu as pltpu
from jax.sharding import PartitionSpec as P

eps = 1e-05
f32, bf16 = jnp.float32, jnp.bfloat16
MESH = pl.DeviceIdType.MESH
side = 16
cells = side * side
wide = 384
chips = 4
half = 128
flat_rows = 768
transposed_rhs = (((1,), (1,)), ((), ()))
transposed_lhs = (((0,), (0,)), ((), ()))


def sigmoid(value):
    return 0.5 * jnp.tanh(0.5 * value) + 0.5


def slope(value):
    gate = sigmoid(value)
    return gate * (1.0 + value * (1.0 - gate))


def silu(value):
    return value * sigmoid(value)


def put_shifted(buffer, value, stride, offset=0):
    column = lax.broadcasted_iota(jnp.int32, (cells, 1), 0) % side
    width = value.shape[1]
    before = jnp.where(column == 0, 0.0, pltpu.roll(value, 1, 0))
    after = jnp.where(column == side - 1, 0.0, pltpu.roll(value, cells - 1, 0))
    for group, shifted in enumerate((before, value, after)):
        start = group * stride + offset
        buffer[side : side + cells, start : start + width] = shifted.astype(bf16)


def total_of(terms):
    total = None
    for term in terms:
        total = term if total is None else total + term
    return total


def conv(buffer, weight):
    return total_of(
        jnp.dot(buffer[side * i : side * i + cells, :], weight(i), preferred_element_type=f32) for i in range(3)
    )


def conv_transposed(buffer, weight, width):
    return total_of(
        lax.dot_general(
            buffer[side * (2 - i) : side * (2 - i) + cells, width * (2 - j) : width * (3 - j)],
            weight(3 * i + j),
            transposed_rhs,
            preferred_element_type=f32,
        )
        for i in range(3)
        for j in range(3)
    )


plan = {
    "start": [("offer", 0, "near", 0), ("offer", 1, "near", 3), ("offer", 1, "near", 1), ("offer", 1, "near", 2), ("offer", 0, "near", 1)],
    "lift1": [("offer", 1, "near", 0), ("offer", 0, "near", 2)],
    "lift2": [("offer", 0, "far", 0)],
    "united": [("relay", 0, 0), ("offer", 1, "far", 2), ("offer", 1, "far", 0), ("relay", 2, 1)],
    "united2": [("relay", 0, 1), ("offer", 0, "far", 1)],
    "merged": [("offer", 1, "far", 1), ("offer", 0, "near", 3), ("offer", 0, "far", 2), ("relay", 1, 0)],
    "entered1": [("relay", 1, 1), ("relay", 3, 0)],
    "entered3": [("relay", 2, 0), ("arrive", 0, 0), ("offer", 0, "far", 3)],
    "entered2": [("arrive", 2, 1)],
    "entered": [("relay", 3, 1)],
    ("first", 0): [("arrive", 0, 1)],
    ("second", 0): [("offer", 1, "far", 3), ("arrive", 1, 0)],
    ("first", 1): [("arrive", 2, 0), ("arrive", 1, 1)],
    ("first", 2): [("arrive", 3, 0)],
    ("first", 3): [("arrive", 3, 1)],
}


def kernel(
    peers, sections,
    lidar_ref, context_ref, logit_ref, cell_ref, unite_ref, unite_gain, unite_bias, first_ref, second_ref,
    first_gain, first_bias, second_gain, second_bias, cotangent_ref,
    act_ref, lidar_grad, context_grad, logit_grad, unite_out, camera_out, first_out, second_out, small_out,
    weights, unite_weight, vectors, joined, shifted, current, kept, normed, scales, held, gathered, upstream,
    lidars, cameras, mine, slots, unite_mine, unite_slots, probability, places, histogram,
    partial, core_part, own_part, section_part, whole, flat, flat_core, flat_own, flat_section, flat_whole,
    totals, group_part, flat_group,
    local_sem, unite_send, unite_recv, stat_send, stat_recv, raw_send, raw_recv, cot_send, cot_recv,
    lidar_send, lidar_recv, camera_send, camera_recv, weight_send, weight_recv, relay_send, pass_send, pass_recv,
    vector_send, vector_recv, grad_send, grad_recv, total_send, total_recv, group_send, group_recv,
):
    me = lax.axis_index("dp")
    section = lax.axis_index("section")
    core = lax.rem(me, 2)
    chip = lax.rem(lax.div(me, 2), chips)
    group = lax.div(me, 2 * chips)
    groups = peers // (2 * chips)
    blocks = sections
    stages = 2 * blocks + 1
    channels = vectors.shape[-1]
    bins = logit_ref.shape[0]
    cam = context_ref.shape[0]
    united_in = channels + cam
    taken = 9 * channels
    row_half = lax.div(chip, 2)
    lane_half = lax.rem(chip, 2)
    count = float(peers * cells)

    def at(other_section=None, other=None):
        return (section if other_section is None else other_section, me if other is None else other)

    def chip_peer(step):
        return group * (2 * chips) + lax.rem(chip + step, chips) * 2 + core

    sibling = me + 1 - 2 * core

    def remote(source, target, send, recv, device):
        return pltpu.make_async_remote_copy(
            src_ref=source, dst_ref=target, send_sem=send, recv_sem=recv, device_id=device, device_id_type=MESH
        )

    def wait_for(part, semaphore):
        pltpu.make_async_copy(part, part, semaphore).wait()

    barrier = pltpu.get_barrier_semaphore()
    for step in range(1, sections):
        pl.semaphore_signal(
            barrier, inc=1, device_id=at(other_section=lax.rem(section + step, sections)), device_id_type=MESH
        )

    def greet(step, unused):
        pl.semaphore_signal(barrier, inc=1, device_id=at(other=lax.rem(me + step, peers)), device_id_type=MESH)
        return 0

    lax.fori_loop(1, peers, greet, 0)

    unite_copy = pltpu.make_async_copy(unite_ref, unite_weight, local_sem.at[0])
    own_first = pltpu.make_async_copy(first_ref, weights.at[2 * section], local_sem.at[1])
    own_second = pltpu.make_async_copy(second_ref, weights.at[2 * section + 1], local_sem.at[2])
    own_cot = pltpu.make_async_copy(cotangent_ref.at[section], upstream.at[chip], local_sem.at[3])
    own_lidar = pltpu.make_async_copy(lidar_ref, lidars.at[chip], local_sem.at[4])
    own_lidar.start()
    unite_copy.start()
    own_first.start()
    own_second.start()
    own_cot.start()
    for number, part in enumerate((first_gain, first_bias, second_gain, second_bias)):
        vectors[section, number : number + 1] = part[...]
    joined[...] = jnp.zeros_like(joined)
    probability[...] = jnp.zeros_like(probability)
    places[...] = jnp.zeros_like(places)
    cameras[chip] = jnp.zeros((cells, half), bf16)
    pl.semaphore_wait(barrier, peers - 1 + sections - 1)

    beside = section + 1 - 2 * lax.rem(section, 2)
    across = lax.rem(section + 2, sections)
    near = beside + core * (across - beside)
    far = across + core * (beside - across)
    part_rows = taken // 2
    part = pl.ds(pl.multiple_of(core * part_rows, part_rows), part_rows)
    sources = (first_ref, second_ref)

    def offer(which, target, number):
        index = 2 * section + which
        remote(
            sources[which].at[part], weights.at[index, part], weight_send.at[number], weight_recv.at[index],
            at(other_section=target),
        ).start()

    def arrived(index):
        wait_for(weights.at[index, part], weight_recv.at[index])

    def pass_on(index):
        remote(
            weights.at[index, part], weights.at[index, part], pass_send.at[index], pass_recv.at[index],
            at(other=sibling),
        ).start()

    def relay(block, which):
        index = 2 * block + which

        @pl.when(near == block)
        def _():
            arrived(index)
            remote(
                weights.at[index, part], weights.at[index, part], relay_send.at[which], weight_recv.at[index],
                at(other_section=far),
            ).start()
            pass_on(index)

    def arrive(block, which):
        index = 2 * block + which

        @pl.when((section != block) & (near != block))
        def _():
            arrived(index)
            pass_on(index)

    def ready(block, which):
        index = 2 * block + which
        rest = pl.ds(pl.multiple_of((1 - core) * part_rows, part_rows), part_rows)

        @pl.when(section != block)
        def _():
            wait_for(weights.at[index, rest], pass_recv.at[index])

        @pl.when(section == block)
        def _():
            (own_second if which else own_first).wait()

    def act_on(entry):
        name, one, two = entry[0:3]
        if name == "relay":
            relay(one, two)
        elif name == "arrive":
            arrive(one, two)
        else:
            @pl.when(section == entry[3])
            def _():
                offer(one, near if two == "near" else far, 2 * one + (two == "far"))

    def point(name, block=None):
        for key, entries in plan.items():
            if isinstance(key, tuple) and key[0] == name:
                @pl.when(block == key[1])
                def _():
                    for entry in entries:
                        act_on(entry)
            elif key == name:
                for entry in entries:
                    act_on(entry)

    point("start")
    for step in range(1, sections):
        remote(
            vectors.at[section], vectors.at[section], vector_send, vector_recv,
            at(other_section=lax.rem(section + step, sections)),
        ).start()

    logits = logit_ref[...].astype(f32)
    raised = jnp.exp(logits - jnp.max(logits, axis=0, keepdims=True))
    probability[0:bins] = raised / jnp.sum(raised, axis=0, keepdims=True)
    address = lax.broadcasted_iota(jnp.int32, (cells, half), 0)

    def add_bin(number, total):
        place = cell_ref[number]
        places[pl.ds(number, 1)] = place.astype(f32)
        return total + jnp.where(place == address, probability[pl.ds(number, 1)], 0.0)

    counted = jnp.zeros((cells, half), f32)
    for number in range(3):
        counted = lax.fori_loop(bins * number // 3, bins * (number + 1) // 3, add_bin, counted)
        if number < 2:
            point(f"lift{number + 1}")
    counted = counted.astype(bf16)
    histogram[...] = counted
    pooled = lax.dot_general(counted, context_ref[...], transposed_rhs, preferred_element_type=f32)
    cameras[chip, :, 0:cam] = pooled.astype(bf16)

    own_lidar.wait()
    put_shifted(joined, lidars[chip].astype(f32), wide)
    put_shifted(joined, pooled, wide, channels)
    unite_copy.wait()
    united = total_of(
        jnp.dot(
            joined[side * i : side * i + cells, wide * j : wide * j + united_in],
            unite_weight[united_in * (3 * i + j) : united_in * (3 * i + j + 1), :],
            preferred_element_type=f32,
        )
        for i in range(3)
        for j in range(3)
    )
    gathered[chip] = united.astype(bf16)
    for step in range(1, chips):
        remote(
            gathered.at[chip], gathered.at[chip], raw_send.at[step], raw_recv.at[step], at(other=chip_peer(step))
        ).start()
    center = jnp.sum(united, axis=0, keepdims=True) * (1.0 / cells)
    offsets = united - center
    unite_mine[0:1] = center
    unite_mine[1:2] = jnp.sum(offsets * offsets, axis=0, keepdims=True)
    unite_slots[me] = unite_mine[...]

    def send_unite(step, unused):
        remote(
            unite_mine, unite_slots.at[me], unite_send, unite_recv, at(other=lax.rem(me + step, peers))
        ).start()
        return 0

    lax.fori_loop(1, peers, send_unite, 0)

    point("united")
    shifted[...] = jnp.zeros_like(shifted)
    flat[9 * cam :, :] = jnp.zeros((flat_rows - 9 * cam, half), bf16)

    def merged(centers, squares, each):
        parts = centers.shape[0]
        center = jnp.sum(centers, axis=0, keepdims=True) * (1.0 / parts)
        apart = centers - center
        square = jnp.sum(squares, axis=0, keepdims=True) + each * jnp.sum(apart * apart, axis=0, keepdims=True)
        return center, square

    point("united2")
    wait_for(unite_slots.at[pl.ds(0, peers - 1)], unite_recv)
    center, square = merged(unite_slots[:, 0, :], unite_slots[:, 1, :], cells)
    scales[0] = lax.rsqrt(square * (1.0 / count) + eps)
    scales[stages] = center
    point("merged")

    def enter(number):
        value = (gathered[number].astype(f32) - scales[stages]) * scales[0]
        normed[0, number] = value
        entering = silu(unite_gain[...] * value + unite_bias[...])
        current[number] = entering.astype(bf16)
        kept[0, number] = entering.astype(bf16)
        put_shifted(shifted.at[number], entering, channels)

    enter(chip)
    for step in (1, 3, 2):
        wait_for(gathered.at[0], raw_recv.at[step])
        enter(lax.rem(chip - step + chips, chips))
        point(f"entered{step}")

    own_cot.wait()
    for step in range(1, chips):
        peer = at(other=chip_peer(step))
        remote(upstream.at[chip], upstream.at[chip], cot_send.at[step], cot_recv.at[step], peer).start()
    for step in range(1, chips):
        peer = at(other=chip_peer(step))
        remote(lidars.at[chip], lidars.at[chip], lidar_send.at[step], lidar_recv.at[step], peer).start()
        remote(cameras.at[chip], cameras.at[chip], camera_send.at[step], camera_recv.at[step], peer).start()

    point("entered")
    wait_for(vectors.at[pl.ds(0, sections - 1)], vector_recv)

    members = 2 * groups
    place = group * 2 + core

    def copy_stats(event, step):
        to = lax.rem(place + step, members)
        return remote(
            mine.at[event], slots.at[event, place], stat_send.at[event], stat_recv.at[event],
            at(other=lax.div(to, 2) * (2 * chips) + chip * 2 + lax.rem(to, 2)),
        )

    def send_stats(event, first, second):
        mine[event, 0:1] = first
        mine[event, 1:2] = second
        slots[event, place] = mine[event]
        for step in range(1, members):
            copy_stats(event, step).start()

    def take_stats(event):
        wait_for(slots.at[event, pl.ds(0, members - 1)], stat_recv.at[event])
        return slots[event, :, 0, :], slots[event, :, 1, :]

    def forward_stage(stage, weight, meanwhile, use):
        centers, squares = [], []
        for number in range(chips):
            activ = conv(shifted.at[number], weight)
            held[number] = activ
            center = jnp.sum(activ, axis=0, keepdims=True) * (1.0 / cells)
            offsets = activ - center
            centers.append(center)
            squares.append(jnp.sum(offsets * offsets, axis=0, keepdims=True))
        center, square = merged(jnp.concatenate(centers, axis=0), jnp.concatenate(squares, axis=0), cells)
        send_stats(stage - 1, center, square)
        meanwhile()
        centers, squares = take_stats(stage - 1)
        center, square = merged(centers, squares, chips * cells)
        scale = lax.rsqrt(square * (1.0 / count) + eps)
        scales[stage] = scale
        for number in range(chips):
            value = (held[number] - center) * scale
            normed[stage, number] = value
            use(number, value)

    def block(s, unused):
        stage = 2 * s + 1

        def vector(number):
            return vectors[s, number : number + 1]

        def during_first():
            point("first", s)

        def during_second():
            point("second", s)

        def use_first(number, value):
            hidden = silu(vector(0) * value + vector(1))
            kept[stage, number] = hidden.astype(bf16)
            put_shifted(shifted.at[number], hidden, channels)

        def use_second(number, value):
            output = current[number].astype(f32) + silu(vector(2) * value + vector(3))
            held[number] = output
            current[number] = output.astype(bf16)

            @pl.when(s < blocks - 1)
            def _():
                kept[stage + 1, number] = output.astype(bf16)
                put_shifted(shifted.at[number], output, channels)

        ready(s, 0)
        forward_stage(
            stage, lambda i: weights[2 * s, 3 * channels * i : 3 * channels * (i + 1), :], during_first, use_first
        )
        ready(s, 1)
        forward_stage(
            stage + 1, lambda i: weights[2 * s + 1, 3 * channels * i : 3 * channels * (i + 1), :],
            during_second, use_second,
        )
        return 0

    lax.fori_loop(0, blocks, block, 0)
    act_ref[...] = held[chip]

    rows16 = pl.ds(pl.multiple_of(section * 16, 16), 16)
    lanes = pl.ds(pl.multiple_of(lane_half * half, half), half)
    flat48 = pl.ds(pl.multiple_of(section * 48, 16), 48)

    def lateral(j):
        return pl.ds(pl.multiple_of(channels * (2 - j) + lane_half * half, half), half)

    def weight_grad(stage, inputs):
        columns = pl.ds(pl.multiple_of(row_half * half, half), half)
        values = [inputs[number, :, columns] for number in range(chips)]
        for i in range(3):
            for j in range(3):
                taps = total_of(
                    lax.dot_general(
                        values[number],
                        shifted[number, side * (2 - i) : side * (2 - i) + cells, lateral(j)],
                        transposed_lhs,
                        preferred_element_type=f32,
                    )
                    for number in range(chips)
                ).astype(bf16)
                partial[stage, 3 * i + j, 0] = taps[0:64]
                partial[stage, 3 * i + j, 1] = taps[64:128]
        to_sibling(stage)

    def to_sibling(k):
        remote(
            partial.at[k, :, 1 - core], core_part.at[k], grad_send.at[0, k], grad_recv.at[0, k], at(other=sibling)
        ).start()

    def to_sections(k):
        wait_for(core_part.at[k], grad_recv.at[0, k])
        for tap in range(9):
            own_part[k, tap] = (partial[k, tap, core].astype(f32) + core_part[k, tap].astype(f32)).astype(bf16)
        section_part[k, section] = own_part[k, :, rows16]
        for step in range(1, sections):
            other = lax.rem(section + step, sections)
            remote(
                own_part.at[k, :, pl.ds(pl.multiple_of(other * 16, 16), 16)], section_part.at[k, section],
                grad_send.at[1, k], grad_recv.at[1, k], at(other_section=other),
            ).start()

    def over_groups(k, value, buffer, number):
        if groups == 1:
            return value
        buffer[k, group] = value
        for step in range(1, groups):
            to = lax.rem(group + step, groups) * (2 * chips) + chip * 2 + core
            remote(
                buffer.at[k, group], buffer.at[k, group], group_send.at[number], group_recv.at[number], at(other=to)
            ).start()
        wait_for(buffer.at[k, pl.ds(0, groups - 1)], group_recv.at[number])
        return jnp.sum(buffer[k].astype(f32), axis=0).astype(bf16)

    def to_column(k):
        wait_for(section_part.at[k, pl.ds(0, sections - 1)], grad_recv.at[1, k])
        piece = total_of(section_part[k, number].astype(f32) for number in range(sections)).astype(bf16)
        place = whole.at[k, :, row_half, core, rows16, lanes]
        place[...] = over_groups(k, piece, group_part, k)
        for step in range(1, chips):
            remote(place, place, grad_send.at[2, k], grad_recv.at[2, k], at(other=chip_peer(step))).start()

    def column_arrived(k):
        wait_for(whole.at[k, :, 0, 0, pl.ds(0, 16 * (chips - 1)), pl.ds(0, half)], grad_recv.at[2, k])

    def to_owner(k):
        block = block_of(k)
        column_arrived(k)
        place = whole.at[k, :, :, core, rows16]

        @pl.when(section != block)
        def _():
            remote(place, place, grad_send.at[3, k], grad_recv.at[3, k], at(other_section=block)).start()

    def to_all(k):
        column_arrived(k)
        place = whole.at[k, :, :, core, rows16]
        for step in range(1, sections):
            other = lax.rem(section + step, sections)
            remote(place, place, grad_send.at[3, k], grad_recv.at[3, k], at(other_section=other)).start()

    def share(k):
        wait_for(whole.at[k, :, :, 0, pl.ds(0, 16 * (sections - 1))], grad_recv.at[3, k])
        place = whole.at[k, :, :, core]
        remote(place, place, grad_send.at[4, k], grad_recv.at[4, k], at(other=sibling)).start()

    def owner_share(k):
        @pl.when(section == block_of(k))
        def _():
            share(k)

    def shared(k):
        wait_for(whole.at[k, :, :, 0], grad_recv.at[4, k])

    def block_of(k):
        return lax.div(k - 1, 2)

    def when_due(k, act):
        @pl.when(k <= stages - 1)
        def _():
            act(k)

    def backward_stage(stage, gain, bias, gradient, meanwhile):
        event = stages - 1 + stage
        firsts, seconds = None, None
        for number in range(chips):
            value = normed[stage, number]
            grads = gradient(number) * slope(gain * value + bias)
            held[number] = grads
            first = jnp.sum(grads, axis=0, keepdims=True)
            second = jnp.sum(grads * value, axis=0, keepdims=True)
            firsts = first if firsts is None else firsts + first
            seconds = second if seconds is None else seconds + second
        send_stats(event, firsts, seconds)
        meanwhile()
        first, second = take_stats(event)
        first = jnp.sum(first, axis=0, keepdims=True)
        second = jnp.sum(second, axis=0, keepdims=True)
        totals[section, stage, 0:1] = first
        totals[section, stage, 1:2] = second
        first = first * (1.0 / count)
        second = second * (1.0 / count)
        factor = gain * scales[stage]
        for number in range(chips):
            put_shifted(
                shifted.at[number], factor * (held[number] - first - normed[stage, number] * second), channels
            )

    for step in range(1, chips):
        wait_for(upstream.at[0], cot_recv.at[step])
        wait_for(upstream.at[0], cot_send.at[step])

    def block_back(back, unused):
        s = blocks - 1 - back
        stage = 2 * s + 1

        def vector(number):
            return vectors[s, number : number + 1]

        def during_second():
            @pl.when(back > 0)
            def _():
                weight_grad(stage + 2, kept.at[stage + 1])
            when_due(stage + 4, to_column)

        def during_first():
            weight_grad(stage + 1, kept.at[stage])
            when_due(stage + 3, to_column)

        backward_stage(stage + 1, vector(2), vector(3), lambda number: upstream[number].astype(f32), during_second)
        for number in range(chips):
            held[number] = conv_transposed(
                shifted.at[number], lambda tap: weights[2 * s + 1, channels * tap : channels * (tap + 1), :], channels
            )
        when_due(stage + 2, to_sections)
        when_due(stage + 6, to_owner)
        backward_stage(stage, vector(0), vector(1), lambda number: held[number], during_first)
        for number in range(chips):
            passed = conv_transposed(
                shifted.at[number], lambda tap: weights[2 * s, channels * tap : channels * (tap + 1), :], channels
            )
            upstream[number] = (upstream[number].astype(f32) + passed).astype(bf16)
        when_due(stage + 1, to_sections)
        when_due(stage + 5, to_owner)
        return 0

    lax.fori_loop(0, blocks, block_back, 0)

    def during_unite():
        weight_grad(1, kept.at[0])
        to_column(3)

    backward_stage(
        0, unite_gain[...], unite_bias[...], lambda number: upstream[number].astype(f32), during_unite
    )
    for step in range(1, chips):
        wait_for(lidars.at[0], lidar_recv.at[step])
        wait_for(cameras.at[0], camera_recv.at[step])
    weight_grad(0, lidars)
    to_sections(1)
    held_cameras = [cameras[number] for number in range(chips)]
    for i in range(3):
        for j in range(3):
            taps = total_of(
                lax.dot_general(
                    held_cameras[number],
                    shifted[number, side * (2 - i) : side * (2 - i) + cells, lateral(j)],
                    transposed_lhs,
                    preferred_element_type=f32,
                )
                for number in range(chips)
            ).astype(bf16)
            flat[cam * (3 * i + j) : cam * (3 * i + j + 1)] = taps[0:cam]
    quarter = flat_rows // 4
    kept_rows = pl.ds(pl.multiple_of(row_half * (2 * quarter) + core * quarter, 16), quarter)
    sent_rows = pl.ds(pl.multiple_of(row_half * (2 * quarter) + (1 - core) * quarter, 16), quarter)
    extra = stages
    remote(
        flat.at[sent_rows], flat_core, grad_send.at[0, extra], grad_recv.at[0, extra], at(other=sibling)
    ).start()
    to_sections(0)
    to_column(2)
    to_owner(5)
    for step in range(1, sections):
        remote(
            totals.at[section], totals.at[section], total_send, total_recv,
            at(other_section=lax.rem(section + step, sections)),
        ).start()
    own = shifted.at[chip]
    pooled_grad = conv_transposed(
        own, lambda tap: unite_weight[united_in * tap + channels : united_in * (tap + 1), :], channels
    ).astype(bf16)

    wait_for(flat_core, grad_recv.at[0, extra])
    flat_own[...] = (flat[kept_rows].astype(f32) + flat_core[...].astype(f32)).astype(bf16)
    flat_section[section] = flat_own[flat48]
    for step in range(1, sections):
        other = lax.rem(section + step, sections)
        remote(
            flat_own.at[pl.ds(pl.multiple_of(other * 48, 16), 48)], flat_section.at[section],
            grad_send.at[1, extra], grad_recv.at[1, extra], at(other_section=other),
        ).start()
    to_owner(4)
    lidar_grad[...] = conv_transposed(
        own, lambda tap: unite_weight[united_in * tap : united_in * tap + channels, :], channels
    )
    to_column(1)

    context_grad[...] = lax.dot_general(pooled_grad, histogram[...], transposed_lhs, preferred_element_type=f32)
    table = lax.dot_general(
        context_ref[...], pooled_grad, (((0,), (1,)), ((), ())), preferred_element_type=f32
    )
    wanted = places[...].T.astype(jnp.int32)
    within = lax.rem(wanted, half)
    low = jnp.take_along_axis(table[:, 0:half], within, axis=1)
    high = jnp.take_along_axis(table[:, half : 2 * half], within, axis=1)
    chance_grad = jnp.where(wanted < half, low, high).T
    chance = probability[...]
    places[...] = chance * (chance_grad - jnp.sum(chance_grad * chance, axis=0, keepdims=True))

    def store_bin(number, unused):
        logit_grad[number] = places[pl.ds(number, 1)]
        return 0

    lax.fori_loop(0, bins, store_bin, 0)

    to_owner(3)
    to_column(0)
    wait_for(flat_section.at[pl.ds(0, sections - 1)], grad_recv.at[1, extra])
    piece = total_of(flat_section[number].astype(f32) for number in range(sections)).astype(bf16)
    flat_place = flat_whole.at[row_half, core, flat48, lanes]
    flat_place[...] = over_groups(0, piece, flat_group, extra)
    for step in range(1, chips):
        remote(
            flat_place, flat_place, grad_send.at[2, extra], grad_recv.at[2, extra], at(other=chip_peer(step))
        ).start()
    to_owner(2)
    to_owner(1)
    to_all(0)
    wait_for(flat_whole.at[0, 0, pl.ds(0, 48 * (chips - 1)), pl.ds(0, half)], grad_recv.at[2, extra])
    flat_rows_place = flat_whole.at[:, core, flat48]
    for step in range(1, sections):
        other = lax.rem(section + step, sections)
        remote(
            flat_rows_place, flat_rows_place, grad_send.at[3, extra], grad_recv.at[3, extra],
            at(other_section=other),
        ).start()

    def share_all(back, unused):
        owner_share(stages - 1 - back)
        return 0

    lax.fori_loop(0, stages - 1, share_all, 0)
    share(0)
    wait_for(flat_whole.at[:, 0, pl.ds(0, 48 * (sections - 1))], grad_recv.at[3, extra])
    flat_half = flat_whole.at[:, core]
    remote(flat_half, flat_half, grad_send.at[4, extra], grad_recv.at[4, extra], at(other=sibling)).start()

    wait_for(totals.at[pl.ds(0, sections - 1)], total_recv)
    def summed(stage, row):
        return total_of(totals[number, stage, row : row + 1] for number in range(sections))

    small_out[0] = summed(0, 1)
    small_out[1] = summed(0, 0)
    for number in range(2):
        small_out[2 + 2 * number] = summed(2 * section + 1 + number, 1)
        small_out[3 + 2 * number] = summed(2 * section + 1 + number, 0)
    shared(2 * section + 1)
    shared(2 * section + 2)
    first_copy = pltpu.make_async_copy(whole.at[2 * section + 1], first_out, local_sem.at[5])
    second_copy = pltpu.make_async_copy(whole.at[2 * section + 2], second_out, local_sem.at[6])
    first_copy.start()
    second_copy.start()
    shared(0)
    unite_done = pltpu.make_async_copy(whole.at[0], unite_out, local_sem.at[7])
    unite_done.start()
    wait_for(flat_whole.at[:, 0], grad_recv.at[4, extra])
    camera_done = pltpu.make_async_copy(flat_whole, camera_out, local_sem.at[8])
    camera_done.start()

    wait_for(unite_slots.at[pl.ds(0, peers - 1)], unite_send)
    for step in range(1, chips):
        wait_for(gathered.at[0], raw_send.at[step])
        wait_for(lidars.at[0], lidar_send.at[step])
        wait_for(cameras.at[0], camera_send.at[step])
    for number in range(4):
        wait_for(weights.at[0, part], weight_send.at[number])
    for number in range(2):
        wait_for(weights.at[0, part], relay_send.at[number])
    wait_for(vectors.at[pl.ds(0, sections - 1)], vector_send)
    wait_for(totals.at[pl.ds(0, sections - 1)], total_send)

    def drain_stats(event, unused):
        wait_for(slots.at[event, pl.ds(0, members - 1)], stat_send.at[event])
        return 0

    lax.fori_loop(0, 2 * stages - 1, drain_stats, 0)

    def drain_weights(index, unused):
        @pl.when(section != lax.div(index, 2))
        def _():
            wait_for(weights.at[index, part], pass_send.at[index])
        return 0

    lax.fori_loop(0, 2 * blocks, drain_weights, 0)

    def drain_grads(k, unused):
        wait_for(core_part.at[k], grad_send.at[0, k])
        wait_for(section_part.at[k, pl.ds(0, sections - 1)], grad_send.at[1, k])
        wait_for(whole.at[k, :, 0, 0, pl.ds(0, 16 * (chips - 1)), pl.ds(0, half)], grad_send.at[2, k])
        if groups > 1:
            wait_for(group_part.at[k, pl.ds(0, groups - 1)], group_send.at[k])

        @pl.when((k > 0) & (section != block_of(k)))
        def _():
            wait_for(whole.at[k, :, :, 0, pl.ds(0, 16)], grad_send.at[3, k])

        @pl.when((k > 0) & (section == block_of(k)))
        def _():
            wait_for(whole.at[k, :, :, 0], grad_send.at[4, k])
        return 0

    lax.fori_loop(0, stages, drain_grads, 0)
    wait_for(whole.at[0, :, :, 0, pl.ds(0, 16 * (sections - 1))], grad_send.at[3, 0])
    wait_for(whole.at[0, :, :, 0], grad_send.at[4, 0])
    wait_for(flat_core, grad_send.at[0, extra])
    wait_for(flat_section.at[pl.ds(0, sections - 1)], grad_send.at[1, extra])
    wait_for(flat_whole.at[0, 0, pl.ds(0, 48 * (chips - 1)), pl.ds(0, half)], grad_send.at[2, extra])
    wait_for(flat_whole.at[:, 0, pl.ds(0, 48 * (sections - 1))], grad_send.at[3, extra])
    wait_for(flat_whole.at[:, 0], grad_send.at[4, extra])
    if groups > 1:
        wait_for(flat_group.at[0, pl.ds(0, groups - 1)], group_send.at[extra])
    first_copy.wait()
    second_copy.wait()
    unite_done.wait()
    camera_done.wait()


def widen(cam, *refs):
    held_in, outs, narrow, full = refs[0:9], refs[9:22], refs[22:31], refs[31:34]
    in_sem, out_sem, plain_sem = refs[34:37]
    loads = [pltpu.make_async_copy(a, b, in_sem.at[n]) for n, (a, b) in enumerate(zip(held_in, narrow))]
    for load in loads:
        load.start()
    passed = []
    channels = full[1].shape[-1]

    def store(number, tap):
        return pltpu.make_async_copy(full[number].at[tap], outs[10 + number].at[tap], out_sem.at[number, tap])

    loads[0].wait()
    loads[1].wait()

    def unite_tap(tap, unused):
        full[0][tap, 0:channels] = narrow[0][tap].astype(f32)
        rows = pl.ds(pl.multiple_of(cam * tap, 16), cam)
        full[0][tap, channels : channels + cam] = narrow[1][rows].astype(f32)
        store(0, tap).start()
        return 0

    lax.fori_loop(0, 9, unite_tap, 0)
    for number in (1, 2):
        loads[number + 1].wait()

        def block_tap(tap, unused):
            full[number][tap] = narrow[number + 1][tap].astype(f32)
            store(number, tap).start()
            return 0

        lax.fori_loop(0, 9, block_tap, 0)
    for number in range(4, 9):
        loads[number].wait()
    for number in range(10):
        source = narrow[4 + number] if number < 4 else narrow[8].at[number - 4]
        passed.append(pltpu.make_async_copy(source, outs[number], plain_sem.at[number]))
        passed[-1].start()
    for number in range(3):
        for tap in range(9):
            store(number, tap).wait()
    for copy in passed:
        copy.wait()


def body(
    lidar, context, depth_logits, cell_index, unite_weight, unite_gain, unite_bias, first_weight, second_weight,
    first_gain, first_bias, second_gain, second_bias, cotangent,
):
    peers = lax.axis_size("dp")
    sections = lax.axis_size("section")
    section = lax.axis_index("section")
    channels = cotangent.shape[-1]
    pixels, bins = depth_logits.shape[2:]
    cam = context.shape[-1]
    united_in = unite_weight.shape[1]
    blocks = sections
    stages = 2 * blocks + 1
    events = 2 * stages - 1
    groups = peers // (2 * chips)
    taken = 9 * channels

    vmem = pl.BlockSpec(memory_space=pltpu.VMEM)
    hbm = pl.BlockSpec(memory_space=pltpu.HBM)
    shape = jax.ShapeDtypeStruct
    dma = pltpu.SemaphoreType.DMA
    results = pl.pallas_call(
        functools.partial(kernel, peers, sections),
        out_shape=(
            shape((cells, channels), f32),
            shape((cells, channels), f32),
            shape((cam, pixels), f32),
            shape((bins, 1, pixels), f32),
            shape((9, 2, 2, 64, channels), bf16),
            shape((2, 2, flat_rows // 4, channels), bf16),
            shape((9, 2, 2, 64, channels), bf16),
            shape((9, 2, 2, 64, channels), bf16),
            shape((6, 1, channels), f32),
        ),
        in_specs=[hbm, vmem, vmem, vmem, hbm, vmem, vmem, hbm, hbm, vmem, vmem, vmem, vmem, hbm],
        out_specs=[vmem, vmem, vmem, vmem, hbm, hbm, hbm, hbm, vmem],
        scratch_shapes=[
            pltpu.VMEM((2 * blocks, taken, channels), bf16),
            pltpu.VMEM((9 * united_in, channels), bf16),
            pltpu.VMEM((blocks, 4, channels), f32),
            pltpu.VMEM((cells + 2 * side, 3 * wide), bf16),
            pltpu.VMEM((chips, cells + 2 * side, 3 * channels), bf16),
            pltpu.VMEM((chips, cells, channels), bf16),
            pltpu.VMEM((2 * blocks, chips, cells, channels), bf16),
            pltpu.VMEM((stages, chips, cells, channels), f32),
            pltpu.VMEM((stages + 1, 1, channels), f32),
            pltpu.VMEM((chips, cells, channels), f32),
            pltpu.VMEM((chips, cells, channels), bf16),
            pltpu.VMEM((chips, cells, channels), bf16),
            pltpu.VMEM((chips, cells, channels), bf16),
            pltpu.VMEM((chips, cells, half), bf16),
            pltpu.VMEM((events, 2, channels), f32),
            pltpu.VMEM((events, 2 * groups, 2, channels), f32),
            pltpu.VMEM((2, channels), f32),
            pltpu.VMEM((peers, 2, channels), f32),
            pltpu.VMEM((half, pixels), f32),
            pltpu.VMEM((half, pixels), f32),
            pltpu.VMEM((cells, pixels), bf16),
            pltpu.VMEM((stages, 9, 2, 64, half), bf16),
            pltpu.VMEM((stages, 9, 64, half), bf16),
            pltpu.VMEM((stages, 9, 64, half), bf16),
            pltpu.VMEM((stages, sections, 9, 16, half), bf16),
            pltpu.VMEM((stages, 9, 2, 2, 64, channels), bf16),
            pltpu.VMEM((flat_rows, half), bf16),
            pltpu.VMEM((flat_rows // 4, half), bf16),
            pltpu.VMEM((flat_rows // 4, half), bf16),
            pltpu.VMEM((sections, 48, half), bf16),
            pltpu.VMEM((2, 2, flat_rows // 4, channels), bf16),
            pltpu.VMEM((sections, stages, 2, channels), f32),
            pltpu.VMEM((stages if groups > 1 else 1, groups, 9, 16, half), bf16),
            pltpu.VMEM((1, groups, 48, half), bf16),
            dma((9,)), dma, dma, dma((events,)), dma((events,)), dma((chips,)), dma((chips,)), dma((chips,)),
            dma((chips,)), dma((chips,)), dma((chips,)), dma((chips,)), dma((chips,)), dma((4,)),
            dma((2 * blocks,)), dma((2,)), dma((2 * blocks,)), dma((2 * blocks,)), dma, dma,
            dma((5, stages + 1)), dma((5, stages + 1)), dma, dma, dma((stages + 1,)), dma((stages + 1,)),
        ],
        compiler_params=pltpu.CompilerParams(
            collective_id=0, has_side_effects=True, vmem_limit_bytes=56 << 20
        ),
    )(
        lidar.reshape(cells, channels), context.reshape(pixels, cam).T, depth_logits.reshape(pixels, bins).T,
        jnp.transpose(cell_index, (0, 3, 1, 2)).reshape(bins, 1, pixels), unite_weight.reshape(-1, channels),
        unite_gain[None], unite_bias[None], first_weight.reshape(taken, channels),
        second_weight.reshape(taken, channels), first_gain, first_bias, second_gain, second_bias,
        cotangent.reshape(-1, cells, channels),
    )

    act, lidar_grad, context_grad, logit_grad, *small, unite_whole, first_whole, second_whole = pl.pallas_call(
        functools.partial(widen, cam),
        out_shape=(
            shape((cells, channels), f32),
            shape((cells, channels), f32),
            shape((cam, pixels), f32),
            shape((bins, 1, pixels), f32),
            *[shape((1, channels), f32)] * 6,
            shape((9, united_in, channels), f32),
            shape((9, channels, channels), f32),
            shape((9, channels, channels), f32),
        ),
        in_specs=[hbm] * 9,
        out_specs=[hbm] * 13,
        scratch_shapes=[
            pltpu.VMEM((9, channels, channels), bf16),
            pltpu.VMEM((flat_rows, channels), bf16),
            pltpu.VMEM((9, channels, channels), bf16),
            pltpu.VMEM((9, channels, channels), bf16),
            pltpu.VMEM((cells, channels), f32),
            pltpu.VMEM((cells, channels), f32),
            pltpu.VMEM((cam, pixels), f32),
            pltpu.VMEM((bins, 1, pixels), f32),
            pltpu.VMEM((6, 1, channels), f32),
            pltpu.VMEM((9, united_in, channels), f32),
            pltpu.VMEM((9, channels, channels), f32),
            pltpu.VMEM((9, channels, channels), f32),
            dma((9,)), dma((3, 9)), dma((10,)),
        ],
        compiler_params=pltpu.CompilerParams(vmem_limit_bytes=60 << 20),
    )(
        results[4].reshape(9, channels, channels), results[5].reshape(flat_rows, channels),
        results[6].reshape(9, channels, channels), results[7].reshape(9, channels, channels), *results[0:4], results[8],
    )
    return (
        act.reshape(lidar.shape),
        lidar_grad.reshape(lidar.shape),
        context_grad.T.reshape(context.shape),
        jnp.transpose(logit_grad.reshape(1, bins, 1, pixels), (0, 2, 3, 1)),
        unite_whole,
        small[0].reshape(channels),
        small[1].reshape(channels),
        first_whole.reshape(first_weight.shape),
        second_whole.reshape(second_weight.shape),
        *small[2:6],
    )


def solution(mesh):
    split, by_dp = P("section"), P("section", "dp")
    in_specs = (by_dp, by_dp, by_dp, by_dp, P(), P(), P(), split, split, split, split, split, split, P(None, "dp"))
    out_specs = (by_dp, by_dp, by_dp, by_dp, P(), P(), P(), split, split, split, split, split, split)
    return jax.shard_map(body, mesh=mesh, in_specs=in_specs, out_specs=out_specs, check_vma=False)
```

```python
import functools

import jax
import jax.numpy as jnp
from jax import lax
from jax.experimental import pallas as pl
from jax.experimental.pallas import tpu as pltpu
from jax.sharding import PartitionSpec as P

eps = 1e-05
f32, bf16 = jnp.float32, jnp.bfloat16
MESH = pl.DeviceIdType.MESH
side = 16
cells = side * side
wide = 384
chips = 4
half = 128
flat_rows = 768
transposed_rhs = (((1,), (1,)), ((), ()))
transposed_lhs = (((0,), (0,)), ((), ()))


def sigmoid(value):
    return 0.5 * jnp.tanh(0.5 * value) + 0.5


def slope(value):
    gate = sigmoid(value)
    return gate * (1.0 + value * (1.0 - gate))


def silu(value):
    return value * sigmoid(value)


def put_shifted(buffer, value, stride, offset=0):
    column = lax.broadcasted_iota(jnp.int32, (cells, 1), 0) % side
    width = value.shape[1]
    before = jnp.where(column == 0, 0.0, pltpu.roll(value, 1, 0))
    after = jnp.where(column == side - 1, 0.0, pltpu.roll(value, cells - 1, 0))
    for group, shifted in enumerate((before, value, after)):
        start = group * stride + offset
        buffer[side : side + cells, start : start + width] = shifted.astype(bf16)


def total_of(terms):
    total = None
    for term in terms:
        total = term if total is None else total + term
    return total


def conv(buffer, weight):
    return total_of(
        jnp.dot(buffer[side * i : side * i + cells, :], weight(i), preferred_element_type=f32) for i in range(3)
    )


def conv_transposed(buffer, weight, width):
    return total_of(
        lax.dot_general(
            buffer[side * (2 - i) : side * (2 - i) + cells, width * (2 - j) : width * (3 - j)],
            weight(3 * i + j),
            transposed_rhs,
            preferred_element_type=f32,
        )
        for i in range(3)
        for j in range(3)
    )


plan = {
    "start": [("offer", 0, "near", 0), ("offer", 0, "far", 3), ("offer", 0, "near", 2), ("offer", 0, "near", 1)],
    "lift2": [("offer", 0, "near", 3), ("offer", 1, "near", 0)],
    "united": [("relay", 0, 0), ("offer", 1, "near", 1), ("offer", 1, "near", 3)],
    "united2": [("offer", 1, "far", 0), ("offer", 1, "near", 2), ("offer", 0, "far", 1)],
    "merged": [("offer", 0, "far", 0), ("relay", 1, 0)],
    "entered1": [("relay", 3, 0), ("relay", 0, 1), ("relay", 2, 0)],
    "entered3": [("offer", 0, "far", 2), ("offer", 1, "far", 1)],
    "entered2": [("relay", 2, 1)],
    "entered": [("offer", 1, "far", 2), ("arrive", 0, 0)],
    ("first", 0): [("relay", 1, 1), ("arrive", 1, 0), ("offer", 1, "far", 3), ("arrive", 0, 1)],
    ("second", 0): [("relay", 3, 1)],
    ("first", 1): [("arrive", 1, 1), ("arrive", 2, 0)],
    ("second", 1): [("arrive", 3, 0), ("arrive", 2, 1)],
    ("second", 2): [("arrive", 3, 1)],
}


def kernel(
    peers, sections,
    lidar_ref, context_ref, logit_ref, cell_ref, unite_ref, unite_gain, unite_bias, first_ref, second_ref,
    first_gain, first_bias, second_gain, second_bias, cotangent_ref,
    act_ref, lidar_grad, context_grad, logit_grad, unite_out, camera_out, first_out, second_out, small_out,
    weights, unite_weight, vectors, joined, shifted, current, kept, normed, scales, held, gathered, upstream,
    lidars, cameras, mine, slots, unite_mine, unite_slots, probability, places, histogram,
    partial, core_part, own_part, section_part, whole, flat, flat_core, flat_own, flat_section, flat_whole,
    totals, group_part, flat_group,
    local_sem, unite_send, unite_recv, stat_send, stat_recv, raw_send, raw_recv, cot_send, cot_recv,
    lidar_send, lidar_recv, camera_send, camera_recv, weight_send, weight_recv, relay_send, pass_send, pass_recv,
    vector_send, vector_recv, grad_send, grad_recv, total_send, total_recv, group_send, group_recv,
):
    me = lax.axis_index("dp")
    section = lax.axis_index("section")
    core = lax.rem(me, 2)
    chip = lax.rem(lax.div(me, 2), chips)
    group = lax.div(me, 2 * chips)
    groups = peers // (2 * chips)
    blocks = sections
    stages = 2 * blocks + 1
    channels = vectors.shape[-1]
    bins = logit_ref.shape[0]
    cam = context_ref.shape[0]
    united_in = channels + cam
    taken = 9 * channels
    row_half = lax.div(chip, 2)
    lane_half = lax.rem(chip, 2)
    count = float(peers * cells)

    def at(other_section=None, other=None):
        return (section if other_section is None else other_section, me if other is None else other)

    def chip_peer(step):
        return group * (2 * chips) + lax.rem(chip + step, chips) * 2 + core

    sibling = me + 1 - 2 * core

    def remote(source, target, send, recv, device):
        return pltpu.make_async_remote_copy(
            src_ref=source, dst_ref=target, send_sem=send, recv_sem=recv, device_id=device, device_id_type=MESH
        )

    def wait_for(part, semaphore):
        pltpu.make_async_copy(part, part, semaphore).wait()

    barrier = pltpu.get_barrier_semaphore()
    for step in range(1, sections):
        pl.semaphore_signal(
            barrier, inc=1, device_id=at(other_section=lax.rem(section + step, sections)), device_id_type=MESH
        )

    def greet(step, unused):
        pl.semaphore_signal(barrier, inc=1, device_id=at(other=lax.rem(me + step, peers)), device_id_type=MESH)
        return 0

    lax.fori_loop(1, peers, greet, 0)

    unite_copy = pltpu.make_async_copy(unite_ref, unite_weight, local_sem.at[0])
    own_first = pltpu.make_async_copy(first_ref, weights.at[2 * section], local_sem.at[1])
    own_second = pltpu.make_async_copy(second_ref, weights.at[2 * section + 1], local_sem.at[2])
    own_cot = pltpu.make_async_copy(cotangent_ref.at[section], upstream.at[chip], local_sem.at[3])
    own_lidar = pltpu.make_async_copy(lidar_ref, lidars.at[chip], local_sem.at[4])
    own_lidar.start()
    unite_copy.start()
    own_first.start()
    own_second.start()
    own_cot.start()
    for number, part in enumerate((first_gain, first_bias, second_gain, second_bias)):
        vectors[section, number : number + 1] = part[...]
    joined[...] = jnp.zeros_like(joined)
    probability[...] = jnp.zeros_like(probability)
    places[...] = jnp.zeros_like(places)
    cameras[chip] = jnp.zeros((cells, half), bf16)
    pl.semaphore_wait(barrier, peers - 1 + sections - 1)

    beside = section + 1 - 2 * lax.rem(section, 2)
    across = lax.rem(section + 2, sections)
    near = beside + core * (across - beside)
    far = across + core * (beside - across)
    part_rows = taken // 2
    part = pl.ds(pl.multiple_of(core * part_rows, part_rows), part_rows)
    sources = (first_ref, second_ref)

    def offer(which, target, number):
        index = 2 * section + which
        remote(
            sources[which].at[part], weights.at[index, part], weight_send.at[number], weight_recv.at[index],
            at(other_section=target),
        ).start()

    def arrived(index):
        wait_for(weights.at[index, part], weight_recv.at[index])

    def pass_on(index):
        remote(
            weights.at[index, part], weights.at[index, part], pass_send.at[index], pass_recv.at[index],
            at(other=sibling),
        ).start()

    def relay(block, which):
        index = 2 * block + which

        @pl.when(near == block)
        def _():
            arrived(index)
            remote(
                weights.at[index, part], weights.at[index, part], relay_send.at[which], weight_recv.at[index],
                at(other_section=far),
            ).start()
            pass_on(index)

    def arrive(block, which):
        index = 2 * block + which

        @pl.when((section != block) & (near != block))
        def _():
            arrived(index)
            pass_on(index)

    def ready(block, which):
        index = 2 * block + which
        rest = pl.ds(pl.multiple_of((1 - core) * part_rows, part_rows), part_rows)

        @pl.when(section != block)
        def _():
            wait_for(weights.at[index, rest], pass_recv.at[index])

        @pl.when(section == block)
        def _():
            (own_second if which else own_first).wait()

    def act_on(entry):
        name, one, two = entry[0:3]
        if name == "relay":
            relay(one, two)
        elif name == "arrive":
            arrive(one, two)
        else:
            @pl.when(section == entry[3])
            def _():
                offer(one, near if two == "near" else far, 2 * one + (two == "far"))

    def point(name, block=None):
        for key, entries in plan.items():
            if isinstance(key, tuple) and key[0] == name:
                @pl.when(block == key[1])
                def _():
                    for entry in entries:
                        act_on(entry)
            elif key == name:
                for entry in entries:
                    act_on(entry)

    point("start")
    for step in range(1, sections):
        remote(
            vectors.at[section], vectors.at[section], vector_send, vector_recv,
            at(other_section=lax.rem(section + step, sections)),
        ).start()

    logits = logit_ref[...].astype(f32)
    raised = jnp.exp(logits - jnp.max(logits, axis=0, keepdims=True))
    probability[0:bins] = raised / jnp.sum(raised, axis=0, keepdims=True)
    address = lax.broadcasted_iota(jnp.int32, (cells, half), 0)

    def add_bin(number, total):
        place = cell_ref[number]
        places[pl.ds(number, 1)] = place.astype(f32)
        return total + jnp.where(place == address, probability[pl.ds(number, 1)], 0.0)

    counted = jnp.zeros((cells, half), f32)
    for number in range(3):
        counted = lax.fori_loop(bins * number // 3, bins * (number + 1) // 3, add_bin, counted)
        if number < 2:
            point(f"lift{number + 1}")
    counted = counted.astype(bf16)
    histogram[...] = counted
    pooled = lax.dot_general(counted, context_ref[...], transposed_rhs, preferred_element_type=f32)
    cameras[chip, :, 0:cam] = pooled.astype(bf16)

    own_lidar.wait()
    put_shifted(joined, lidars[chip].astype(f32), wide)
    put_shifted(joined, pooled, wide, channels)
    unite_copy.wait()
    united = total_of(
        jnp.dot(
            joined[side * i : side * i + cells, wide * j : wide * j + united_in],
            unite_weight[united_in * (3 * i + j) : united_in * (3 * i + j + 1), :],
            preferred_element_type=f32,
        )
        for i in range(3)
        for j in range(3)
    )
    gathered[chip] = united.astype(bf16)
    for step in range(1, chips):
        remote(
            gathered.at[chip], gathered.at[chip], raw_send.at[step], raw_recv.at[step], at(other=chip_peer(step))
        ).start()
    center = jnp.sum(united, axis=0, keepdims=True) * (1.0 / cells)
    offsets = united - center
    unite_mine[0:1] = center
    unite_mine[1:2] = jnp.sum(offsets * offsets, axis=0, keepdims=True)
    unite_slots[me] = unite_mine[...]

    def send_unite(step, unused):
        remote(
            unite_mine, unite_slots.at[me], unite_send, unite_recv, at(other=lax.rem(me + step, peers))
        ).start()
        return 0

    lax.fori_loop(1, peers, send_unite, 0)

    point("united")
    shifted[...] = jnp.zeros_like(shifted)
    flat[9 * cam :, :] = jnp.zeros((flat_rows - 9 * cam, half), bf16)

    def merged(centers, squares, each):
        parts = centers.shape[0]
        center = jnp.sum(centers, axis=0, keepdims=True) * (1.0 / parts)
        apart = centers - center
        square = jnp.sum(squares, axis=0, keepdims=True) + each * jnp.sum(apart * apart, axis=0, keepdims=True)
        return center, square

    point("united2")
    wait_for(unite_slots.at[pl.ds(0, peers - 1)], unite_recv)
    center, square = merged(unite_slots[:, 0, :], unite_slots[:, 1, :], cells)
    scales[0] = lax.rsqrt(square * (1.0 / count) + eps)
    scales[stages] = center
    point("merged")

    def enter(number):
        value = (gathered[number].astype(f32) - scales[stages]) * scales[0]
        normed[0, number] = value
        entering = silu(unite_gain[...] * value + unite_bias[...])
        current[number] = entering.astype(bf16)
        kept[0, number] = entering.astype(bf16)
        put_shifted(shifted.at[number], entering, channels)

    enter(chip)
    for step in (1, 3, 2):
        wait_for(gathered.at[0], raw_recv.at[step])
        enter(lax.rem(chip - step + chips, chips))
        point(f"entered{step}")

    own_cot.wait()
    for step in range(1, chips):
        peer = at(other=chip_peer(step))
        remote(upstream.at[chip], upstream.at[chip], cot_send.at[step], cot_recv.at[step], peer).start()
    for step in range(1, chips):
        peer = at(other=chip_peer(step))
        remote(lidars.at[chip], lidars.at[chip], lidar_send.at[step], lidar_recv.at[step], peer).start()
        remote(cameras.at[chip], cameras.at[chip], camera_send.at[step], camera_recv.at[step], peer).start()

    point("entered")
    wait_for(vectors.at[pl.ds(0, sections - 1)], vector_recv)

    members = 2 * groups
    place = group * 2 + core

    def copy_stats(event, step):
        to = lax.rem(place + step, members)
        return remote(
            mine.at[event], slots.at[event, place], stat_send.at[event], stat_recv.at[event],
            at(other=lax.div(to, 2) * (2 * chips) + chip * 2 + lax.rem(to, 2)),
        )

    def send_stats(event, first, second):
        mine[event, 0:1] = first
        mine[event, 1:2] = second
        slots[event, place] = mine[event]
        for step in range(1, members):
            copy_stats(event, step).start()

    def take_stats(event):
        wait_for(slots.at[event, pl.ds(0, members - 1)], stat_recv.at[event])
        return slots[event, :, 0, :], slots[event, :, 1, :]

    def forward_stage(stage, weight, meanwhile, use):
        centers, squares = [], []
        for number in range(chips):
            activ = conv(shifted.at[number], weight)
            held[number] = activ
            center = jnp.sum(activ, axis=0, keepdims=True) * (1.0 / cells)
            offsets = activ - center
            centers.append(center)
            squares.append(jnp.sum(offsets * offsets, axis=0, keepdims=True))
        center, square = merged(jnp.concatenate(centers, axis=0), jnp.concatenate(squares, axis=0), cells)
        send_stats(stage - 1, center, square)
        meanwhile()
        centers, squares = take_stats(stage - 1)
        center, square = merged(centers, squares, chips * cells)
        scale = lax.rsqrt(square * (1.0 / count) + eps)
        scales[stage] = scale
        for number in range(chips):
            value = (held[number] - center) * scale
            normed[stage, number] = value
            use(number, value)

    def block(s, unused):
        stage = 2 * s + 1

        def vector(number):
            return vectors[s, number : number + 1]

        def during_first():
            point("first", s)

        def during_second():
            point("second", s)

        def use_first(number, value):
            hidden = silu(vector(0) * value + vector(1))
            kept[stage, number] = hidden.astype(bf16)
            put_shifted(shifted.at[number], hidden, channels)

        def use_second(number, value):
            output = current[number].astype(f32) + silu(vector(2) * value + vector(3))
            held[number] = output
            current[number] = output.astype(bf16)

            @pl.when(s < blocks - 1)
            def _():
                kept[stage + 1, number] = output.astype(bf16)
                put_shifted(shifted.at[number], output, channels)

        ready(s, 0)
        forward_stage(
            stage, lambda i: weights[2 * s, 3 * channels * i : 3 * channels * (i + 1), :], during_first, use_first
        )
        ready(s, 1)
        forward_stage(
            stage + 1, lambda i: weights[2 * s + 1, 3 * channels * i : 3 * channels * (i + 1), :],
            during_second, use_second,
        )
        return 0

    lax.fori_loop(0, blocks, block, 0)
    act_ref[...] = held[chip]

    lanes = pl.ds(pl.multiple_of(lane_half * half, half), half)
    flat48 = pl.ds(pl.multiple_of(section * 48, 16), 48)

    def lateral(j):
        return pl.ds(pl.multiple_of(channels * (2 - j) + lane_half * half, half), half)

    def weight_grad(stage, inputs):
        columns = pl.ds(pl.multiple_of(row_half * half, half), half)
        values = [inputs[number, :, columns] for number in range(chips)]
        for i in range(3):
            for j in range(3):
                taps = total_of(
                    lax.dot_general(
                        values[number],
                        shifted[number, side * (2 - i) : side * (2 - i) + cells, lateral(j)],
                        transposed_lhs,
                        preferred_element_type=f32,
                    )
                    for number in range(chips)
                ).astype(bf16)
                partial[stage, 3 * i + j, 0] = taps[0:64]
                partial[stage, 3 * i + j, 1] = taps[64:128]
        to_sibling(stage)

    def to_sibling(k):
        remote(
            partial.at[k, :, 1 - core], core_part.at[k], grad_send.at[0, k], grad_recv.at[0, k], at(other=sibling)
        ).start()

    def block_of(k):
        return lax.div(k - 1, 2)

    def roles(k):
        block = block_of(k)
        across_x = block + 1 - 2 * lax.rem(block, 2)
        across_y = lax.rem(block + 2, sections)
        return block, sections - 1 - block, across_x + core * (across_y - across_x)

    def tile(index):
        return pl.ds(pl.multiple_of(index * 16, 16), 16)

    def sum_cores(k):
        wait_for(core_part.at[k], grad_recv.at[0, k])
        for tap in range(9):
            own_part[k, tap] = (partial[k, tap, core].astype(f32) + core_part[k, tap].astype(f32)).astype(bf16)

    def send_tile(k, index, slot, other):
        remote(
            own_part.at[k, :, tile(index)], section_part.at[k, slot, section], grad_send.at[1, k], grad_recv.at[1, k],
            at(other_section=other),
        ).start()

    def to_sections(k):
        sum_cores(k)
        block, diagonal, helper = roles(k)
        for step in range(1, sections):
            other = lax.rem(section + step, sections)

            @pl.when(other != diagonal)
            def _():
                send_tile(k, other, 0, other)

            @pl.when(other == helper)
            def _():
                send_tile(k, diagonal, 1, other)

        section_part[k, 0, section] = own_part[k, :, tile(section)]

        @pl.when(section == helper)
        def _():
            section_part[k, 1, section] = own_part[k, :, tile(diagonal)]

    def over_groups(slot, k, value, buffer, number):
        if groups == 1:
            return value
        mine_here = buffer.at[k, slot, group]
        mine_here[...] = value
        for step in range(1, groups):
            to = lax.rem(group + step, groups) * (2 * chips) + chip * 2 + core
            remote(
                mine_here, mine_here, group_send.at[slot, number], group_recv.at[slot, number], at(other=to)
            ).start()
        wait_for(buffer.at[k, slot, pl.ds(0, groups - 1)], group_recv.at[slot, number])
        return jnp.sum(buffer[k, slot].astype(f32), axis=0).astype(bf16)

    def reduce_tile(k, slot, index):
        piece = total_of(section_part[k, slot, number].astype(f32) for number in range(sections)).astype(bf16)
        place = whole.at[k, :, row_half, core, tile(index), lanes]
        place[...] = over_groups(slot, k, piece, group_part, k)
        for step in range(1, chips):
            remote(place, place, grad_send.at[2, k], grad_recv.at[2, k], at(other=chip_peer(step))).start()

    def to_column(k):
        block, diagonal, helper = roles(k)

        @pl.when(section == helper)
        def _():
            wait_for(section_part.at[k, :, pl.ds(0, sections - 1)], grad_recv.at[1, k])
            reduce_tile(k, 0, section)
            reduce_tile(k, 1, diagonal)

        @pl.when((section != helper) & (section != diagonal))
        def _():
            wait_for(section_part.at[k, 0, pl.ds(0, sections - 1)], grad_recv.at[1, k])
            reduce_tile(k, 0, section)

    def column_part(k, tiles):
        return whole.at[k, :, 0, 0, pl.ds(0, 16 * (chips - 1)), pl.ds(0, half * tiles)]

    def hand_over(k, index, block):
        place = whole.at[k, :, :, core, tile(index)]
        remote(place, place, grad_send.at[3, k], grad_recv.at[3, k], at(other_section=block)).start()

    def to_owner(k):
        block, diagonal, helper = roles(k)

        @pl.when(section == helper)
        def _():
            wait_for(column_part(k, 2), grad_recv.at[2, k])
            hand_over(k, section, block)
            hand_over(k, diagonal, block)

        @pl.when((section != helper) & (section != diagonal))
        def _():
            wait_for(column_part(k, 1), grad_recv.at[2, k])

            @pl.when(section != block)
            def _():
                hand_over(k, section, block)

    def to_sections_all(k):
        sum_cores(k)
        section_part[k, 0, section] = own_part[k, :, tile(section)]
        for step in range(1, sections):
            other = lax.rem(section + step, sections)
            send_tile(k, other, 0, other)

    def to_column_all(k):
        wait_for(section_part.at[k, 0, pl.ds(0, sections - 1)], grad_recv.at[1, k])
        reduce_tile(k, 0, section)

    def to_all(k):
        wait_for(column_part(k, 1), grad_recv.at[2, k])
        place = whole.at[k, :, :, core, tile(section)]
        for step in range(1, sections):
            other = lax.rem(section + step, sections)
            remote(place, place, grad_send.at[3, k], grad_recv.at[3, k], at(other_section=other)).start()

    def share(k):
        wait_for(whole.at[k, :, :, 0, pl.ds(0, 16 * (sections - 1))], grad_recv.at[3, k])
        place = whole.at[k, :, :, core]
        remote(place, place, grad_send.at[4, k], grad_recv.at[4, k], at(other=sibling)).start()

    def owner_share(k):
        @pl.when(section == block_of(k))
        def _():
            share(k)

    def shared(k):
        wait_for(whole.at[k, :, :, 0], grad_recv.at[4, k])

    def when_due(k, act):
        @pl.when(k <= stages - 1)
        def _():
            act(k)

    def backward_stage(stage, gain, bias, gradient, meanwhile):
        event = stages - 1 + stage
        firsts, seconds = None, None
        for number in range(chips):
            value = normed[stage, number]
            grads = gradient(number) * slope(gain * value + bias)
            held[number] = grads
            first = jnp.sum(grads, axis=0, keepdims=True)
            second = jnp.sum(grads * value, axis=0, keepdims=True)
            firsts = first if firsts is None else firsts + first
            seconds = second if seconds is None else seconds + second
        send_stats(event, firsts, seconds)
        meanwhile()
        first, second = take_stats(event)
        first = jnp.sum(first, axis=0, keepdims=True)
        second = jnp.sum(second, axis=0, keepdims=True)
        totals[section, stage, 0:1] = first
        totals[section, stage, 1:2] = second
        first = first * (1.0 / count)
        second = second * (1.0 / count)
        factor = gain * scales[stage]
        for number in range(chips):
            put_shifted(
                shifted.at[number], factor * (held[number] - first - normed[stage, number] * second), channels
            )

    for step in range(1, chips):
        wait_for(upstream.at[0], cot_recv.at[step])
        wait_for(upstream.at[0], cot_send.at[step])

    def block_back(back, unused):
        s = blocks - 1 - back
        stage = 2 * s + 1

        def vector(number):
            return vectors[s, number : number + 1]

        def during_second():
            @pl.when(back > 0)
            def _():
                weight_grad(stage + 2, kept.at[stage + 1])
            when_due(stage + 4, to_column)

        def during_first():
            weight_grad(stage + 1, kept.at[stage])
            when_due(stage + 3, to_column)

        backward_stage(stage + 1, vector(2), vector(3), lambda number: upstream[number].astype(f32), during_second)
        for number in range(chips):
            held[number] = conv_transposed(
                shifted.at[number], lambda tap: weights[2 * s + 1, channels * tap : channels * (tap + 1), :], channels
            )
        when_due(stage + 2, to_sections)
        when_due(stage + 5, to_owner)
        backward_stage(stage, vector(0), vector(1), lambda number: held[number], during_first)
        for number in range(chips):
            passed = conv_transposed(
                shifted.at[number], lambda tap: weights[2 * s, channels * tap : channels * (tap + 1), :], channels
            )
            upstream[number] = (upstream[number].astype(f32) + passed).astype(bf16)
        when_due(stage + 1, to_sections)
        when_due(stage + 4, to_owner)
        return 0

    lax.fori_loop(0, blocks, block_back, 0)

    def during_unite():
        weight_grad(1, kept.at[0])
        to_column(3)

    backward_stage(
        0, unite_gain[...], unite_bias[...], lambda number: upstream[number].astype(f32), during_unite
    )
    for step in range(1, chips):
        wait_for(lidars.at[0], lidar_recv.at[step])
        wait_for(cameras.at[0], camera_recv.at[step])
    weight_grad(0, lidars)
    to_sections(1)
    held_cameras = [cameras[number] for number in range(chips)]
    for i in range(3):
        for j in range(3):
            taps = total_of(
                lax.dot_general(
                    held_cameras[number],
                    shifted[number, side * (2 - i) : side * (2 - i) + cells, lateral(j)],
                    transposed_lhs,
                    preferred_element_type=f32,
                )
                for number in range(chips)
            ).astype(bf16)
            flat[cam * (3 * i + j) : cam * (3 * i + j + 1)] = taps[0:cam]
    quarter = flat_rows // 4
    kept_rows = pl.ds(pl.multiple_of(row_half * (2 * quarter) + core * quarter, 16), quarter)
    sent_rows = pl.ds(pl.multiple_of(row_half * (2 * quarter) + (1 - core) * quarter, 16), quarter)
    extra = stages
    remote(
        flat.at[sent_rows], flat_core, grad_send.at[0, extra], grad_recv.at[0, extra], at(other=sibling)
    ).start()
    to_sections_all(0)
    to_column(2)
    for step in range(1, sections):
        remote(
            totals.at[section], totals.at[section], total_send, total_recv,
            at(other_section=lax.rem(section + step, sections)),
        ).start()
    own = shifted.at[chip]
    pooled_grad = conv_transposed(
        own, lambda tap: unite_weight[united_in * tap + channels : united_in * (tap + 1), :], channels
    ).astype(bf16)

    wait_for(flat_core, grad_recv.at[0, extra])
    flat_own[...] = (flat[kept_rows].astype(f32) + flat_core[...].astype(f32)).astype(bf16)
    flat_section[section] = flat_own[flat48]
    for step in range(1, sections):
        other = lax.rem(section + step, sections)
        remote(
            flat_own.at[pl.ds(pl.multiple_of(other * 48, 16), 48)], flat_section.at[section],
            grad_send.at[1, extra], grad_recv.at[1, extra], at(other_section=other),
        ).start()
    to_owner(4)
    lidar_grad[...] = conv_transposed(
        own, lambda tap: unite_weight[united_in * tap : united_in * tap + channels, :], channels
    )
    to_column(1)

    context_grad[...] = lax.dot_general(pooled_grad, histogram[...], transposed_lhs, preferred_element_type=f32)
    table = lax.dot_general(
        context_ref[...], pooled_grad, (((0,), (1,)), ((), ())), preferred_element_type=f32
    )
    wanted = places[...].T.astype(jnp.int32)
    within = lax.rem(wanted, half)
    low = jnp.take_along_axis(table[:, 0:half], within, axis=1)
    high = jnp.take_along_axis(table[:, half : 2 * half], within, axis=1)
    chance_grad = jnp.where(wanted < half, low, high).T
    chance = probability[...]
    places[...] = chance * (chance_grad - jnp.sum(chance_grad * chance, axis=0, keepdims=True))

    def store_bin(number, unused):
        logit_grad[number] = places[pl.ds(number, 1)]
        return 0

    lax.fori_loop(0, bins, store_bin, 0)

    to_owner(3)
    to_column_all(0)
    wait_for(flat_section.at[pl.ds(0, sections - 1)], grad_recv.at[1, extra])
    piece = total_of(flat_section[number].astype(f32) for number in range(sections)).astype(bf16)
    flat_place = flat_whole.at[row_half, core, flat48, lanes]
    flat_place[...] = over_groups(0, 0, piece, flat_group, extra)
    for step in range(1, chips):
        remote(
            flat_place, flat_place, grad_send.at[2, extra], grad_recv.at[2, extra], at(other=chip_peer(step))
        ).start()
    to_owner(2)
    to_owner(1)
    to_all(0)
    wait_for(flat_whole.at[0, 0, pl.ds(0, 48 * (chips - 1)), pl.ds(0, half)], grad_recv.at[2, extra])
    flat_rows_place = flat_whole.at[:, core, flat48]
    for step in range(1, sections):
        other = lax.rem(section + step, sections)
        remote(
            flat_rows_place, flat_rows_place, grad_send.at[3, extra], grad_recv.at[3, extra],
            at(other_section=other),
        ).start()

    def share_all(back, unused):
        owner_share(stages - 1 - back)
        return 0

    lax.fori_loop(0, stages - 1, share_all, 0)
    share(0)
    wait_for(flat_whole.at[:, 0, pl.ds(0, 48 * (sections - 1))], grad_recv.at[3, extra])
    flat_half = flat_whole.at[:, core]
    remote(flat_half, flat_half, grad_send.at[4, extra], grad_recv.at[4, extra], at(other=sibling)).start()

    wait_for(totals.at[pl.ds(0, sections - 1)], total_recv)
    def summed(stage, row):
        return total_of(totals[number, stage, row : row + 1] for number in range(sections))

    small_out[0] = summed(0, 1)
    small_out[1] = summed(0, 0)
    for number in range(2):
        small_out[2 + 2 * number] = summed(2 * section + 1 + number, 1)
        small_out[3 + 2 * number] = summed(2 * section + 1 + number, 0)
    shared(2 * section + 1)
    shared(2 * section + 2)
    first_copy = pltpu.make_async_copy(whole.at[2 * section + 1], first_out, local_sem.at[5])
    second_copy = pltpu.make_async_copy(whole.at[2 * section + 2], second_out, local_sem.at[6])
    first_copy.start()
    second_copy.start()
    shared(0)
    unite_done = pltpu.make_async_copy(whole.at[0], unite_out, local_sem.at[7])
    unite_done.start()
    wait_for(flat_whole.at[:, 0], grad_recv.at[4, extra])
    camera_done = pltpu.make_async_copy(flat_whole, camera_out, local_sem.at[8])
    camera_done.start()

    wait_for(unite_slots.at[pl.ds(0, peers - 1)], unite_send)
    for step in range(1, chips):
        wait_for(gathered.at[0], raw_send.at[step])
        wait_for(lidars.at[0], lidar_send.at[step])
        wait_for(cameras.at[0], camera_send.at[step])
    for number in range(4):
        wait_for(weights.at[0, part], weight_send.at[number])
    for number in range(2):
        wait_for(weights.at[0, part], relay_send.at[number])
    wait_for(vectors.at[pl.ds(0, sections - 1)], vector_send)
    wait_for(totals.at[pl.ds(0, sections - 1)], total_send)

    def drain_stats(event, unused):
        wait_for(slots.at[event, pl.ds(0, members - 1)], stat_send.at[event])
        return 0

    lax.fori_loop(0, 2 * stages - 1, drain_stats, 0)

    def drain_weights(index, unused):
        @pl.when(section != lax.div(index, 2))
        def _():
            wait_for(weights.at[index, part], pass_send.at[index])
        return 0

    lax.fori_loop(0, 2 * blocks, drain_weights, 0)

    def drain_grads(k, unused):
        block, diagonal, helper = roles(k)
        own_tiles = section_part.at[k, 0]
        column = whole.at[k, :, :, 0]
        wait_for(core_part.at[k], grad_send.at[0, k])

        @pl.when(section == diagonal)
        def _():
            wait_for(own_tiles.at[pl.ds(0, 4)], grad_send.at[1, k])

        @pl.when(section == helper)
        def _():
            wait_for(own_tiles.at[pl.ds(0, 2)], grad_send.at[1, k])
            wait_for(column_part(k, 2), grad_send.at[2, k])
            wait_for(column.at[:, :, pl.ds(0, 32)], grad_send.at[3, k])

        @pl.when((section != helper) & (section != diagonal))
        def _():
            wait_for(own_tiles.at[pl.ds(0, 3)], grad_send.at[1, k])
            wait_for(column_part(k, 1), grad_send.at[2, k])

            @pl.when(section != block)
            def _():
                wait_for(column.at[:, :, pl.ds(0, 16)], grad_send.at[3, k])

        @pl.when(section == block)
        def _():
            wait_for(column, grad_send.at[4, k])

        if groups > 1:
            @pl.when(section != diagonal)
            def _():
                wait_for(group_part.at[k, 0, pl.ds(0, groups - 1)], group_send.at[0, k])

            @pl.when(section == helper)
            def _():
                wait_for(group_part.at[k, 1, pl.ds(0, groups - 1)], group_send.at[1, k])
        return 0

    lax.fori_loop(1, stages, drain_grads, 0)
    wait_for(core_part.at[0], grad_send.at[0, 0])
    wait_for(section_part.at[0, 0, pl.ds(0, sections - 1)], grad_send.at[1, 0])
    wait_for(column_part(0, 1), grad_send.at[2, 0])
    if groups > 1:
        wait_for(group_part.at[0, 0, pl.ds(0, groups - 1)], group_send.at[0, 0])
    wait_for(whole.at[0, :, :, 0, pl.ds(0, 16 * (sections - 1))], grad_send.at[3, 0])
    wait_for(whole.at[0, :, :, 0], grad_send.at[4, 0])
    wait_for(flat_core, grad_send.at[0, extra])
    wait_for(flat_section.at[pl.ds(0, sections - 1)], grad_send.at[1, extra])
    wait_for(flat_whole.at[0, 0, pl.ds(0, 48 * (chips - 1)), pl.ds(0, half)], grad_send.at[2, extra])
    wait_for(flat_whole.at[:, 0, pl.ds(0, 48 * (sections - 1))], grad_send.at[3, extra])
    wait_for(flat_whole.at[:, 0], grad_send.at[4, extra])
    if groups > 1:
        wait_for(flat_group.at[0, 0, pl.ds(0, groups - 1)], group_send.at[0, extra])
    first_copy.wait()
    second_copy.wait()
    unite_done.wait()
    camera_done.wait()


def widen(cam, *refs):
    held_in, outs, narrow, full = refs[0:9], refs[9:22], refs[22:31], refs[31:34]
    in_sem, out_sem, plain_sem = refs[34:37]
    loads = [pltpu.make_async_copy(a, b, in_sem.at[n]) for n, (a, b) in enumerate(zip(held_in, narrow))]
    for load in loads:
        load.start()
    passed = []
    channels = full[1].shape[-1]

    def store(number, tap):
        return pltpu.make_async_copy(full[number].at[tap], outs[10 + number].at[tap], out_sem.at[number, tap])

    loads[0].wait()
    loads[1].wait()

    def unite_tap(tap, unused):
        full[0][tap, 0:channels] = narrow[0][tap].astype(f32)
        rows = pl.ds(pl.multiple_of(cam * tap, 16), cam)
        full[0][tap, channels : channels + cam] = narrow[1][rows].astype(f32)
        store(0, tap).start()
        return 0

    lax.fori_loop(0, 9, unite_tap, 0)
    for number in (1, 2):
        loads[number + 1].wait()

        def block_tap(tap, unused):
            full[number][tap] = narrow[number + 1][tap].astype(f32)
            store(number, tap).start()
            return 0

        lax.fori_loop(0, 9, block_tap, 0)
    for number in range(4, 9):
        loads[number].wait()
    for number in range(10):
        source = narrow[4 + number] if number < 4 else narrow[8].at[number - 4]
        passed.append(pltpu.make_async_copy(source, outs[number], plain_sem.at[number]))
        passed[-1].start()
    for number in range(3):
        for tap in range(9):
            store(number, tap).wait()
    for copy in passed:
        copy.wait()


def body(
    lidar, context, depth_logits, cell_index, unite_weight, unite_gain, unite_bias, first_weight, second_weight,
    first_gain, first_bias, second_gain, second_bias, cotangent,
):
    peers = lax.axis_size("dp")
    sections = lax.axis_size("section")
    section = lax.axis_index("section")
    channels = cotangent.shape[-1]
    pixels, bins = depth_logits.shape[2:]
    cam = context.shape[-1]
    united_in = unite_weight.shape[1]
    blocks = sections
    stages = 2 * blocks + 1
    events = 2 * stages - 1
    groups = peers // (2 * chips)
    taken = 9 * channels

    vmem = pl.BlockSpec(memory_space=pltpu.VMEM)
    hbm = pl.BlockSpec(memory_space=pltpu.HBM)
    shape = jax.ShapeDtypeStruct
    dma = pltpu.SemaphoreType.DMA
    results = pl.pallas_call(
        functools.partial(kernel, peers, sections),
        out_shape=(
            shape((cells, channels), f32),
            shape((cells, channels), f32),
            shape((cam, pixels), f32),
            shape((bins, 1, pixels), f32),
            shape((9, 2, 2, 64, channels), bf16),
            shape((2, 2, flat_rows // 4, channels), bf16),
            shape((9, 2, 2, 64, channels), bf16),
            shape((9, 2, 2, 64, channels), bf16),
            shape((6, 1, channels), f32),
        ),
        in_specs=[hbm, vmem, vmem, vmem, hbm, vmem, vmem, hbm, hbm, vmem, vmem, vmem, vmem, hbm],
        out_specs=[vmem, vmem, vmem, vmem, hbm, hbm, hbm, hbm, vmem],
        scratch_shapes=[
            pltpu.VMEM((2 * blocks, taken, channels), bf16),
            pltpu.VMEM((9 * united_in, channels), bf16),
            pltpu.VMEM((blocks, 4, channels), f32),
            pltpu.VMEM((cells + 2 * side, 3 * wide), bf16),
            pltpu.VMEM((chips, cells + 2 * side, 3 * channels), bf16),
            pltpu.VMEM((chips, cells, channels), bf16),
            pltpu.VMEM((2 * blocks, chips, cells, channels), bf16),
            pltpu.VMEM((stages, chips, cells, channels), f32),
            pltpu.VMEM((stages + 1, 1, channels), f32),
            pltpu.VMEM((chips, cells, channels), f32),
            pltpu.VMEM((chips, cells, channels), bf16),
            pltpu.VMEM((chips, cells, channels), bf16),
            pltpu.VMEM((chips, cells, channels), bf16),
            pltpu.VMEM((chips, cells, half), bf16),
            pltpu.VMEM((events, 2, channels), f32),
            pltpu.VMEM((events, 2 * groups, 2, channels), f32),
            pltpu.VMEM((2, channels), f32),
            pltpu.VMEM((peers, 2, channels), f32),
            pltpu.VMEM((half, pixels), f32),
            pltpu.VMEM((half, pixels), f32),
            pltpu.VMEM((cells, pixels), bf16),
            pltpu.VMEM((stages, 9, 2, 64, half), bf16),
            pltpu.VMEM((stages, 9, 64, half), bf16),
            pltpu.VMEM((stages, 9, 64, half), bf16),
            pltpu.VMEM((stages, 2, sections, 9, 16, half), bf16),
            pltpu.VMEM((stages, 9, 2, 2, 64, channels), bf16),
            pltpu.VMEM((flat_rows, half), bf16),
            pltpu.VMEM((flat_rows // 4, half), bf16),
            pltpu.VMEM((flat_rows // 4, half), bf16),
            pltpu.VMEM((sections, 48, half), bf16),
            pltpu.VMEM((2, 2, flat_rows // 4, channels), bf16),
            pltpu.VMEM((sections, stages, 2, channels), f32),
            pltpu.VMEM((stages if groups > 1 else 1, 2, groups, 9, 16, half), bf16),
            pltpu.VMEM((1, 1, groups, 48, half), bf16),
            dma((9,)), dma, dma, dma((events,)), dma((events,)), dma((chips,)), dma((chips,)), dma((chips,)),
            dma((chips,)), dma((chips,)), dma((chips,)), dma((chips,)), dma((chips,)), dma((4,)),
            dma((2 * blocks,)), dma((2,)), dma((2 * blocks,)), dma((2 * blocks,)), dma, dma,
            dma((5, stages + 1)), dma((5, stages + 1)), dma, dma, dma((2, stages + 1)), dma((2, stages + 1)),
        ],
        compiler_params=pltpu.CompilerParams(
            collective_id=0, has_side_effects=True, vmem_limit_bytes=60 << 20
        ),
    )(
        lidar.reshape(cells, channels), context.reshape(pixels, cam).T, depth_logits.reshape(pixels, bins).T,
        jnp.transpose(cell_index, (0, 3, 1, 2)).reshape(bins, 1, pixels), unite_weight.reshape(-1, channels),
        unite_gain[None], unite_bias[None], first_weight.reshape(taken, channels),
        second_weight.reshape(taken, channels), first_gain, first_bias, second_gain, second_bias,
        cotangent.reshape(-1, cells, channels),
    )

    act, lidar_grad, context_grad, logit_grad, *small, unite_whole, first_whole, second_whole = pl.pallas_call(
        functools.partial(widen, cam),
        out_shape=(
            shape((cells, channels), f32),
            shape((cells, channels), f32),
            shape((cam, pixels), f32),
            shape((bins, 1, pixels), f32),
            *[shape((1, channels), f32)] * 6,
            shape((9, united_in, channels), f32),
            shape((9, channels, channels), f32),
            shape((9, channels, channels), f32),
        ),
        in_specs=[hbm] * 9,
        out_specs=[hbm] * 13,
        scratch_shapes=[
            pltpu.VMEM((9, channels, channels), bf16),
            pltpu.VMEM((flat_rows, channels), bf16),
            pltpu.VMEM((9, channels, channels), bf16),
            pltpu.VMEM((9, channels, channels), bf16),
            pltpu.VMEM((cells, channels), f32),
            pltpu.VMEM((cells, channels), f32),
            pltpu.VMEM((cam, pixels), f32),
            pltpu.VMEM((bins, 1, pixels), f32),
            pltpu.VMEM((6, 1, channels), f32),
            pltpu.VMEM((9, united_in, channels), f32),
            pltpu.VMEM((9, channels, channels), f32),
            pltpu.VMEM((9, channels, channels), f32),
            dma((9,)), dma((3, 9)), dma((10,)),
        ],
        compiler_params=pltpu.CompilerParams(vmem_limit_bytes=60 << 20),
    )(
        results[4].reshape(9, channels, channels), results[5].reshape(flat_rows, channels),
        results[6].reshape(9, channels, channels), results[7].reshape(9, channels, channels), *results[0:4], results[8],
    )
    return (
        act.reshape(lidar.shape),
        lidar_grad.reshape(lidar.shape),
        context_grad.T.reshape(context.shape),
        jnp.transpose(logit_grad.reshape(1, bins, 1, pixels), (0, 2, 3, 1)),
        unite_whole,
        small[0].reshape(channels),
        small[1].reshape(channels),
        first_whole.reshape(first_weight.shape),
        second_whole.reshape(second_weight.shape),
        *small[2:6],
    )


def solution(mesh):
    split, by_dp = P("section"), P("section", "dp")
    in_specs = (by_dp, by_dp, by_dp, by_dp, P(), P(), P(), split, split, split, split, split, split, P(None, "dp"))
    out_specs = (by_dp, by_dp, by_dp, by_dp, P(), P(), P(), split, split, split, split, split, split)
    return jax.shard_map(body, mesh=mesh, in_specs=in_specs, out_specs=out_specs, check_vma=False)
```

```python
import functools

import jax
import jax.numpy as jnp
from jax import lax
from jax.experimental import pallas as pl
from jax.experimental.pallas import tpu as pltpu
from jax.sharding import PartitionSpec as P

eps = 1e-05
f32, bf16 = jnp.float32, jnp.bfloat16
MESH = pl.DeviceIdType.MESH
side = 16
cells = side * side
wide = 384
chips = 4
half = 128
column_lag = 4
owner_lag = 8
flat_rows = 768
transposed_rhs = (((1,), (1,)), ((), ()))
transposed_lhs = (((0,), (0,)), ((), ()))


def sigmoid(value):
    return 0.5 * jnp.tanh(0.5 * value) + 0.5


def slope(value):
    gate = sigmoid(value)
    return gate * (1.0 + value * (1.0 - gate))


def silu(value):
    return value * sigmoid(value)


def put_shifted(buffer, value, stride, offset=0):
    column = lax.broadcasted_iota(jnp.int32, (cells, 1), 0) % side
    width = value.shape[1]
    before = jnp.where(column == 0, 0.0, pltpu.roll(value, 1, 0))
    after = jnp.where(column == side - 1, 0.0, pltpu.roll(value, cells - 1, 0))
    for group, shifted in enumerate((before, value, after)):
        start = group * stride + offset
        buffer[side : side + cells, start : start + width] = shifted.astype(bf16)


def total_of(terms):
    total = None
    for term in terms:
        total = term if total is None else total + term
    return total


def conv(buffer, weight):
    return total_of(
        jnp.dot(buffer[side * i : side * i + cells, :], weight(i), preferred_element_type=f32) for i in range(3)
    )


def conv_transposed(buffer, weight, width):
    return total_of(
        lax.dot_general(
            buffer[side * (2 - i) : side * (2 - i) + cells, width * (2 - j) : width * (3 - j)],
            weight(3 * i + j),
            transposed_rhs,
            preferred_element_type=f32,
        )
        for i in range(3)
        for j in range(3)
    )


plan = {
    "start": [("offer", 0, "near", 0), ("offer", 0, "far", 3), ("offer", 0, "near", 2), ("offer", 0, "near", 1)],
    "lift2": [("offer", 0, "near", 3), ("offer", 1, "near", 0)],
    "united": [("relay", 0, 0), ("offer", 1, "near", 1), ("offer", 1, "near", 3)],
    "united2": [("offer", 1, "far", 0), ("offer", 1, "near", 2), ("offer", 0, "far", 1)],
    "merged": [("offer", 0, "far", 0), ("relay", 1, 0)],
    "entered1": [("relay", 3, 0), ("relay", 0, 1), ("relay", 2, 0)],
    "entered3": [("offer", 0, "far", 2), ("offer", 1, "far", 1)],
    "entered2": [("relay", 2, 1)],
    "entered": [("offer", 1, "far", 2), ("arrive", 0, 0)],
    ("first", 0): [("relay", 1, 1), ("arrive", 1, 0), ("offer", 1, "far", 3), ("arrive", 0, 1)],
    ("second", 0): [("relay", 3, 1)],
    ("first", 1): [("arrive", 1, 1), ("arrive", 2, 0)],
    ("second", 1): [("arrive", 3, 0), ("arrive", 2, 1)],
    ("second", 2): [("arrive", 3, 1)],
}


def kernel(
    peers, sections,
    lidar_ref, context_ref, logit_ref, cell_ref, unite_ref, unite_gain, unite_bias, first_ref, second_ref,
    first_gain, first_bias, second_gain, second_bias, cotangent_ref,
    act_ref, lidar_grad, context_grad, logit_grad, unite_out, camera_out, first_out, second_out, small_out,
    weights, unite_weight, vectors, joined, shifted, current, kept, normed, scales, held, gathered, upstream,
    lidars, cameras, mine, slots, unite_mine, unite_slots, probability, places, histogram,
    partial, core_part, own_part, section_part, whole, flat, flat_core, flat_own, flat_section, flat_whole,
    totals, gains, group_part, flat_group,
    local_sem, unite_send, unite_recv, stat_send, stat_recv, raw_send, raw_recv, cot_send, cot_recv,
    lidar_send, lidar_recv, camera_send, camera_recv, weight_send, weight_recv, relay_send, pass_send, pass_recv,
    vector_send, vector_recv, grad_send, grad_recv, total_send, total_recv, group_send, group_recv,
):
    me = lax.axis_index("dp")
    section = lax.axis_index("section")
    core = lax.rem(me, 2)
    chip = lax.rem(lax.div(me, 2), chips)
    group = lax.div(me, 2 * chips)
    groups = peers // (2 * chips)
    blocks = sections
    stages = 2 * blocks + 1
    channels = vectors.shape[-1]
    bins = logit_ref.shape[0]
    cam = context_ref.shape[0]
    united_in = channels + cam
    taken = 9 * channels
    row_half = lax.div(chip, 2)
    lane_half = lax.rem(chip, 2)
    count = float(peers * cells)

    def at(other_section=None, other=None):
        return (section if other_section is None else other_section, me if other is None else other)

    def chip_peer(step):
        return group * (2 * chips) + lax.rem(chip + step, chips) * 2 + core

    sibling = me + 1 - 2 * core

    def remote(source, target, send, recv, device):
        return pltpu.make_async_remote_copy(
            src_ref=source, dst_ref=target, send_sem=send, recv_sem=recv, device_id=device, device_id_type=MESH
        )

    def wait_for(part, semaphore):
        pltpu.make_async_copy(part, part, semaphore).wait()

    barrier = pltpu.get_barrier_semaphore()
    for step in range(1, sections):
        pl.semaphore_signal(
            barrier, inc=1, device_id=at(other_section=lax.rem(section + step, sections)), device_id_type=MESH
        )

    def greet(step, unused):
        pl.semaphore_signal(barrier, inc=1, device_id=at(other=lax.rem(me + step, peers)), device_id_type=MESH)
        return 0

    lax.fori_loop(1, peers, greet, 0)

    unite_copy = pltpu.make_async_copy(unite_ref, unite_weight, local_sem.at[0])
    own_first = pltpu.make_async_copy(first_ref, weights.at[2 * section], local_sem.at[1])
    own_second = pltpu.make_async_copy(second_ref, weights.at[2 * section + 1], local_sem.at[2])
    own_cot = pltpu.make_async_copy(cotangent_ref.at[section], upstream.at[chip], local_sem.at[3])
    own_lidar = pltpu.make_async_copy(lidar_ref, lidars.at[chip], local_sem.at[4])
    own_lidar.start()
    unite_copy.start()
    own_first.start()
    own_second.start()
    own_cot.start()
    for number, part in enumerate((first_gain, first_bias, second_gain, second_bias)):
        vectors[section, number : number + 1] = part[...]
    joined[...] = jnp.zeros_like(joined)
    probability[...] = jnp.zeros_like(probability)
    places[...] = jnp.zeros_like(places)
    cameras[chip] = jnp.zeros((cells, half), bf16)
    pl.semaphore_wait(barrier, peers - 1 + sections - 1)

    beside = section + 1 - 2 * lax.rem(section, 2)
    across = lax.rem(section + 2, sections)
    near = beside + core * (across - beside)
    far = across + core * (beside - across)
    part_rows = taken // 2
    part = pl.ds(pl.multiple_of(core * part_rows, part_rows), part_rows)
    sources = (first_ref, second_ref)

    def offer(which, target, number):
        index = 2 * section + which
        remote(
            sources[which].at[part], weights.at[index, part], weight_send.at[number], weight_recv.at[index],
            at(other_section=target),
        ).start()

    def arrived(index):
        wait_for(weights.at[index, part], weight_recv.at[index])

    def pass_on(index):
        remote(
            weights.at[index, part], weights.at[index, part], pass_send.at[index], pass_recv.at[index],
            at(other=sibling),
        ).start()

    def relay(block, which):
        index = 2 * block + which

        @pl.when(near == block)
        def _():
            arrived(index)
            remote(
                weights.at[index, part], weights.at[index, part], relay_send.at[which], weight_recv.at[index],
                at(other_section=far),
            ).start()
            pass_on(index)

    def arrive(block, which):
        index = 2 * block + which

        @pl.when((section != block) & (near != block))
        def _():
            arrived(index)
            pass_on(index)

    def ready(block, which):
        index = 2 * block + which
        rest = pl.ds(pl.multiple_of((1 - core) * part_rows, part_rows), part_rows)

        @pl.when(section != block)
        def _():
            wait_for(weights.at[index, rest], pass_recv.at[index])

        @pl.when(section == block)
        def _():
            (own_second if which else own_first).wait()

    def act_on(entry):
        name, one, two = entry[0:3]
        if name == "relay":
            relay(one, two)
        elif name == "arrive":
            arrive(one, two)
        else:
            @pl.when(section == entry[3])
            def _():
                offer(one, near if two == "near" else far, 2 * one + (two == "far"))

    def point(name, block=None):
        for key, entries in plan.items():
            if isinstance(key, tuple) and key[0] == name:
                @pl.when(block == key[1])
                def _():
                    for entry in entries:
                        act_on(entry)
            elif key == name:
                for entry in entries:
                    act_on(entry)

    point("start")
    for step in range(1, sections):
        remote(
            vectors.at[section], vectors.at[section], vector_send, vector_recv,
            at(other_section=lax.rem(section + step, sections)),
        ).start()

    logits = logit_ref[...].astype(f32)
    raised = jnp.exp(logits - jnp.max(logits, axis=0, keepdims=True))
    probability[0:bins] = raised / jnp.sum(raised, axis=0, keepdims=True)
    address = lax.broadcasted_iota(jnp.int32, (cells, half), 0)

    def add_bin(number, total):
        place = cell_ref[number]
        places[pl.ds(number, 1)] = place.astype(f32)
        return total + jnp.where(place == address, probability[pl.ds(number, 1)], 0.0)

    counted = jnp.zeros((cells, half), f32)
    for number in range(3):
        counted = lax.fori_loop(bins * number // 3, bins * (number + 1) // 3, add_bin, counted)
        if number < 2:
            point(f"lift{number + 1}")
    counted = counted.astype(bf16)
    histogram[...] = counted
    pooled = lax.dot_general(counted, context_ref[...], transposed_rhs, preferred_element_type=f32)
    cameras[chip, :, 0:cam] = pooled.astype(bf16)

    own_lidar.wait()
    put_shifted(joined, lidars[chip].astype(f32), wide)
    put_shifted(joined, pooled, wide, channels)
    unite_copy.wait()
    united = total_of(
        jnp.dot(
            joined[side * i : side * i + cells, wide * j : wide * j + united_in],
            unite_weight[united_in * (3 * i + j) : united_in * (3 * i + j + 1), :],
            preferred_element_type=f32,
        )
        for i in range(3)
        for j in range(3)
    )
    gathered[chip] = united.astype(bf16)
    for step in range(1, chips):
        remote(
            gathered.at[chip], gathered.at[chip], raw_send.at[step], raw_recv.at[step], at(other=chip_peer(step))
        ).start()
    center = jnp.sum(united, axis=0, keepdims=True) * (1.0 / cells)
    offsets = united - center
    unite_mine[0:1] = center
    unite_mine[1:2] = jnp.sum(offsets * offsets, axis=0, keepdims=True)
    unite_slots[me] = unite_mine[...]

    def send_unite(step, unused):
        remote(
            unite_mine, unite_slots.at[me], unite_send, unite_recv, at(other=lax.rem(me + step, peers))
        ).start()
        return 0

    lax.fori_loop(1, peers, send_unite, 0)

    point("united")
    shifted[...] = jnp.zeros_like(shifted)
    flat[9 * cam :, :] = jnp.zeros((flat_rows - 9 * cam, half), bf16)

    def merged(centers, squares, each):
        parts = centers.shape[0]
        center = jnp.sum(centers, axis=0, keepdims=True) * (1.0 / parts)
        apart = centers - center
        square = jnp.sum(squares, axis=0, keepdims=True) + each * jnp.sum(apart * apart, axis=0, keepdims=True)
        return center, square

    point("united2")
    wait_for(unite_slots.at[pl.ds(0, peers - 1)], unite_recv)
    center, square = merged(unite_slots[:, 0, :], unite_slots[:, 1, :], cells)
    scales[0] = lax.rsqrt(square * (1.0 / count) + eps)
    scales[stages] = center
    point("merged")

    def enter(number):
        value = (gathered[number].astype(f32) - scales[stages]) * scales[0]
        normed[0, number] = value
        entering = silu(unite_gain[...] * value + unite_bias[...])
        current[number] = entering.astype(bf16)
        kept[0, number] = entering.astype(bf16)
        put_shifted(shifted.at[number], entering, channels)

    enter(chip)
    for step in (1, 3, 2):
        wait_for(gathered.at[0], raw_recv.at[step])
        enter(lax.rem(chip - step + chips, chips))
        point(f"entered{step}")

    own_cot.wait()
    for step in range(1, chips):
        peer = at(other=chip_peer(step))
        remote(upstream.at[chip], upstream.at[chip], cot_send.at[step], cot_recv.at[step], peer).start()
    for step in range(1, chips):
        peer = at(other=chip_peer(step))
        remote(lidars.at[chip], lidars.at[chip], lidar_send.at[step], lidar_recv.at[step], peer).start()
        remote(cameras.at[chip], cameras.at[chip], camera_send.at[step], camera_recv.at[step], peer).start()

    point("entered")
    wait_for(vectors.at[pl.ds(0, sections - 1)], vector_recv)

    members = 2 * groups
    place = group * 2 + core

    def copy_stats(event, step):
        to = lax.rem(place + step, members)
        return remote(
            mine.at[event], slots.at[event, place], stat_send.at[event], stat_recv.at[event],
            at(other=lax.div(to, 2) * (2 * chips) + chip * 2 + lax.rem(to, 2)),
        )

    def send_stats(event, first, second):
        mine[event, 0:1] = first
        mine[event, 1:2] = second
        slots[event, place] = mine[event]
        for step in range(1, members):
            copy_stats(event, step).start()

    def take_stats(event):
        wait_for(slots.at[event, pl.ds(0, members - 1)], stat_recv.at[event])
        return slots[event, :, 0, :], slots[event, :, 1, :]

    def local_sums(parts):
        centers, squares = zip(*parts)
        return merged(jnp.concatenate(centers, axis=0), jnp.concatenate(squares, axis=0), cells)

    def start_conv(number, index):
        activ = conv(shifted.at[number], lambda i: weights[index, 3 * channels * i : 3 * channels * (i + 1), :])
        held[number] = activ
        center = jnp.sum(activ, axis=0, keepdims=True) * (1.0 / cells)
        offsets = activ - center
        return center, jnp.sum(offsets * offsets, axis=0, keepdims=True)

    def whole_sums(stage):
        centers, squares = take_stats(stage - 1)
        center, square = merged(centers, squares, chips * cells)
        scale = lax.rsqrt(square * (1.0 / count) + eps)
        scales[stage] = scale
        return center, scale

    def block(s, last):
        stage = 2 * s + 1

        def vector(number):
            return vectors[s, number : number + 1]

        point("first", s)
        ready(s, 1)
        center, scale = whole_sums(stage)
        parts = []
        for number in range(chips):
            value = (held[number] - center) * scale
            normed[stage, number] = value
            hidden = silu(vector(0) * value + vector(1))
            kept[stage, number] = hidden.astype(bf16)
            put_shifted(shifted.at[number], hidden, channels)
            parts.append(start_conv(number, 2 * s + 1))
        send_stats(stage, *local_sums(parts))
        point("second", s)
        if not last:
            ready(s + 1, 0)
        center, scale = whole_sums(stage + 1)
        parts = []
        for number in range(chips):
            value = (held[number] - center) * scale
            normed[stage + 1, number] = value
            output = current[number].astype(f32) + silu(vector(2) * value + vector(3))
            if last:
                held[number] = output
            else:
                current[number] = output.astype(bf16)
                kept[stage + 1, number] = output.astype(bf16)
                put_shifted(shifted.at[number], output, channels)
                parts.append(start_conv(number, 2 * s + 2))
        if not last:
            send_stats(stage + 1, *local_sums(parts))

    def block_step(s, unused):
        block(s, False)
        return 0

    ready(0, 0)
    send_stats(0, *local_sums([start_conv(number, 0) for number in range(chips)]))
    lax.fori_loop(0, blocks - 1, block_step, 0)
    block(blocks - 1, True)
    act_ref[...] = held[chip]

    lanes = pl.ds(pl.multiple_of(lane_half * half, half), half)
    flat48 = pl.ds(pl.multiple_of(section * 48, 16), 48)

    def lateral(j):
        return pl.ds(pl.multiple_of(channels * (2 - j) + lane_half * half, half), half)

    def weight_grad(stage, inputs):
        columns = pl.ds(pl.multiple_of(row_half * half, half), half)
        values = [inputs[number, :, columns] for number in range(chips)]
        for i in range(3):
            for j in range(3):
                taps = total_of(
                    lax.dot_general(
                        values[number],
                        shifted[number, side * (2 - i) : side * (2 - i) + cells, lateral(j)],
                        transposed_lhs,
                        preferred_element_type=f32,
                    )
                    for number in range(chips)
                ).astype(bf16)
                partial[stage, 3 * i + j, 0] = taps[0:64]
                partial[stage, 3 * i + j, 1] = taps[64:128]
        to_sibling(stage)

    def to_sibling(k):
        remote(
            partial.at[k, :, 1 - core], core_part.at[k], grad_send.at[0, k], grad_recv.at[0, k], at(other=sibling)
        ).start()

    def block_of(k):
        return lax.div(k - 1, 2)

    def roles(k):
        block = block_of(k)
        across_x = block + 1 - 2 * lax.rem(block, 2)
        across_y = lax.rem(block + 2, sections)
        return block, sections - 1 - block, across_x + core * (across_y - across_x)

    def tile(index):
        return pl.ds(pl.multiple_of(index * 16, 16), 16)

    def sum_cores(k):
        wait_for(core_part.at[k], grad_recv.at[0, k])
        for tap in range(9):
            own_part[k, tap] = (partial[k, tap, core].astype(f32) + core_part[k, tap].astype(f32)).astype(bf16)

    def send_tile(k, index, slot, other):
        remote(
            own_part.at[k, :, tile(index)], section_part.at[k, slot, section], grad_send.at[1, k], grad_recv.at[1, k],
            at(other_section=other),
        ).start()

    def to_sections(k):
        sum_cores(k)
        block, diagonal, helper = roles(k)
        for step in range(1, sections):
            other = lax.rem(section + step, sections)

            @pl.when(other != diagonal)
            def _():
                send_tile(k, other, 0, other)

            @pl.when(other == helper)
            def _():
                send_tile(k, diagonal, 1, other)

        section_part[k, 0, section] = own_part[k, :, tile(section)]

        @pl.when(section == helper)
        def _():
            section_part[k, 1, section] = own_part[k, :, tile(diagonal)]

    def over_groups(slot, k, value, buffer, number):
        if groups == 1:
            return value
        mine_here = buffer.at[k, slot, group]
        mine_here[...] = value
        for step in range(1, groups):
            to = lax.rem(group + step, groups) * (2 * chips) + chip * 2 + core
            remote(
                mine_here, mine_here, group_send.at[slot, number], group_recv.at[slot, number], at(other=to)
            ).start()
        wait_for(buffer.at[k, slot, pl.ds(0, groups - 1)], group_recv.at[slot, number])
        return jnp.sum(buffer[k, slot].astype(f32), axis=0).astype(bf16)

    def reduce_tile(k, slot, index):
        piece = total_of(section_part[k, slot, number].astype(f32) for number in range(sections)).astype(bf16)
        place = whole.at[k, :, row_half, core, tile(index), lanes]
        place[...] = over_groups(slot, k, piece, group_part, k)
        for step in range(1, chips):
            remote(place, place, grad_send.at[2, k], grad_recv.at[2, k], at(other=chip_peer(step))).start()

    def to_column(k):
        block, diagonal, helper = roles(k)

        @pl.when(section == helper)
        def _():
            wait_for(section_part.at[k, :, pl.ds(0, sections - 1)], grad_recv.at[1, k])
            reduce_tile(k, 0, section)
            reduce_tile(k, 1, diagonal)

        @pl.when((section != helper) & (section != diagonal))
        def _():
            wait_for(section_part.at[k, 0, pl.ds(0, sections - 1)], grad_recv.at[1, k])
            reduce_tile(k, 0, section)

    def column_part(k, tiles):
        return whole.at[k, :, 0, 0, pl.ds(0, 16 * (chips - 1)), pl.ds(0, half * tiles)]

    def hand_over(k, index, block):
        place = whole.at[k, :, :, core, tile(index)]
        remote(place, place, grad_send.at[3, k], grad_recv.at[3, k], at(other_section=block)).start()

    def to_owner(k):
        block, diagonal, helper = roles(k)

        @pl.when(section == helper)
        def _():
            wait_for(column_part(k, 2), grad_recv.at[2, k])
            hand_over(k, section, block)
            hand_over(k, diagonal, block)

        @pl.when((section != helper) & (section != diagonal))
        def _():
            wait_for(column_part(k, 1), grad_recv.at[2, k])

            @pl.when(section != block)
            def _():
                hand_over(k, section, block)

    def to_sections_all(k):
        sum_cores(k)
        section_part[k, 0, section] = own_part[k, :, tile(section)]
        for step in range(1, sections):
            other = lax.rem(section + step, sections)
            send_tile(k, other, 0, other)

    def to_column_all(k):
        wait_for(section_part.at[k, 0, pl.ds(0, sections - 1)], grad_recv.at[1, k])
        reduce_tile(k, 0, section)

    def to_all(k):
        wait_for(column_part(k, 1), grad_recv.at[2, k])
        place = whole.at[k, :, :, core, tile(section)]
        for step in range(1, sections):
            other = lax.rem(section + step, sections)
            remote(place, place, grad_send.at[3, k], grad_recv.at[3, k], at(other_section=other)).start()

    def share(k):
        wait_for(whole.at[k, :, :, 0, pl.ds(0, 16 * (sections - 1))], grad_recv.at[3, k])
        place = whole.at[k, :, :, core]
        remote(place, place, grad_send.at[4, k], grad_recv.at[4, k], at(other=sibling)).start()

    def owner_share(k):
        @pl.when(section == block_of(k))
        def _():
            share(k)

    def shared(k):
        wait_for(whole.at[k, :, :, 0], grad_recv.at[4, k])

    def backwards(first, last, act):
        def step(number, unused):
            act(first - number)
            return 0

        lax.fori_loop(0, first - last + 1, step, 0)

    def when_due(k, act):
        @pl.when(k <= stages - 1)
        def _():
            act(k)

    def start_norm(stage, number, grads, gain, bias):
        value = normed[stage, number]
        grads = grads * slope(gain * value + bias)
        held[number] = grads
        return jnp.sum(grads, axis=0, keepdims=True), jnp.sum(grads * value, axis=0, keepdims=True)

    def send_sums(stage, parts):
        firsts, seconds = zip(*parts)
        send_stats(stages - 1 + stage, total_of(firsts), total_of(seconds))

    def norm_factors(stage, gain):
        first, second = take_stats(stages - 1 + stage)
        first = jnp.sum(first, axis=0, keepdims=True)
        second = jnp.sum(second, axis=0, keepdims=True)
        totals[section, stage, 0:1] = first
        totals[section, stage, 1:2] = second
        return gain * scales[stage], first * (1.0 / count), second * (1.0 / count)

    def end_norm(stage, number, factors):
        factor, first, second = factors
        put_shifted(
            shifted.at[number], factor * (held[number] - first - normed[stage, number] * second), channels
        )

    def passed(number, index):
        return conv_transposed(
            shifted.at[number], lambda tap: weights[index, channels * tap : channels * (tap + 1), :], channels
        )

    def during(stage):
        weight_grad(stage + 1, kept.at[stage])
        when_due(stage + 2, to_sections)
        when_due(stage + column_lag, to_column)
        when_due(stage + owner_lag, to_owner)

    for step in range(1, chips):
        wait_for(upstream.at[0], cot_recv.at[step])
        wait_for(upstream.at[0], cot_send.at[step])
    def take_gains(s):
        @pl.when(s > 0)
        def _():
            gains[0:1] = vectors[jnp.maximum(s - 1, 0), 2:3]
            gains[1:2] = vectors[jnp.maximum(s - 1, 0), 3:4]

        @pl.when(s == 0)
        def _():
            gains[0:1] = unite_gain[...]
            gains[1:2] = unite_bias[...]

    take_gains(blocks)
    send_sums(
        stages - 1,
        [
            start_norm(stages - 1, number, upstream[number].astype(f32), gains[0:1], gains[1:2])
            for number in range(chips)
        ],
    )

    def block_back(back, unused):
        s = blocks - 1 - back
        stage = 2 * s + 1

        def vector(number):
            return vectors[s, number : number + 1]

        @pl.when(back > 0)
        def _():
            during(stage + 1)

        factors = norm_factors(stage + 1, vector(2))
        parts = []
        for number in range(chips):
            end_norm(stage + 1, number, factors)
            parts.append(start_norm(stage, number, passed(number, 2 * s + 1), vector(0), vector(1)))
        send_sums(stage, parts)
        during(stage)
        take_gains(s)
        factors = norm_factors(stage, vector(0))
        parts = []
        for number in range(chips):
            end_norm(stage, number, factors)
            grads = (upstream[number].astype(f32) + passed(number, 2 * s)).astype(bf16)
            upstream[number] = grads
            parts.append(start_norm(stage - 1, number, grads.astype(f32), gains[0:1], gains[1:2]))
        send_sums(stage - 1, parts)
        return 0

    lax.fori_loop(0, blocks, block_back, 0)

    during(0)
    for step in range(1, chips):
        wait_for(lidars.at[0], lidar_recv.at[step])
        wait_for(cameras.at[0], camera_recv.at[step])
    factors = norm_factors(0, gains[0:1])
    for number in range(chips):
        end_norm(0, number, factors)
    weight_grad(0, lidars)
    to_sections(1)
    held_cameras = [cameras[number] for number in range(chips)]
    for i in range(3):
        for j in range(3):
            taps = total_of(
                lax.dot_general(
                    held_cameras[number],
                    shifted[number, side * (2 - i) : side * (2 - i) + cells, lateral(j)],
                    transposed_lhs,
                    preferred_element_type=f32,
                )
                for number in range(chips)
            ).astype(bf16)
            flat[cam * (3 * i + j) : cam * (3 * i + j + 1)] = taps[0:cam]
    quarter = flat_rows // 4
    kept_rows = pl.ds(pl.multiple_of(row_half * (2 * quarter) + core * quarter, 16), quarter)
    sent_rows = pl.ds(pl.multiple_of(row_half * (2 * quarter) + (1 - core) * quarter, 16), quarter)
    extra = stages
    remote(
        flat.at[sent_rows], flat_core, grad_send.at[0, extra], grad_recv.at[0, extra], at(other=sibling)
    ).start()
    to_sections_all(0)
    backwards(min(column_lag - 1, stages - 1), 2, to_column)
    for step in range(1, sections):
        remote(
            totals.at[section], totals.at[section], total_send, total_recv,
            at(other_section=lax.rem(section + step, sections)),
        ).start()
    own = shifted.at[chip]
    pooled_grad = conv_transposed(
        own, lambda tap: unite_weight[united_in * tap + channels : united_in * (tap + 1), :], channels
    ).astype(bf16)

    wait_for(flat_core, grad_recv.at[0, extra])
    flat_own[...] = (flat[kept_rows].astype(f32) + flat_core[...].astype(f32)).astype(bf16)
    flat_section[section] = flat_own[flat48]
    for step in range(1, sections):
        other = lax.rem(section + step, sections)
        remote(
            flat_own.at[pl.ds(pl.multiple_of(other * 48, 16), 48)], flat_section.at[section],
            grad_send.at[1, extra], grad_recv.at[1, extra], at(other_section=other),
        ).start()
    lidar_grad[...] = conv_transposed(
        own, lambda tap: unite_weight[united_in * tap : united_in * tap + channels, :], channels
    )
    to_column(1)

    context_grad[...] = lax.dot_general(pooled_grad, histogram[...], transposed_lhs, preferred_element_type=f32)
    table = lax.dot_general(
        context_ref[...], pooled_grad, (((0,), (1,)), ((), ())), preferred_element_type=f32
    )
    wanted = places[...].T.astype(jnp.int32)
    within = lax.rem(wanted, half)
    low = jnp.take_along_axis(table[:, 0:half], within, axis=1)
    high = jnp.take_along_axis(table[:, half : 2 * half], within, axis=1)
    chance_grad = jnp.where(wanted < half, low, high).T
    chance = probability[...]
    places[...] = chance * (chance_grad - jnp.sum(chance_grad * chance, axis=0, keepdims=True))

    def store_bin(number, unused):
        logit_grad[number] = places[pl.ds(number, 1)]
        return 0

    lax.fori_loop(0, bins, store_bin, 0)

    to_column_all(0)
    wait_for(flat_section.at[pl.ds(0, sections - 1)], grad_recv.at[1, extra])
    piece = total_of(flat_section[number].astype(f32) for number in range(sections)).astype(bf16)
    flat_place = flat_whole.at[row_half, core, flat48, lanes]
    flat_place[...] = over_groups(0, 0, piece, flat_group, extra)
    for step in range(1, chips):
        remote(
            flat_place, flat_place, grad_send.at[2, extra], grad_recv.at[2, extra], at(other=chip_peer(step))
        ).start()
    backwards(min(owner_lag - 1, stages - 1), 1, to_owner)
    to_all(0)
    wait_for(flat_whole.at[0, 0, pl.ds(0, 48 * (chips - 1)), pl.ds(0, half)], grad_recv.at[2, extra])
    flat_rows_place = flat_whole.at[:, core, flat48]
    for step in range(1, sections):
        other = lax.rem(section + step, sections)
        remote(
            flat_rows_place, flat_rows_place, grad_send.at[3, extra], grad_recv.at[3, extra],
            at(other_section=other),
        ).start()

    backwards(stages - 1, 1, owner_share)
    share(0)
    wait_for(flat_whole.at[:, 0, pl.ds(0, 48 * (sections - 1))], grad_recv.at[3, extra])
    flat_half = flat_whole.at[:, core]
    remote(flat_half, flat_half, grad_send.at[4, extra], grad_recv.at[4, extra], at(other=sibling)).start()

    wait_for(totals.at[pl.ds(0, sections - 1)], total_recv)
    def summed(stage, row):
        return total_of(totals[number, stage, row : row + 1] for number in range(sections))

    small_out[0] = summed(0, 1)
    small_out[1] = summed(0, 0)
    for number in range(2):
        small_out[2 + 2 * number] = summed(2 * section + 1 + number, 1)
        small_out[3 + 2 * number] = summed(2 * section + 1 + number, 0)
    shared(2 * section + 1)
    shared(2 * section + 2)
    first_copy = pltpu.make_async_copy(whole.at[2 * section + 1], first_out, local_sem.at[5])
    second_copy = pltpu.make_async_copy(whole.at[2 * section + 2], second_out, local_sem.at[6])
    first_copy.start()
    second_copy.start()
    shared(0)
    unite_done = pltpu.make_async_copy(whole.at[0], unite_out, local_sem.at[7])
    unite_done.start()
    wait_for(flat_whole.at[:, 0], grad_recv.at[4, extra])
    camera_done = pltpu.make_async_copy(flat_whole, camera_out, local_sem.at[8])
    camera_done.start()

    wait_for(unite_slots.at[pl.ds(0, peers - 1)], unite_send)
    for step in range(1, chips):
        wait_for(gathered.at[0], raw_send.at[step])
        wait_for(lidars.at[0], lidar_send.at[step])
        wait_for(cameras.at[0], camera_send.at[step])
    for number in range(4):
        wait_for(weights.at[0, part], weight_send.at[number])
    for number in range(2):
        wait_for(weights.at[0, part], relay_send.at[number])
    wait_for(vectors.at[pl.ds(0, sections - 1)], vector_send)
    wait_for(totals.at[pl.ds(0, sections - 1)], total_send)

    def drain_stats(event, unused):
        wait_for(slots.at[event, pl.ds(0, members - 1)], stat_send.at[event])
        return 0

    lax.fori_loop(0, 2 * stages - 1, drain_stats, 0)

    def drain_weights(index, unused):
        @pl.when(section != lax.div(index, 2))
        def _():
            wait_for(weights.at[index, part], pass_send.at[index])
        return 0

    lax.fori_loop(0, 2 * blocks, drain_weights, 0)

    def drain_grads(k, unused):
        block, diagonal, helper = roles(k)
        own_tiles = section_part.at[k, 0]
        column = whole.at[k, :, :, 0]
        wait_for(core_part.at[k], grad_send.at[0, k])

        @pl.when(section == diagonal)
        def _():
            wait_for(own_tiles.at[pl.ds(0, 4)], grad_send.at[1, k])

        @pl.when(section == helper)
        def _():
            wait_for(own_tiles.at[pl.ds(0, 2)], grad_send.at[1, k])
            wait_for(column_part(k, 2), grad_send.at[2, k])
            wait_for(column.at[:, :, pl.ds(0, 32)], grad_send.at[3, k])

        @pl.when((section != helper) & (section != diagonal))
        def _():
            wait_for(own_tiles.at[pl.ds(0, 3)], grad_send.at[1, k])
            wait_for(column_part(k, 1), grad_send.at[2, k])

            @pl.when(section != block)
            def _():
                wait_for(column.at[:, :, pl.ds(0, 16)], grad_send.at[3, k])

        @pl.when(section == block)
        def _():
            wait_for(column, grad_send.at[4, k])

        if groups > 1:
            @pl.when(section != diagonal)
            def _():
                wait_for(group_part.at[k, 0, pl.ds(0, groups - 1)], group_send.at[0, k])

            @pl.when(section == helper)
            def _():
                wait_for(group_part.at[k, 1, pl.ds(0, groups - 1)], group_send.at[1, k])
        return 0

    lax.fori_loop(1, stages, drain_grads, 0)
    wait_for(core_part.at[0], grad_send.at[0, 0])
    wait_for(section_part.at[0, 0, pl.ds(0, sections - 1)], grad_send.at[1, 0])
    wait_for(column_part(0, 1), grad_send.at[2, 0])
    if groups > 1:
        wait_for(group_part.at[0, 0, pl.ds(0, groups - 1)], group_send.at[0, 0])
    wait_for(whole.at[0, :, :, 0, pl.ds(0, 16 * (sections - 1))], grad_send.at[3, 0])
    wait_for(whole.at[0, :, :, 0], grad_send.at[4, 0])
    wait_for(flat_core, grad_send.at[0, extra])
    wait_for(flat_section.at[pl.ds(0, sections - 1)], grad_send.at[1, extra])
    wait_for(flat_whole.at[0, 0, pl.ds(0, 48 * (chips - 1)), pl.ds(0, half)], grad_send.at[2, extra])
    wait_for(flat_whole.at[:, 0, pl.ds(0, 48 * (sections - 1))], grad_send.at[3, extra])
    wait_for(flat_whole.at[:, 0], grad_send.at[4, extra])
    if groups > 1:
        wait_for(flat_group.at[0, 0, pl.ds(0, groups - 1)], group_send.at[0, extra])
    first_copy.wait()
    second_copy.wait()
    unite_done.wait()
    camera_done.wait()


def widen(cam, *refs):
    held_in, outs, narrow, full = refs[0:9], refs[9:22], refs[22:31], refs[31:34]
    in_sem, out_sem, plain_sem = refs[34:37]
    loads = [pltpu.make_async_copy(a, b, in_sem.at[n]) for n, (a, b) in enumerate(zip(held_in, narrow))]
    for load in loads:
        load.start()
    passed = []
    channels = full[1].shape[-1]

    def store(number, tap):
        return pltpu.make_async_copy(full[number].at[tap], outs[10 + number].at[tap], out_sem.at[number, tap])

    loads[0].wait()
    loads[1].wait()

    def unite_tap(tap, unused):
        full[0][tap, 0:channels] = narrow[0][tap].astype(f32)
        rows = pl.ds(pl.multiple_of(cam * tap, 16), cam)
        full[0][tap, channels : channels + cam] = narrow[1][rows].astype(f32)
        store(0, tap).start()
        return 0

    lax.fori_loop(0, 9, unite_tap, 0)
    for number in (1, 2):
        loads[number + 1].wait()

        def block_tap(tap, unused):
            full[number][tap] = narrow[number + 1][tap].astype(f32)
            store(number, tap).start()
            return 0

        lax.fori_loop(0, 9, block_tap, 0)
    for number in range(4, 9):
        loads[number].wait()
    for number in range(10):
        source = narrow[4 + number] if number < 4 else narrow[8].at[number - 4]
        passed.append(pltpu.make_async_copy(source, outs[number], plain_sem.at[number]))
        passed[-1].start()
    for number in range(3):
        for tap in range(9):
            store(number, tap).wait()
    for copy in passed:
        copy.wait()


def body(
    lidar, context, depth_logits, cell_index, unite_weight, unite_gain, unite_bias, first_weight, second_weight,
    first_gain, first_bias, second_gain, second_bias, cotangent,
):
    peers = lax.axis_size("dp")
    sections = lax.axis_size("section")
    section = lax.axis_index("section")
    channels = cotangent.shape[-1]
    pixels, bins = depth_logits.shape[2:]
    cam = context.shape[-1]
    united_in = unite_weight.shape[1]
    blocks = sections
    stages = 2 * blocks + 1
    events = 2 * stages - 1
    groups = peers // (2 * chips)
    taken = 9 * channels

    vmem = pl.BlockSpec(memory_space=pltpu.VMEM)
    hbm = pl.BlockSpec(memory_space=pltpu.HBM)
    shape = jax.ShapeDtypeStruct
    dma = pltpu.SemaphoreType.DMA
    results = pl.pallas_call(
        functools.partial(kernel, peers, sections),
        out_shape=(
            shape((cells, channels), f32),
            shape((cells, channels), f32),
            shape((cam, pixels), f32),
            shape((bins, 1, pixels), f32),
            shape((9, 2, 2, 64, channels), bf16),
            shape((2, 2, flat_rows // 4, channels), bf16),
            shape((9, 2, 2, 64, channels), bf16),
            shape((9, 2, 2, 64, channels), bf16),
            shape((6, 1, channels), f32),
        ),
        in_specs=[hbm, vmem, vmem, vmem, hbm, vmem, vmem, hbm, hbm, vmem, vmem, vmem, vmem, hbm],
        out_specs=[vmem, vmem, vmem, vmem, hbm, hbm, hbm, hbm, vmem],
        scratch_shapes=[
            pltpu.VMEM((2 * blocks, taken, channels), bf16),
            pltpu.VMEM((9 * united_in, channels), bf16),
            pltpu.VMEM((blocks, 4, channels), f32),
            pltpu.VMEM((cells + 2 * side, 3 * wide), bf16),
            pltpu.VMEM((chips, cells + 2 * side, 3 * channels), bf16),
            pltpu.VMEM((chips, cells, channels), bf16),
            pltpu.VMEM((2 * blocks, chips, cells, channels), bf16),
            pltpu.VMEM((stages, chips, cells, channels), f32),
            pltpu.VMEM((stages + 1, 1, channels), f32),
            pltpu.VMEM((chips, cells, channels), f32),
            pltpu.VMEM((chips, cells, channels), bf16),
            pltpu.VMEM((chips, cells, channels), bf16),
            pltpu.VMEM((chips, cells, channels), bf16),
            pltpu.VMEM((chips, cells, half), bf16),
            pltpu.VMEM((events, 2, channels), f32),
            pltpu.VMEM((events, 2 * groups, 2, channels), f32),
            pltpu.VMEM((2, channels), f32),
            pltpu.VMEM((peers, 2, channels), f32),
            pltpu.VMEM((half, pixels), f32),
            pltpu.VMEM((half, pixels), f32),
            pltpu.VMEM((cells, pixels), bf16),
            pltpu.VMEM((stages, 9, 2, 64, half), bf16),
            pltpu.VMEM((stages, 9, 64, half), bf16),
            pltpu.VMEM((stages, 9, 64, half), bf16),
            pltpu.VMEM((stages, 2, sections, 9, 16, half), bf16),
            pltpu.VMEM((stages, 9, 2, 2, 64, channels), bf16),
            pltpu.VMEM((flat_rows, half), bf16),
            pltpu.VMEM((flat_rows // 4, half), bf16),
            pltpu.VMEM((flat_rows // 4, half), bf16),
            pltpu.VMEM((sections, 48, half), bf16),
            pltpu.VMEM((2, 2, flat_rows // 4, channels), bf16),
            pltpu.VMEM((sections, stages, 2, channels), f32),
            pltpu.VMEM((2, channels), f32),
            pltpu.VMEM((stages if groups > 1 else 1, 2, groups, 9, 16, half), bf16),
            pltpu.VMEM((1, 1, groups, 48, half), bf16),
            dma((9,)), dma, dma, dma((events,)), dma((events,)), dma((chips,)), dma((chips,)), dma((chips,)),
            dma((chips,)), dma((chips,)), dma((chips,)), dma((chips,)), dma((chips,)), dma((4,)),
            dma((2 * blocks,)), dma((2,)), dma((2 * blocks,)), dma((2 * blocks,)), dma, dma,
            dma((5, stages + 1)), dma((5, stages + 1)), dma, dma, dma((2, stages + 1)), dma((2, stages + 1)),
        ],
        compiler_params=pltpu.CompilerParams(
            collective_id=0, has_side_effects=True, vmem_limit_bytes=60 << 20
        ),
    )(
        lidar.reshape(cells, channels), context.reshape(pixels, cam).T, depth_logits.reshape(pixels, bins).T,
        jnp.transpose(cell_index, (0, 3, 1, 2)).reshape(bins, 1, pixels), unite_weight.reshape(-1, channels),
        unite_gain[None], unite_bias[None], first_weight.reshape(taken, channels),
        second_weight.reshape(taken, channels), first_gain, first_bias, second_gain, second_bias,
        cotangent.reshape(-1, cells, channels),
    )

    act, lidar_grad, context_grad, logit_grad, *small, unite_whole, first_whole, second_whole = pl.pallas_call(
        functools.partial(widen, cam),
        out_shape=(
            shape((cells, channels), f32),
            shape((cells, channels), f32),
            shape((cam, pixels), f32),
            shape((bins, 1, pixels), f32),
            *[shape((1, channels), f32)] * 6,
            shape((9, united_in, channels), f32),
            shape((9, channels, channels), f32),
            shape((9, channels, channels), f32),
        ),
        in_specs=[hbm] * 9,
        out_specs=[hbm] * 13,
        scratch_shapes=[
            pltpu.VMEM((9, channels, channels), bf16),
            pltpu.VMEM((flat_rows, channels), bf16),
            pltpu.VMEM((9, channels, channels), bf16),
            pltpu.VMEM((9, channels, channels), bf16),
            pltpu.VMEM((cells, channels), f32),
            pltpu.VMEM((cells, channels), f32),
            pltpu.VMEM((cam, pixels), f32),
            pltpu.VMEM((bins, 1, pixels), f32),
            pltpu.VMEM((6, 1, channels), f32),
            pltpu.VMEM((9, united_in, channels), f32),
            pltpu.VMEM((9, channels, channels), f32),
            pltpu.VMEM((9, channels, channels), f32),
            dma((9,)), dma((3, 9)), dma((10,)),
        ],
        compiler_params=pltpu.CompilerParams(vmem_limit_bytes=60 << 20),
    )(
        results[4].reshape(9, channels, channels), results[5].reshape(flat_rows, channels),
        results[6].reshape(9, channels, channels), results[7].reshape(9, channels, channels), *results[0:4], results[8],
    )
    return (
        act.reshape(lidar.shape),
        lidar_grad.reshape(lidar.shape),
        context_grad.T.reshape(context.shape),
        jnp.transpose(logit_grad.reshape(1, bins, 1, pixels), (0, 2, 3, 1)),
        unite_whole,
        small[0].reshape(channels),
        small[1].reshape(channels),
        first_whole.reshape(first_weight.shape),
        second_whole.reshape(second_weight.shape),
        *small[2:6],
    )


def solution(mesh):
    split, by_dp = P("section"), P("section", "dp")
    in_specs = (by_dp, by_dp, by_dp, by_dp, P(), P(), P(), split, split, split, split, split, split, P(None, "dp"))
    out_specs = (by_dp, by_dp, by_dp, by_dp, P(), P(), P(), split, split, split, split, split, split)
    return jax.shard_map(body, mesh=mesh, in_specs=in_specs, out_specs=out_specs, check_vma=False)
```

```python
import functools

import jax
import jax.numpy as jnp
from jax import lax
from jax.experimental import pallas as pl
from jax.experimental.pallas import tpu as pltpu
from jax.sharding import PartitionSpec as P

eps = 1e-05
f32, bf16 = jnp.float32, jnp.bfloat16
MESH = pl.DeviceIdType.MESH
side = 16
cells = side * side
wide = 384
chips = 4
half = 128
column_lag = 4
owner_lag = 8
flat_rows = 768
transposed_rhs = (((1,), (1,)), ((), ()))
transposed_lhs = (((0,), (0,)), ((), ()))


def silu_of_half(half_value):
    return half_value + half_value * jnp.tanh(half_value)


def twice_slope_of_half(half_value):
    bent = jnp.tanh(half_value)
    return 1.0 + bent + half_value * (1.0 - bent * bent)


def put_shifted(buffer, value, stride, offset=0):
    width = value.shape[1]
    split = value.reshape(side, 2, 8, width)
    row = lax.broadcasted_iota(jnp.int32, (1, 8, width), 1)
    down = pltpu.roll(split, 1, 2)
    up = pltpu.roll(split, 7, 2)
    before = jnp.stack([jnp.where(row == 0, 0.0, down[:, 0]), jnp.where(row == 0, down[:, 0], down[:, 1])], axis=1)
    after = jnp.stack([jnp.where(row == 7, up[:, 1], up[:, 0]), jnp.where(row == 7, 0.0, up[:, 1])], axis=1)
    for group, shifted in enumerate((before, split, after)):
        start = group * stride + offset
        buffer[side : side + cells, start : start + width] = shifted.reshape(cells, width).astype(bf16)


def total_of(terms):
    total = None
    for term in terms:
        total = term if total is None else total + term
    return total


def conv(buffer, weight):
    return total_of(
        jnp.dot(buffer[side * i : side * i + cells, :], weight(i), preferred_element_type=f32) for i in range(3)
    )


def conv_transposed(buffer, weight, width):
    return total_of(
        lax.dot_general(
            buffer[side * (2 - i) : side * (2 - i) + cells, width * (2 - j) : width * (3 - j)],
            weight(3 * i + j),
            transposed_rhs,
            preferred_element_type=f32,
        )
        for i in range(3)
        for j in range(3)
    )


plan = {
    "start": [("offer", 0, "near", 0), ("offer", 0, "far", 3), ("offer", 0, "near", 2), ("offer", 0, "near", 1)],
    "lift2": [("offer", 0, "near", 3), ("offer", 1, "near", 0)],
    "united": [("relay", 0, 0), ("offer", 1, "near", 1), ("offer", 1, "near", 3)],
    "united2": [("offer", 1, "far", 0), ("offer", 1, "near", 2), ("offer", 0, "far", 1)],
    "merged": [("offer", 0, "far", 0), ("relay", 1, 0)],
    "entered1": [("relay", 3, 0), ("relay", 0, 1), ("relay", 2, 0)],
    "entered3": [("offer", 0, "far", 2), ("offer", 1, "far", 1)],
    "entered2": [("relay", 2, 1)],
    "entered": [("offer", 1, "far", 2), ("arrive", 0, 0)],
    ("first", 0): [("relay", 1, 1), ("arrive", 1, 0), ("offer", 1, "far", 3), ("arrive", 0, 1)],
    ("second", 0): [("relay", 3, 1)],
    ("first", 1): [("arrive", 1, 1), ("arrive", 2, 0)],
    ("second", 1): [("arrive", 3, 0), ("arrive", 2, 1)],
    ("second", 2): [("arrive", 3, 1)],
}


def kernel(
    peers, sections,
    lidar_ref, context_ref, logit_ref, cell_ref, unite_ref, unite_gain, unite_bias, first_ref, second_ref,
    first_gain, first_bias, second_gain, second_bias, cotangent_ref,
    act_ref, lidar_grad, context_grad, logit_grad, unite_out, camera_out, first_out, second_out, small_out,
    weights, unite_weight, vectors, joined, shifted, current, kept, halves, scales, held, gathered, upstream,
    lidars, cameras, mine, slots, unite_mine, unite_slots, probability, places, histogram,
    partial, core_part, own_part, section_part, whole, flat, flat_core, flat_own, flat_section, flat_whole,
    totals, gains, group_part, flat_group,
    local_sem, unite_send, unite_recv, stat_send, stat_recv, raw_send, raw_recv, cot_send, cot_recv,
    lidar_send, lidar_recv, camera_send, camera_recv, weight_send, weight_recv, relay_send, pass_send, pass_recv,
    vector_send, vector_recv, grad_send, grad_recv, total_send, total_recv, group_send, group_recv,
):
    me = lax.axis_index("dp")
    section = lax.axis_index("section")
    core = lax.rem(me, 2)
    chip = lax.rem(lax.div(me, 2), chips)
    group = lax.div(me, 2 * chips)
    groups = peers // (2 * chips)
    blocks = sections
    stages = 2 * blocks + 1
    channels = vectors.shape[-1]
    bins = logit_ref.shape[0]
    cam = context_ref.shape[0]
    united_in = channels + cam
    taken = 9 * channels
    row_half = lax.div(chip, 2)
    lane_half = lax.rem(chip, 2)
    count = float(peers * cells)

    def at(other_section=None, other=None):
        return (section if other_section is None else other_section, me if other is None else other)

    def chip_peer(step):
        return group * (2 * chips) + lax.rem(chip + step, chips) * 2 + core

    sibling = me + 1 - 2 * core

    def remote(source, target, send, recv, device):
        return pltpu.make_async_remote_copy(
            src_ref=source, dst_ref=target, send_sem=send, recv_sem=recv, device_id=device, device_id_type=MESH
        )

    def wait_for(part, semaphore):
        pltpu.make_async_copy(part, part, semaphore).wait()

    barrier = pltpu.get_barrier_semaphore()
    for step in range(1, sections):
        pl.semaphore_signal(
            barrier, inc=1, device_id=at(other_section=lax.rem(section + step, sections)), device_id_type=MESH
        )

    def greet(step, unused):
        pl.semaphore_signal(barrier, inc=1, device_id=at(other=lax.rem(me + step, peers)), device_id_type=MESH)
        return 0

    lax.fori_loop(1, peers, greet, 0)

    unite_copy = pltpu.make_async_copy(unite_ref, unite_weight, local_sem.at[0])
    own_first = pltpu.make_async_copy(first_ref, weights.at[2 * section], local_sem.at[1])
    own_second = pltpu.make_async_copy(second_ref, weights.at[2 * section + 1], local_sem.at[2])
    own_cot = pltpu.make_async_copy(cotangent_ref.at[section], upstream.at[chip], local_sem.at[3])
    own_lidar = pltpu.make_async_copy(lidar_ref, lidars.at[chip], local_sem.at[4])
    own_lidar.start()
    unite_copy.start()
    own_first.start()
    own_second.start()
    own_cot.start()
    for number, part in enumerate((first_gain, first_bias, second_gain, second_bias)):
        vectors[section, number : number + 1] = part[...]
    joined[...] = jnp.zeros_like(joined)
    probability[...] = jnp.zeros_like(probability)
    places[...] = jnp.zeros_like(places)
    cameras[chip] = jnp.zeros((cells, half), bf16)
    pl.semaphore_wait(barrier, peers - 1 + sections - 1)

    beside = section + 1 - 2 * lax.rem(section, 2)
    across = lax.rem(section + 2, sections)
    near = beside + core * (across - beside)
    far = across + core * (beside - across)
    part_rows = taken // 2
    part = pl.ds(pl.multiple_of(core * part_rows, part_rows), part_rows)
    sources = (first_ref, second_ref)

    def offer(which, target, number):
        index = 2 * section + which
        remote(
            sources[which].at[part], weights.at[index, part], weight_send.at[number], weight_recv.at[index],
            at(other_section=target),
        ).start()

    def arrived(index):
        wait_for(weights.at[index, part], weight_recv.at[index])

    def pass_on(index):
        remote(
            weights.at[index, part], weights.at[index, part], pass_send.at[index], pass_recv.at[index],
            at(other=sibling),
        ).start()

    def relay(block, which):
        index = 2 * block + which

        @pl.when(near == block)
        def _():
            arrived(index)
            remote(
                weights.at[index, part], weights.at[index, part], relay_send.at[which], weight_recv.at[index],
                at(other_section=far),
            ).start()
            pass_on(index)

    def arrive(block, which):
        index = 2 * block + which

        @pl.when((section != block) & (near != block))
        def _():
            arrived(index)
            pass_on(index)

    def ready(block, which):
        index = 2 * block + which
        rest = pl.ds(pl.multiple_of((1 - core) * part_rows, part_rows), part_rows)

        @pl.when(section != block)
        def _():
            wait_for(weights.at[index, rest], pass_recv.at[index])

        @pl.when(section == block)
        def _():
            (own_second if which else own_first).wait()

    def act_on(entry):
        name, one, two = entry[0:3]
        if name == "relay":
            relay(one, two)
        elif name == "arrive":
            arrive(one, two)
        else:
            @pl.when(section == entry[3])
            def _():
                offer(one, near if two == "near" else far, 2 * one + (two == "far"))

    def point(name, block=None):
        for key, entries in plan.items():
            if isinstance(key, tuple) and key[0] == name:
                @pl.when(block == key[1])
                def _():
                    for entry in entries:
                        act_on(entry)
            elif key == name:
                for entry in entries:
                    act_on(entry)

    point("start")
    for step in range(1, sections):
        remote(
            vectors.at[section], vectors.at[section], vector_send, vector_recv,
            at(other_section=lax.rem(section + step, sections)),
        ).start()

    logits = logit_ref[...].astype(f32)
    raised = jnp.exp(logits - jnp.max(logits, axis=0, keepdims=True))
    probability[0:bins] = raised / jnp.sum(raised, axis=0, keepdims=True)
    address = lax.broadcasted_iota(jnp.int32, (cells, half), 0)

    def add_bin(number, total):
        place = cell_ref[number]
        places[pl.ds(number, 1)] = place.astype(f32)
        return total + jnp.where(place == address, probability[pl.ds(number, 1)], 0.0)

    counted = jnp.zeros((cells, half), f32)
    for number in range(3):
        counted = lax.fori_loop(bins * number // 3, bins * (number + 1) // 3, add_bin, counted)
        if number < 2:
            point(f"lift{number + 1}")
    counted = counted.astype(bf16)
    histogram[...] = counted
    pooled = lax.dot_general(counted, context_ref[...], transposed_rhs, preferred_element_type=f32)
    cameras[chip, :, 0:cam] = pooled.astype(bf16)

    own_lidar.wait()
    put_shifted(joined, lidars[chip].astype(f32), wide)
    put_shifted(joined, pooled, wide, channels)
    unite_copy.wait()
    united = total_of(
        jnp.dot(
            joined[side * i : side * i + cells, wide * j : wide * j + united_in],
            unite_weight[united_in * (3 * i + j) : united_in * (3 * i + j + 1), :],
            preferred_element_type=f32,
        )
        for i in range(3)
        for j in range(3)
    )
    gathered[chip] = united.astype(bf16)
    for step in range(1, chips):
        remote(
            gathered.at[chip], gathered.at[chip], raw_send.at[step], raw_recv.at[step], at(other=chip_peer(step))
        ).start()
    center = jnp.sum(united, axis=0, keepdims=True) * (1.0 / cells)
    offsets = united - center
    unite_mine[0:1] = center
    unite_mine[1:2] = jnp.sum(offsets * offsets, axis=0, keepdims=True)
    unite_slots[me] = unite_mine[...]

    def send_unite(step, unused):
        remote(
            unite_mine, unite_slots.at[me], unite_send, unite_recv, at(other=lax.rem(me + step, peers))
        ).start()
        return 0

    lax.fori_loop(1, peers, send_unite, 0)

    point("united")
    shifted[...] = jnp.zeros_like(shifted)
    flat[9 * cam :, :] = jnp.zeros((flat_rows - 9 * cam, half), bf16)

    def merged(centers, squares, each):
        parts = centers.shape[0]
        center = jnp.sum(centers, axis=0, keepdims=True) * (1.0 / parts)
        apart = centers - center
        square = jnp.sum(squares, axis=0, keepdims=True) + each * jnp.sum(apart * apart, axis=0, keepdims=True)
        return center, square

    point("united2")
    wait_for(unite_slots.at[pl.ds(0, peers - 1)], unite_recv)
    center, square = merged(unite_slots[:, 0, :], unite_slots[:, 1, :], cells)
    scales[0] = lax.rsqrt(square * (1.0 / count) + eps)
    scales[stages] = center
    point("merged")

    def half_affine(center, scale, gain, bias):
        factor = 0.5 * gain * scale
        return factor, 0.5 * bias - center * factor

    factor, offset = half_affine(scales[stages], scales[0], unite_gain[...], unite_bias[...])

    def enter(number):
        value = gathered[number].astype(f32) * factor + offset
        halves[0, number] = value
        entering = silu_of_half(value)
        current[number] = entering.astype(bf16)
        kept[0, number] = entering.astype(bf16)
        put_shifted(shifted.at[number], entering, channels)

    enter(chip)
    for step in (1, 3, 2):
        wait_for(gathered.at[0], raw_recv.at[step])
        enter(lax.rem(chip - step + chips, chips))
        point(f"entered{step}")

    own_cot.wait()
    for step in range(1, chips):
        peer = at(other=chip_peer(step))
        remote(upstream.at[chip], upstream.at[chip], cot_send.at[step], cot_recv.at[step], peer).start()
    for step in range(1, chips):
        peer = at(other=chip_peer(step))
        remote(lidars.at[chip], lidars.at[chip], lidar_send.at[step], lidar_recv.at[step], peer).start()
        remote(cameras.at[chip], cameras.at[chip], camera_send.at[step], camera_recv.at[step], peer).start()

    point("entered")
    wait_for(vectors.at[pl.ds(0, sections - 1)], vector_recv)

    members = 2 * groups
    place = group * 2 + core

    def copy_stats(event, step):
        to = lax.rem(place + step, members)
        return remote(
            mine.at[event], slots.at[event, place], stat_send.at[event], stat_recv.at[event],
            at(other=lax.div(to, 2) * (2 * chips) + chip * 2 + lax.rem(to, 2)),
        )

    def send_stats(event, first, second):
        mine[event, 0:1] = first
        mine[event, 1:2] = second
        slots[event, place] = mine[event]
        for step in range(1, members):
            copy_stats(event, step).start()

    def take_stats(event):
        wait_for(slots.at[event, pl.ds(0, members - 1)], stat_recv.at[event])
        return slots[event, :, 0, :], slots[event, :, 1, :]

    def local_sums(parts):
        centers, squares = zip(*parts)
        return merged(jnp.concatenate(centers, axis=0), jnp.concatenate(squares, axis=0), cells)

    def start_conv(number, index):
        activ = conv(shifted.at[number], lambda i: weights[index, 3 * channels * i : 3 * channels * (i + 1), :])
        held[number] = activ
        center = jnp.sum(activ, axis=0, keepdims=True) * (1.0 / cells)
        offsets = activ - center
        return center, jnp.sum(offsets * offsets, axis=0, keepdims=True)

    def whole_sums(stage):
        centers, squares = take_stats(stage - 1)
        center, square = merged(centers, squares, chips * cells)
        scale = lax.rsqrt(square * (1.0 / count) + eps)
        scales[stage] = scale
        return center, scale

    def block(s, last):
        stage = 2 * s + 1

        def vector(number):
            return vectors[s, number : number + 1]

        point("first", s)
        ready(s, 1)
        factor, offset = half_affine(*whole_sums(stage), vector(0), vector(1))
        parts = []
        for number in range(chips):
            value = held[number] * factor + offset
            halves[stage, number] = value
            hidden = silu_of_half(value)
            kept[stage, number] = hidden.astype(bf16)
            put_shifted(shifted.at[number], hidden, channels)
            parts.append(start_conv(number, 2 * s + 1))
        send_stats(stage, *local_sums(parts))
        point("second", s)
        if not last:
            ready(s + 1, 0)
        factor, offset = half_affine(*whole_sums(stage + 1), vector(2), vector(3))
        parts = []
        for number in range(chips):
            value = held[number] * factor + offset
            halves[stage + 1, number] = value
            output = current[number].astype(f32) + silu_of_half(value)
            if last:
                held[number] = output
            else:
                current[number] = output.astype(bf16)
                kept[stage + 1, number] = output.astype(bf16)
                put_shifted(shifted.at[number], output, channels)
                parts.append(start_conv(number, 2 * s + 2))
        if not last:
            send_stats(stage + 1, *local_sums(parts))

    def block_step(s, unused):
        block(s, False)
        return 0

    ready(0, 0)
    send_stats(0, *local_sums([start_conv(number, 0) for number in range(chips)]))
    lax.fori_loop(0, blocks - 1, block_step, 0)
    block(blocks - 1, True)
    act_ref[...] = held[chip]

    lanes = pl.ds(pl.multiple_of(lane_half * half, half), half)
    flat48 = pl.ds(pl.multiple_of(section * 48, 16), 48)

    def lateral(j):
        return pl.ds(pl.multiple_of(channels * (2 - j) + lane_half * half, half), half)

    def weight_grad(stage, inputs):
        columns = pl.ds(pl.multiple_of(row_half * half, half), half)
        values = [inputs[number, :, columns] for number in range(chips)]
        for i in range(3):
            for j in range(3):
                taps = total_of(
                    lax.dot_general(
                        values[number],
                        shifted[number, side * (2 - i) : side * (2 - i) + cells, lateral(j)],
                        transposed_lhs,
                        preferred_element_type=f32,
                    )
                    for number in range(chips)
                ).astype(bf16)
                partial[stage, 3 * i + j, 0] = taps[0:64]
                partial[stage, 3 * i + j, 1] = taps[64:128]
        to_sibling(stage)

    def to_sibling(k):
        remote(
            partial.at[k, :, 1 - core], core_part.at[k], grad_send.at[0, k], grad_recv.at[0, k], at(other=sibling)
        ).start()

    def block_of(k):
        return lax.div(k - 1, 2)

    def roles(k):
        block = block_of(k)
        across_x = block + 1 - 2 * lax.rem(block, 2)
        across_y = lax.rem(block + 2, sections)
        return block, sections - 1 - block, across_x + core * (across_y - across_x)

    def tile(index):
        return pl.ds(pl.multiple_of(index * 16, 16), 16)

    def sum_cores(k):
        wait_for(core_part.at[k], grad_recv.at[0, k])
        for tap in range(9):
            own_part[k, tap] = (partial[k, tap, core].astype(f32) + core_part[k, tap].astype(f32)).astype(bf16)

    def send_tile(k, index, slot, other):
        remote(
            own_part.at[k, :, tile(index)], section_part.at[k, slot, section], grad_send.at[1, k], grad_recv.at[1, k],
            at(other_section=other),
        ).start()

    def to_sections(k):
        sum_cores(k)
        block, diagonal, helper = roles(k)
        for step in range(1, sections):
            other = lax.rem(section + step, sections)

            @pl.when(other != diagonal)
            def _():
                send_tile(k, other, 0, other)

            @pl.when(other == helper)
            def _():
                send_tile(k, diagonal, 1, other)

        section_part[k, 0, section] = own_part[k, :, tile(section)]

        @pl.when(section == helper)
        def _():
            section_part[k, 1, section] = own_part[k, :, tile(diagonal)]

    def over_groups(slot, k, value, buffer, number):
        if groups == 1:
            return value
        mine_here = buffer.at[k, slot, group]
        mine_here[...] = value
        for step in range(1, groups):
            to = lax.rem(group + step, groups) * (2 * chips) + chip * 2 + core
            remote(
                mine_here, mine_here, group_send.at[slot, number], group_recv.at[slot, number], at(other=to)
            ).start()
        wait_for(buffer.at[k, slot, pl.ds(0, groups - 1)], group_recv.at[slot, number])
        return jnp.sum(buffer[k, slot].astype(f32), axis=0).astype(bf16)

    def reduce_tile(k, slot, index):
        piece = total_of(section_part[k, slot, number].astype(f32) for number in range(sections)).astype(bf16)
        place = whole.at[k, :, row_half, core, tile(index), lanes]
        place[...] = over_groups(slot, k, piece, group_part, k)
        for step in range(1, chips):
            remote(place, place, grad_send.at[2, k], grad_recv.at[2, k], at(other=chip_peer(step))).start()

    def to_column(k):
        block, diagonal, helper = roles(k)

        @pl.when(section == helper)
        def _():
            wait_for(section_part.at[k, :, pl.ds(0, sections - 1)], grad_recv.at[1, k])
            reduce_tile(k, 0, section)
            reduce_tile(k, 1, diagonal)

        @pl.when((section != helper) & (section != diagonal))
        def _():
            wait_for(section_part.at[k, 0, pl.ds(0, sections - 1)], grad_recv.at[1, k])
            reduce_tile(k, 0, section)

    def column_part(k, tiles):
        return whole.at[k, :, 0, 0, pl.ds(0, 16 * (chips - 1)), pl.ds(0, half * tiles)]

    def hand_over(k, index, block):
        place = whole.at[k, :, :, core, tile(index)]
        remote(place, place, grad_send.at[3, k], grad_recv.at[3, k], at(other_section=block)).start()

    def to_owner(k):
        block, diagonal, helper = roles(k)

        @pl.when(section == helper)
        def _():
            wait_for(column_part(k, 2), grad_recv.at[2, k])
            hand_over(k, section, block)
            hand_over(k, diagonal, block)

        @pl.when((section != helper) & (section != diagonal))
        def _():
            wait_for(column_part(k, 1), grad_recv.at[2, k])

            @pl.when(section != block)
            def _():
                hand_over(k, section, block)

    def to_sections_all(k):
        sum_cores(k)
        section_part[k, 0, section] = own_part[k, :, tile(section)]
        for step in range(1, sections):
            other = lax.rem(section + step, sections)
            send_tile(k, other, 0, other)

    def to_column_all(k):
        wait_for(section_part.at[k, 0, pl.ds(0, sections - 1)], grad_recv.at[1, k])
        reduce_tile(k, 0, section)

    def to_all(k):
        wait_for(column_part(k, 1), grad_recv.at[2, k])
        place = whole.at[k, :, :, core, tile(section)]
        for step in range(1, sections):
            other = lax.rem(section + step, sections)
            remote(place, place, grad_send.at[3, k], grad_recv.at[3, k], at(other_section=other)).start()

    def share(k):
        wait_for(whole.at[k, :, :, 0, pl.ds(0, 16 * (sections - 1))], grad_recv.at[3, k])
        place = whole.at[k, :, :, core]
        remote(place, place, grad_send.at[4, k], grad_recv.at[4, k], at(other=sibling)).start()

    def owner_share(k):
        @pl.when(section == block_of(k))
        def _():
            share(k)

    def shared(k):
        wait_for(whole.at[k, :, :, 0], grad_recv.at[4, k])

    def backwards(first, last, act):
        def step(number, unused):
            act(first - number)
            return 0

        lax.fori_loop(0, first - last + 1, step, 0)

    def when_due(k, act):
        @pl.when(k <= stages - 1)
        def _():
            act(k)

    def start_norm(stage, number, grads):
        value = halves[stage, number]
        grads = grads * twice_slope_of_half(value)
        held[number] = grads
        return jnp.sum(grads, axis=0, keepdims=True), jnp.sum(grads * value, axis=0, keepdims=True)

    def send_sums(stage, parts, gain, bias):
        firsts, seconds = zip(*parts)
        first = 0.5 * total_of(firsts)
        send_stats(stages - 1 + stage, first, (total_of(seconds) - bias * first) / gain)

    def norm_factors(stage, gain, bias):
        first, second = take_stats(stages - 1 + stage)
        first = jnp.sum(first, axis=0, keepdims=True)
        second = jnp.sum(second, axis=0, keepdims=True)
        totals[section, stage, 0:1] = first
        totals[section, stage, 1:2] = second
        first = first * (1.0 / count)
        second = second * (1.0 / count)
        scale = scales[stage]
        return 0.5 * gain * scale, 2.0 * scale * second, scale * (gain * first - bias * second)

    def end_norm(stage, number, factors):
        by_grads, by_halves, constant = factors
        put_shifted(
            shifted.at[number], held[number] * by_grads - halves[stage, number] * by_halves - constant, channels
        )

    def passed(number, index):
        return conv_transposed(
            shifted.at[number], lambda tap: weights[index, channels * tap : channels * (tap + 1), :], channels
        )

    def during(stage):
        when_due(stage + 2, to_sections)
        weight_grad(stage + 1, kept.at[stage])
        when_due(stage + column_lag, to_column)
        when_due(stage + owner_lag, to_owner)

    for step in range(1, chips):
        wait_for(upstream.at[0], cot_recv.at[step])
        wait_for(upstream.at[0], cot_send.at[step])
    def take_gains(s):
        @pl.when(s > 0)
        def _():
            gains[0:1] = vectors[jnp.maximum(s - 1, 0), 2:3]
            gains[1:2] = vectors[jnp.maximum(s - 1, 0), 3:4]

        @pl.when(s == 0)
        def _():
            gains[0:1] = unite_gain[...]
            gains[1:2] = unite_bias[...]

    take_gains(blocks)
    send_sums(
        stages - 1,
        [
            start_norm(stages - 1, number, upstream[number].astype(f32))
            for number in range(chips)
        ],
        gains[0:1], gains[1:2],
    )

    def block_back(back, unused):
        s = blocks - 1 - back
        stage = 2 * s + 1

        def vector(number):
            return vectors[s, number : number + 1]

        @pl.when(back > 0)
        def _():
            during(stage + 1)

        factors = norm_factors(stage + 1, vector(2), vector(3))
        parts = []
        for number in range(chips):
            end_norm(stage + 1, number, factors)
            parts.append(start_norm(stage, number, passed(number, 2 * s + 1)))
        send_sums(stage, parts, vector(0), vector(1))
        during(stage)
        take_gains(s)
        factors = norm_factors(stage, vector(0), vector(1))
        parts = []
        for number in range(chips):
            end_norm(stage, number, factors)
            grads = (upstream[number].astype(f32) + passed(number, 2 * s)).astype(bf16)
            upstream[number] = grads
            parts.append(start_norm(stage - 1, number, grads.astype(f32)))
        send_sums(stage - 1, parts, gains[0:1], gains[1:2])
        return 0

    lax.fori_loop(0, blocks, block_back, 0)

    during(0)
    for step in range(1, chips):
        wait_for(lidars.at[0], lidar_recv.at[step])
        wait_for(cameras.at[0], camera_recv.at[step])
    factors = norm_factors(0, unite_gain[...], unite_bias[...])
    for number in range(chips):
        end_norm(0, number, factors)
    weight_grad(0, lidars)
    to_sections(1)
    held_cameras = [cameras[number] for number in range(chips)]
    for i in range(3):
        for j in range(3):
            taps = total_of(
                lax.dot_general(
                    held_cameras[number],
                    shifted[number, side * (2 - i) : side * (2 - i) + cells, lateral(j)],
                    transposed_lhs,
                    preferred_element_type=f32,
                )
                for number in range(chips)
            ).astype(bf16)
            flat[cam * (3 * i + j) : cam * (3 * i + j + 1)] = taps[0:cam]
    quarter = flat_rows // 4
    kept_rows = pl.ds(pl.multiple_of(row_half * (2 * quarter) + core * quarter, 16), quarter)
    sent_rows = pl.ds(pl.multiple_of(row_half * (2 * quarter) + (1 - core) * quarter, 16), quarter)
    extra = stages
    remote(
        flat.at[sent_rows], flat_core, grad_send.at[0, extra], grad_recv.at[0, extra], at(other=sibling)
    ).start()
    to_sections_all(0)
    backwards(min(column_lag - 1, stages - 1), 2, to_column)
    for step in range(1, sections):
        remote(
            totals.at[section], totals.at[section], total_send, total_recv,
            at(other_section=lax.rem(section + step, sections)),
        ).start()
    own = shifted.at[chip]
    pooled_grad = conv_transposed(
        own, lambda tap: unite_weight[united_in * tap + channels : united_in * (tap + 1), :], channels
    ).astype(bf16)

    wait_for(flat_core, grad_recv.at[0, extra])
    flat_own[...] = (flat[kept_rows].astype(f32) + flat_core[...].astype(f32)).astype(bf16)
    flat_section[section] = flat_own[flat48]
    for step in range(1, sections):
        other = lax.rem(section + step, sections)
        remote(
            flat_own.at[pl.ds(pl.multiple_of(other * 48, 16), 48)], flat_section.at[section],
            grad_send.at[1, extra], grad_recv.at[1, extra], at(other_section=other),
        ).start()
    lidar_grad[...] = conv_transposed(
        own, lambda tap: unite_weight[united_in * tap : united_in * tap + channels, :], channels
    )
    to_column(1)

    context_grad[...] = lax.dot_general(pooled_grad, histogram[...], transposed_lhs, preferred_element_type=f32)
    table = lax.dot_general(
        context_ref[...], pooled_grad, (((0,), (1,)), ((), ())), preferred_element_type=f32
    )
    wanted = places[...].T.astype(jnp.int32)
    within = lax.rem(wanted, half)
    low = jnp.take_along_axis(table[:, 0:half], within, axis=1)
    high = jnp.take_along_axis(table[:, half : 2 * half], within, axis=1)
    chance_grad = jnp.where(wanted < half, low, high).T
    chance = probability[...]
    places[...] = chance * (chance_grad - jnp.sum(chance_grad * chance, axis=0, keepdims=True))

    def store_bin(number, unused):
        logit_grad[number] = places[pl.ds(number, 1)]
        return 0

    lax.fori_loop(0, bins, store_bin, 0)

    to_column_all(0)
    wait_for(flat_section.at[pl.ds(0, sections - 1)], grad_recv.at[1, extra])
    piece = total_of(flat_section[number].astype(f32) for number in range(sections)).astype(bf16)
    flat_place = flat_whole.at[row_half, core, flat48, lanes]
    flat_place[...] = over_groups(0, 0, piece, flat_group, extra)
    for step in range(1, chips):
        remote(
            flat_place, flat_place, grad_send.at[2, extra], grad_recv.at[2, extra], at(other=chip_peer(step))
        ).start()
    backwards(min(owner_lag - 1, stages - 1), 1, to_owner)
    to_all(0)
    wait_for(flat_whole.at[0, 0, pl.ds(0, 48 * (chips - 1)), pl.ds(0, half)], grad_recv.at[2, extra])
    flat_rows_place = flat_whole.at[:, core, flat48]
    for step in range(1, sections):
        other = lax.rem(section + step, sections)
        remote(
            flat_rows_place, flat_rows_place, grad_send.at[3, extra], grad_recv.at[3, extra],
            at(other_section=other),
        ).start()

    backwards(stages - 1, 1, owner_share)
    share(0)
    wait_for(flat_whole.at[:, 0, pl.ds(0, 48 * (sections - 1))], grad_recv.at[3, extra])
    flat_half = flat_whole.at[:, core]
    remote(flat_half, flat_half, grad_send.at[4, extra], grad_recv.at[4, extra], at(other=sibling)).start()

    wait_for(totals.at[pl.ds(0, sections - 1)], total_recv)
    def summed(stage, row):
        return total_of(totals[number, stage, row : row + 1] for number in range(sections))

    small_out[0] = summed(0, 1)
    small_out[1] = summed(0, 0)
    for number in range(2):
        small_out[2 + 2 * number] = summed(2 * section + 1 + number, 1)
        small_out[3 + 2 * number] = summed(2 * section + 1 + number, 0)
    shared(2 * section + 1)
    shared(2 * section + 2)
    first_copy = pltpu.make_async_copy(whole.at[2 * section + 1], first_out, local_sem.at[5])
    second_copy = pltpu.make_async_copy(whole.at[2 * section + 2], second_out, local_sem.at[6])
    first_copy.start()
    second_copy.start()
    shared(0)
    unite_done = pltpu.make_async_copy(whole.at[0], unite_out, local_sem.at[7])
    unite_done.start()
    wait_for(flat_whole.at[:, 0], grad_recv.at[4, extra])
    camera_done = pltpu.make_async_copy(flat_whole, camera_out, local_sem.at[8])
    camera_done.start()

    wait_for(unite_slots.at[pl.ds(0, peers - 1)], unite_send)
    for step in range(1, chips):
        wait_for(gathered.at[0], raw_send.at[step])
        wait_for(lidars.at[0], lidar_send.at[step])
        wait_for(cameras.at[0], camera_send.at[step])
    for number in range(4):
        wait_for(weights.at[0, part], weight_send.at[number])
    for number in range(2):
        wait_for(weights.at[0, part], relay_send.at[number])
    wait_for(vectors.at[pl.ds(0, sections - 1)], vector_send)
    wait_for(totals.at[pl.ds(0, sections - 1)], total_send)

    def drain_stats(event, unused):
        wait_for(slots.at[event, pl.ds(0, members - 1)], stat_send.at[event])
        return 0

    lax.fori_loop(0, 2 * stages - 1, drain_stats, 0)

    def drain_weights(index, unused):
        @pl.when(section != lax.div(index, 2))
        def _():
            wait_for(weights.at[index, part], pass_send.at[index])
        return 0

    lax.fori_loop(0, 2 * blocks, drain_weights, 0)

    def drain_grads(k, unused):
        block, diagonal, helper = roles(k)
        own_tiles = section_part.at[k, 0]
        column = whole.at[k, :, :, 0]
        wait_for(core_part.at[k], grad_send.at[0, k])

        @pl.when(section == diagonal)
        def _():
            wait_for(own_tiles.at[pl.ds(0, 4)], grad_send.at[1, k])

        @pl.when(section == helper)
        def _():
            wait_for(own_tiles.at[pl.ds(0, 2)], grad_send.at[1, k])
            wait_for(column_part(k, 2), grad_send.at[2, k])
            wait_for(column.at[:, :, pl.ds(0, 32)], grad_send.at[3, k])

        @pl.when((section != helper) & (section != diagonal))
        def _():
            wait_for(own_tiles.at[pl.ds(0, 3)], grad_send.at[1, k])
            wait_for(column_part(k, 1), grad_send.at[2, k])

            @pl.when(section != block)
            def _():
                wait_for(column.at[:, :, pl.ds(0, 16)], grad_send.at[3, k])

        @pl.when(section == block)
        def _():
            wait_for(column, grad_send.at[4, k])

        if groups > 1:
            @pl.when(section != diagonal)
            def _():
                wait_for(group_part.at[k, 0, pl.ds(0, groups - 1)], group_send.at[0, k])

            @pl.when(section == helper)
            def _():
                wait_for(group_part.at[k, 1, pl.ds(0, groups - 1)], group_send.at[1, k])
        return 0

    lax.fori_loop(1, stages, drain_grads, 0)
    wait_for(core_part.at[0], grad_send.at[0, 0])
    wait_for(section_part.at[0, 0, pl.ds(0, sections - 1)], grad_send.at[1, 0])
    wait_for(column_part(0, 1), grad_send.at[2, 0])
    if groups > 1:
        wait_for(group_part.at[0, 0, pl.ds(0, groups - 1)], group_send.at[0, 0])
    wait_for(whole.at[0, :, :, 0, pl.ds(0, 16 * (sections - 1))], grad_send.at[3, 0])
    wait_for(whole.at[0, :, :, 0], grad_send.at[4, 0])
    wait_for(flat_core, grad_send.at[0, extra])
    wait_for(flat_section.at[pl.ds(0, sections - 1)], grad_send.at[1, extra])
    wait_for(flat_whole.at[0, 0, pl.ds(0, 48 * (chips - 1)), pl.ds(0, half)], grad_send.at[2, extra])
    wait_for(flat_whole.at[:, 0, pl.ds(0, 48 * (sections - 1))], grad_send.at[3, extra])
    wait_for(flat_whole.at[:, 0], grad_send.at[4, extra])
    if groups > 1:
        wait_for(flat_group.at[0, 0, pl.ds(0, groups - 1)], group_send.at[0, extra])
    first_copy.wait()
    second_copy.wait()
    unite_done.wait()
    camera_done.wait()


def widen(cam, *refs):
    held_in, outs, narrow, full = refs[0:9], refs[9:22], refs[22:31], refs[31:34]
    in_sem, out_sem, plain_sem = refs[34:37]
    loads = [pltpu.make_async_copy(a, b, in_sem.at[n]) for n, (a, b) in enumerate(zip(held_in, narrow))]
    for load in loads:
        load.start()
    passed = []
    channels = full[1].shape[-1]

    def store(number, tap):
        return pltpu.make_async_copy(full[number].at[tap], outs[10 + number].at[tap], out_sem.at[number, tap])

    loads[0].wait()
    loads[1].wait()

    def unite_tap(tap, unused):
        full[0][tap, 0:channels] = narrow[0][tap].astype(f32)
        rows = pl.ds(pl.multiple_of(cam * tap, 16), cam)
        full[0][tap, channels : channels + cam] = narrow[1][rows].astype(f32)
        store(0, tap).start()
        return 0

    lax.fori_loop(0, 9, unite_tap, 0)
    for number in (1, 2):
        loads[number + 1].wait()

        def block_tap(tap, unused):
            full[number][tap] = narrow[number + 1][tap].astype(f32)
            store(number, tap).start()
            return 0

        lax.fori_loop(0, 9, block_tap, 0)
    for number in range(4, 9):
        loads[number].wait()
    for number in range(10):
        source = narrow[4 + number] if number < 4 else narrow[8].at[number - 4]
        passed.append(pltpu.make_async_copy(source, outs[number], plain_sem.at[number]))
        passed[-1].start()
    for number in range(3):
        for tap in range(9):
            store(number, tap).wait()
    for copy in passed:
        copy.wait()


def body(
    lidar, context, depth_logits, cell_index, unite_weight, unite_gain, unite_bias, first_weight, second_weight,
    first_gain, first_bias, second_gain, second_bias, cotangent,
):
    peers = lax.axis_size("dp")
    sections = lax.axis_size("section")
    section = lax.axis_index("section")
    channels = cotangent.shape[-1]
    pixels, bins = depth_logits.shape[2:]
    cam = context.shape[-1]
    united_in = unite_weight.shape[1]
    blocks = sections
    stages = 2 * blocks + 1
    events = 2 * stages - 1
    groups = peers // (2 * chips)
    taken = 9 * channels

    vmem = pl.BlockSpec(memory_space=pltpu.VMEM)
    hbm = pl.BlockSpec(memory_space=pltpu.HBM)
    shape = jax.ShapeDtypeStruct
    dma = pltpu.SemaphoreType.DMA
    results = pl.pallas_call(
        functools.partial(kernel, peers, sections),
        out_shape=(
            shape((cells, channels), f32),
            shape((cells, channels), f32),
            shape((cam, pixels), f32),
            shape((bins, 1, pixels), f32),
            shape((9, 2, 2, 64, channels), bf16),
            shape((2, 2, flat_rows // 4, channels), bf16),
            shape((9, 2, 2, 64, channels), bf16),
            shape((9, 2, 2, 64, channels), bf16),
            shape((6, 1, channels), f32),
        ),
        in_specs=[hbm, vmem, vmem, vmem, hbm, vmem, vmem, hbm, hbm, vmem, vmem, vmem, vmem, hbm],
        out_specs=[vmem, vmem, vmem, vmem, hbm, hbm, hbm, hbm, vmem],
        scratch_shapes=[
            pltpu.VMEM((2 * blocks, taken, channels), bf16),
            pltpu.VMEM((9 * united_in, channels), bf16),
            pltpu.VMEM((blocks, 4, channels), f32),
            pltpu.VMEM((cells + 2 * side, 3 * wide), bf16),
            pltpu.VMEM((chips, cells + 2 * side, 3 * channels), bf16),
            pltpu.VMEM((chips, cells, channels), bf16),
            pltpu.VMEM((2 * blocks, chips, cells, channels), bf16),
            pltpu.VMEM((stages, chips, cells, channels), f32),
            pltpu.VMEM((stages + 1, 1, channels), f32),
            pltpu.VMEM((chips, cells, channels), f32),
            pltpu.VMEM((chips, cells, channels), bf16),
            pltpu.VMEM((chips, cells, channels), bf16),
            pltpu.VMEM((chips, cells, channels), bf16),
            pltpu.VMEM((chips, cells, half), bf16),
            pltpu.VMEM((events, 2, channels), f32),
            pltpu.VMEM((events, 2 * groups, 2, channels), f32),
            pltpu.VMEM((2, channels), f32),
            pltpu.VMEM((peers, 2, channels), f32),
            pltpu.VMEM((half, pixels), f32),
            pltpu.VMEM((half, pixels), f32),
            pltpu.VMEM((cells, pixels), bf16),
            pltpu.VMEM((stages, 9, 2, 64, half), bf16),
            pltpu.VMEM((stages, 9, 64, half), bf16),
            pltpu.VMEM((stages, 9, 64, half), bf16),
            pltpu.VMEM((stages, 2, sections, 9, 16, half), bf16),
            pltpu.VMEM((stages, 9, 2, 2, 64, channels), bf16),
            pltpu.VMEM((flat_rows, half), bf16),
            pltpu.VMEM((flat_rows // 4, half), bf16),
            pltpu.VMEM((flat_rows // 4, half), bf16),
            pltpu.VMEM((sections, 48, half), bf16),
            pltpu.VMEM((2, 2, flat_rows // 4, channels), bf16),
            pltpu.VMEM((sections, stages, 2, channels), f32),
            pltpu.VMEM((2, channels), f32),
            pltpu.VMEM((stages if groups > 1 else 1, 2, groups, 9, 16, half), bf16),
            pltpu.VMEM((1, 1, groups, 48, half), bf16),
            dma((9,)), dma, dma, dma((events,)), dma((events,)), dma((chips,)), dma((chips,)), dma((chips,)),
            dma((chips,)), dma((chips,)), dma((chips,)), dma((chips,)), dma((chips,)), dma((4,)),
            dma((2 * blocks,)), dma((2,)), dma((2 * blocks,)), dma((2 * blocks,)), dma, dma,
            dma((5, stages + 1)), dma((5, stages + 1)), dma, dma, dma((2, stages + 1)), dma((2, stages + 1)),
        ],
        compiler_params=pltpu.CompilerParams(
            collective_id=0, has_side_effects=True, vmem_limit_bytes=60 << 20
        ),
    )(
        lidar.reshape(cells, channels), context.reshape(pixels, cam).T, depth_logits.reshape(pixels, bins).T,
        jnp.transpose(cell_index, (0, 3, 1, 2)).reshape(bins, 1, pixels), unite_weight.reshape(-1, channels),
        unite_gain[None], unite_bias[None], first_weight.reshape(taken, channels),
        second_weight.reshape(taken, channels), first_gain, first_bias, second_gain, second_bias,
        cotangent.reshape(-1, cells, channels),
    )

    act, lidar_grad, context_grad, logit_grad, *small, unite_whole, first_whole, second_whole = pl.pallas_call(
        functools.partial(widen, cam),
        out_shape=(
            shape((cells, channels), f32),
            shape((cells, channels), f32),
            shape((cam, pixels), f32),
            shape((bins, 1, pixels), f32),
            *[shape((1, channels), f32)] * 6,
            shape((9, united_in, channels), f32),
            shape((9, channels, channels), f32),
            shape((9, channels, channels), f32),
        ),
        in_specs=[hbm] * 9,
        out_specs=[hbm] * 13,
        scratch_shapes=[
            pltpu.VMEM((9, channels, channels), bf16),
            pltpu.VMEM((flat_rows, channels), bf16),
            pltpu.VMEM((9, channels, channels), bf16),
            pltpu.VMEM((9, channels, channels), bf16),
            pltpu.VMEM((cells, channels), f32),
            pltpu.VMEM((cells, channels), f32),
            pltpu.VMEM((cam, pixels), f32),
            pltpu.VMEM((bins, 1, pixels), f32),
            pltpu.VMEM((6, 1, channels), f32),
            pltpu.VMEM((9, united_in, channels), f32),
            pltpu.VMEM((9, channels, channels), f32),
            pltpu.VMEM((9, channels, channels), f32),
            dma((9,)), dma((3, 9)), dma((10,)),
        ],
        compiler_params=pltpu.CompilerParams(vmem_limit_bytes=60 << 20),
    )(
        results[4].reshape(9, channels, channels), results[5].reshape(flat_rows, channels),
        results[6].reshape(9, channels, channels), results[7].reshape(9, channels, channels), *results[0:4], results[8],
    )
    return (
        act.reshape(lidar.shape),
        lidar_grad.reshape(lidar.shape),
        context_grad.T.reshape(context.shape),
        jnp.transpose(logit_grad.reshape(1, bins, 1, pixels), (0, 2, 3, 1)),
        unite_whole,
        small[0].reshape(channels),
        small[1].reshape(channels),
        first_whole.reshape(first_weight.shape),
        second_whole.reshape(second_weight.shape),
        *small[2:6],
    )


def solution(mesh):
    split, by_dp = P("section"), P("section", "dp")
    in_specs = (by_dp, by_dp, by_dp, by_dp, P(), P(), P(), split, split, split, split, split, split, P(None, "dp"))
    out_specs = (by_dp, by_dp, by_dp, by_dp, P(), P(), P(), split, split, split, split, split, split)
    return jax.shard_map(body, mesh=mesh, in_specs=in_specs, out_specs=out_specs, check_vma=False)
```

```python
import functools

import jax
import jax.numpy as jnp
from jax import lax
from jax.experimental import pallas as pl
from jax.experimental.pallas import tpu as pltpu
from jax.sharding import PartitionSpec as P

eps = 1e-05
f32, bf16 = jnp.float32, jnp.bfloat16
MESH = pl.DeviceIdType.MESH
side = 16
cells = side * side
wide = 384
chips = 4
half = 128
column_lag = 3
owner_lag = 8
flat_rows = 768
transposed_rhs = (((1,), (1,)), ((), ()))
transposed_lhs = (((0,), (0,)), ((), ()))


def silu_of_half(half_value):
    return half_value + half_value * jnp.tanh(half_value)


def twice_slope_of_half(half_value):
    bent = jnp.tanh(half_value)
    return 1.0 + bent + half_value * (1.0 - bent * bent)


def put_shifted(buffer, value, stride, offset=0):
    width = value.shape[1]
    split = value.reshape(side, 2, 8, width)
    row = lax.broadcasted_iota(jnp.int32, (1, 8, width), 1)
    down = pltpu.roll(split, 1, 2)
    up = pltpu.roll(split, 7, 2)
    before = jnp.stack([jnp.where(row == 0, 0.0, down[:, 0]), jnp.where(row == 0, down[:, 0], down[:, 1])], axis=1)
    after = jnp.stack([jnp.where(row == 7, up[:, 1], up[:, 0]), jnp.where(row == 7, 0.0, up[:, 1])], axis=1)
    for group, shifted in enumerate((before, split, after)):
        start = group * stride + offset
        buffer[side : side + cells, start : start + width] = shifted.reshape(cells, width).astype(bf16)


def total_of(terms):
    total = None
    for term in terms:
        total = term if total is None else total + term
    return total


def conv(buffer, weight):
    return total_of(
        jnp.dot(buffer[side * i : side * i + cells, :], weight(i), preferred_element_type=f32) for i in range(3)
    )


def conv_transposed(buffer, weight, width):
    return total_of(
        lax.dot_general(
            buffer[side * (2 - i) : side * (2 - i) + cells, width * (2 - j) : width * (3 - j)],
            weight(3 * i + j),
            transposed_rhs,
            preferred_element_type=f32,
        )
        for i in range(3)
        for j in range(3)
    )


plan = {
    "start": [("offer", 0, "near", 2), ("offer", 0, "near", 0), ("offer", 0, "near", 1)],
    "lift1": [("offer", 0, "far", 3), ("offer", 1, "near", 1)],
    "united": [("offer", 1, "near", 0), ("relay", 0, 0), ("offer", 0, "near", 3)],
    "united2": [("offer", 1, "near", 2), ("offer", 1, "far", 0)],
    "merged": [("offer", 0, "far", 0)],
    "entered1": [("offer", 0, "far", 1)],
    "entered3": [("relay", 0, 1), ("relay", 1, 0), ("offer", 1, "near", 3)],
    "entered2": [("relay", 2, 0), ("offer", 1, "far", 1), ("relay", 2, 1)],
    "entered": [("relay", 3, 0), ("offer", 0, "far", 2), ("arrive", 0, 0)],
    ("first", 0): [("relay", 1, 1), ("offer", 1, "far", 2), ("offer", 1, "far", 3), ("arrive", 1, 0), ("arrive", 0, 1)],
    ("second", 0): [("relay", 3, 1)],
    ("first", 1): [("arrive", 2, 0), ("arrive", 1, 1)],
    ("second", 1): [("arrive", 3, 0), ("arrive", 2, 1)],
    ("second", 2): [("arrive", 3, 1)],
}


def kernel(
    peers, sections,
    lidar_ref, context_ref, logit_ref, cell_ref, unite_ref, unite_gain, unite_bias, first_ref, second_ref,
    first_gain, first_bias, second_gain, second_bias, cotangent_ref,
    act_ref, lidar_grad, context_grad, logit_grad, unite_out, camera_out, first_out, second_out, small_out,
    weights, unite_weight, vectors, joined, shifted, current, kept, halves, scales, held, gathered, upstream,
    lidars, cameras, mine, slots, unite_mine, unite_slots, probability, places, histogram,
    partial, core_part, own_part, section_part, whole, flat, flat_core, flat_own, flat_section, flat_whole,
    totals, gains, group_part, flat_group,
    local_sem, unite_send, unite_recv, stat_send, stat_recv, raw_send, raw_recv, cot_send, cot_recv,
    lidar_send, lidar_recv, camera_send, camera_recv, weight_send, weight_recv, relay_send, pass_send, pass_recv,
    vector_send, vector_recv, grad_send, grad_recv, total_send, total_recv, group_send, group_recv,
):
    me = lax.axis_index("dp")
    section = lax.axis_index("section")
    core = lax.rem(me, 2)
    chip = lax.rem(lax.div(me, 2), chips)
    group = lax.div(me, 2 * chips)
    groups = peers // (2 * chips)
    blocks = sections
    stages = 2 * blocks + 1
    channels = vectors.shape[-1]
    bins = logit_ref.shape[0]
    cam = context_ref.shape[0]
    united_in = channels + cam
    taken = 9 * channels
    row_half = lax.div(chip, 2)
    lane_half = lax.rem(chip, 2)
    count = float(peers * cells)

    def at(other_section=None, other=None):
        return (section if other_section is None else other_section, me if other is None else other)

    def chip_peer(step):
        return group * (2 * chips) + lax.rem(chip + step, chips) * 2 + core

    sibling = me + 1 - 2 * core

    def remote(source, target, send, recv, device):
        return pltpu.make_async_remote_copy(
            src_ref=source, dst_ref=target, send_sem=send, recv_sem=recv, device_id=device, device_id_type=MESH
        )

    def wait_for(part, semaphore):
        pltpu.make_async_copy(part, part, semaphore).wait()

    barrier = pltpu.get_barrier_semaphore()
    for step in range(1, sections):
        pl.semaphore_signal(
            barrier, inc=1, device_id=at(other_section=lax.rem(section + step, sections)), device_id_type=MESH
        )

    def greet(step, unused):
        pl.semaphore_signal(barrier, inc=1, device_id=at(other=lax.rem(me + step, peers)), device_id_type=MESH)
        return 0

    lax.fori_loop(1, peers, greet, 0)

    unite_copy = pltpu.make_async_copy(unite_ref, unite_weight, local_sem.at[0])
    own_first = pltpu.make_async_copy(first_ref, weights.at[2 * section], local_sem.at[1])
    own_second = pltpu.make_async_copy(second_ref, weights.at[2 * section + 1], local_sem.at[2])
    own_cot = pltpu.make_async_copy(cotangent_ref.at[section], upstream.at[chip], local_sem.at[3])
    own_lidar = pltpu.make_async_copy(lidar_ref, lidars.at[chip], local_sem.at[4])
    own_lidar.start()
    unite_copy.start()
    own_first.start()
    own_second.start()
    own_cot.start()
    for number, part in enumerate((first_gain, first_bias, second_gain, second_bias)):
        vectors[section, number : number + 1] = part[...]
    joined[...] = jnp.zeros_like(joined)
    probability[...] = jnp.zeros_like(probability)
    places[...] = jnp.zeros_like(places)
    cameras[chip] = jnp.zeros((cells, half), bf16)
    pl.semaphore_wait(barrier, peers - 1 + sections - 1)

    beside = section + 1 - 2 * lax.rem(section, 2)
    across = lax.rem(section + 2, sections)
    near = beside + core * (across - beside)
    far = across + core * (beside - across)
    part_rows = taken // 2
    part = pl.ds(pl.multiple_of(core * part_rows, part_rows), part_rows)
    sources = (first_ref, second_ref)

    def offer(which, target, number):
        index = 2 * section + which
        remote(
            sources[which].at[part], weights.at[index, part], weight_send.at[number], weight_recv.at[index],
            at(other_section=target),
        ).start()

    def arrived(index):
        wait_for(weights.at[index, part], weight_recv.at[index])

    def pass_on(index):
        remote(
            weights.at[index, part], weights.at[index, part], pass_send.at[index], pass_recv.at[index],
            at(other=sibling),
        ).start()

    def relay(block, which):
        index = 2 * block + which

        @pl.when(near == block)
        def _():
            arrived(index)
            remote(
                weights.at[index, part], weights.at[index, part], relay_send.at[which], weight_recv.at[index],
                at(other_section=far),
            ).start()
            pass_on(index)

    def arrive(block, which):
        index = 2 * block + which

        @pl.when((section != block) & (near != block))
        def _():
            arrived(index)
            pass_on(index)

    def ready(block, which):
        index = 2 * block + which
        rest = pl.ds(pl.multiple_of((1 - core) * part_rows, part_rows), part_rows)

        @pl.when(section != block)
        def _():
            wait_for(weights.at[index, rest], pass_recv.at[index])

        @pl.when(section == block)
        def _():
            (own_second if which else own_first).wait()

    def act_on(entry):
        name, one, two = entry[0:3]
        if name == "relay":
            relay(one, two)
        elif name == "arrive":
            arrive(one, two)
        else:
            @pl.when(section == entry[3])
            def _():
                offer(one, near if two == "near" else far, 2 * one + (two == "far"))

    def point(name, block=None):
        for key, entries in plan.items():
            if isinstance(key, tuple) and key[0] == name:
                @pl.when(block == key[1])
                def _():
                    for entry in entries:
                        act_on(entry)
            elif key == name:
                for entry in entries:
                    act_on(entry)

    point("start")
    for step in range(1, sections):
        remote(
            vectors.at[section], vectors.at[section], vector_send, vector_recv,
            at(other_section=lax.rem(section + step, sections)),
        ).start()

    logits = logit_ref[...].astype(f32)
    raised = jnp.exp(logits - jnp.max(logits, axis=0, keepdims=True))
    probability[0:bins] = raised / jnp.sum(raised, axis=0, keepdims=True)
    address = lax.broadcasted_iota(jnp.int32, (cells, half), 0)

    def add_bin(number, total):
        place = cell_ref[number]
        places[pl.ds(number, 1)] = place.astype(f32)
        return total + jnp.where(place == address, probability[pl.ds(number, 1)], 0.0)

    counted = jnp.zeros((cells, half), f32)
    for number in range(3):
        counted = lax.fori_loop(bins * number // 3, bins * (number + 1) // 3, add_bin, counted)
        if number < 2:
            point(f"lift{number + 1}")
    counted = counted.astype(bf16)
    histogram[...] = counted
    pooled = lax.dot_general(counted, context_ref[...], transposed_rhs, preferred_element_type=f32)
    cameras[chip, :, 0:cam] = pooled.astype(bf16)

    own_lidar.wait()
    put_shifted(joined, lidars[chip].astype(f32), wide)
    put_shifted(joined, pooled, wide, channels)
    unite_copy.wait()
    united = total_of(
        jnp.dot(
            joined[side * i : side * i + cells, wide * j : wide * j + united_in],
            unite_weight[united_in * (3 * i + j) : united_in * (3 * i + j + 1), :],
            preferred_element_type=f32,
        )
        for i in range(3)
        for j in range(3)
    )
    gathered[chip] = united.astype(bf16)
    for step in range(1, chips):
        remote(
            gathered.at[chip], gathered.at[chip], raw_send.at[step], raw_recv.at[step], at(other=chip_peer(step))
        ).start()
    center = jnp.sum(united, axis=0, keepdims=True) * (1.0 / cells)
    offsets = united - center
    unite_mine[0:1] = center
    unite_mine[1:2] = jnp.sum(offsets * offsets, axis=0, keepdims=True)
    unite_slots[me] = unite_mine[...]

    def send_unite(step, unused):
        remote(
            unite_mine, unite_slots.at[me], unite_send, unite_recv, at(other=lax.rem(me + step, peers))
        ).start()
        return 0

    lax.fori_loop(1, peers, send_unite, 0)

    point("united")
    shifted[...] = jnp.zeros_like(shifted)
    flat[9 * cam :, :] = jnp.zeros((flat_rows - 9 * cam, half), bf16)

    def merged(centers, squares, each):
        parts = centers.shape[0]
        center = jnp.sum(centers, axis=0, keepdims=True) * (1.0 / parts)
        apart = centers - center
        square = jnp.sum(squares, axis=0, keepdims=True) + each * jnp.sum(apart * apart, axis=0, keepdims=True)
        return center, square

    point("united2")
    wait_for(unite_slots.at[pl.ds(0, peers - 1)], unite_recv)
    center, square = merged(unite_slots[:, 0, :], unite_slots[:, 1, :], cells)
    scales[0] = lax.rsqrt(square * (1.0 / count) + eps)
    scales[stages] = center
    point("merged")

    def half_affine(center, scale, gain, bias):
        factor = 0.5 * gain * scale
        return factor, 0.5 * bias - center * factor

    factor, offset = half_affine(scales[stages], scales[0], unite_gain[...], unite_bias[...])

    def enter(number):
        value = gathered[number].astype(f32) * factor + offset
        halves[0, number] = value
        entering = silu_of_half(value)
        current[number] = entering.astype(bf16)
        kept[0, number] = entering.astype(bf16)
        put_shifted(shifted.at[number], entering, channels)

    enter(chip)
    for step in (1, 3, 2):
        wait_for(gathered.at[0], raw_recv.at[step])
        enter(lax.rem(chip - step + chips, chips))
        point(f"entered{step}")

    own_cot.wait()
    for step in range(1, chips):
        peer = at(other=chip_peer(step))
        remote(upstream.at[chip], upstream.at[chip], cot_send.at[step], cot_recv.at[step], peer).start()
    for step in range(1, chips):
        peer = at(other=chip_peer(step))
        remote(lidars.at[chip], lidars.at[chip], lidar_send.at[step], lidar_recv.at[step], peer).start()
        remote(cameras.at[chip], cameras.at[chip], camera_send.at[step], camera_recv.at[step], peer).start()

    point("entered")
    wait_for(vectors.at[pl.ds(0, sections - 1)], vector_recv)

    members = 2 * groups
    place = group * 2 + core

    def copy_stats(event, step):
        to = lax.rem(place + step, members)
        return remote(
            mine.at[event], slots.at[event, place], stat_send.at[event], stat_recv.at[event],
            at(other=lax.div(to, 2) * (2 * chips) + chip * 2 + lax.rem(to, 2)),
        )

    def send_stats(event, first, second):
        mine[event, 0:1] = first
        mine[event, 1:2] = second
        slots[event, place] = mine[event]
        for step in range(1, members):
            copy_stats(event, step).start()

    def take_stats(event):
        wait_for(slots.at[event, pl.ds(0, members - 1)], stat_recv.at[event])
        return slots[event, :, 0, :], slots[event, :, 1, :]

    def local_sums(parts):
        centers, squares = zip(*parts)
        return merged(jnp.concatenate(centers, axis=0), jnp.concatenate(squares, axis=0), cells)

    def start_conv(number, index):
        activ = conv(shifted.at[number], lambda i: weights[index, 3 * channels * i : 3 * channels * (i + 1), :])
        held[number] = activ
        center = jnp.sum(activ, axis=0, keepdims=True) * (1.0 / cells)
        offsets = activ - center
        return center, jnp.sum(offsets * offsets, axis=0, keepdims=True)

    def whole_sums(stage):
        centers, squares = take_stats(stage - 1)
        center, square = merged(centers, squares, chips * cells)
        scale = lax.rsqrt(square * (1.0 / count) + eps)
        scales[stage] = scale
        return center, scale

    def block(s, last):
        stage = 2 * s + 1

        def vector(number):
            return vectors[s, number : number + 1]

        point("first", s)
        ready(s, 1)
        factor, offset = half_affine(*whole_sums(stage), vector(0), vector(1))
        parts = []
        for number in range(chips):
            value = held[number] * factor + offset
            halves[stage, number] = value
            hidden = silu_of_half(value)
            kept[stage, number] = hidden.astype(bf16)
            put_shifted(shifted.at[number], hidden, channels)
            parts.append(start_conv(number, 2 * s + 1))
        send_stats(stage, *local_sums(parts))
        point("second", s)
        if not last:
            ready(s + 1, 0)
        factor, offset = half_affine(*whole_sums(stage + 1), vector(2), vector(3))
        parts = []
        for number in range(chips):
            value = held[number] * factor + offset
            halves[stage + 1, number] = value
            output = current[number].astype(f32) + silu_of_half(value)
            if last:
                held[number] = output
            else:
                current[number] = output.astype(bf16)
                kept[stage + 1, number] = output.astype(bf16)
                put_shifted(shifted.at[number], output, channels)
                parts.append(start_conv(number, 2 * s + 2))
        if not last:
            send_stats(stage + 1, *local_sums(parts))

    def block_step(s, unused):
        block(s, False)
        return 0

    ready(0, 0)
    send_stats(0, *local_sums([start_conv(number, 0) for number in range(chips)]))
    lax.fori_loop(0, blocks - 1, block_step, 0)
    block(blocks - 1, True)
    act_ref[...] = held[chip]

    lanes = pl.ds(pl.multiple_of(lane_half * half, half), half)
    flat48 = pl.ds(pl.multiple_of(section * 48, 16), 48)

    def lateral(j):
        return pl.ds(pl.multiple_of(channels * (2 - j) + lane_half * half, half), half)

    def weight_grad(stage, inputs):
        columns = pl.ds(pl.multiple_of(row_half * half, half), half)
        values = [inputs[number, :, columns] for number in range(chips)]
        for i in range(3):
            for j in range(3):
                taps = total_of(
                    lax.dot_general(
                        values[number],
                        shifted[number, side * (2 - i) : side * (2 - i) + cells, lateral(j)],
                        transposed_lhs,
                        preferred_element_type=f32,
                    )
                    for number in range(chips)
                ).astype(bf16)
                partial[stage, 3 * i + j, 0] = taps[0:64]
                partial[stage, 3 * i + j, 1] = taps[64:128]
        to_sibling(stage)

    def to_sibling(k):
        remote(
            partial.at[k, :, 1 - core], core_part.at[k], grad_send.at[0, k], grad_recv.at[0, k], at(other=sibling)
        ).start()

    def block_of(k):
        return lax.div(k - 1, 2)

    def roles(k):
        block = block_of(k)
        across_x = block + 1 - 2 * lax.rem(block, 2)
        across_y = lax.rem(block + 2, sections)
        return block, sections - 1 - block, across_x + core * (across_y - across_x)

    def tile(index):
        return pl.ds(pl.multiple_of(index * 16, 16), 16)

    def sum_cores(k):
        wait_for(core_part.at[k], grad_recv.at[0, k])
        for tap in range(9):
            own_part[k, tap] = (partial[k, tap, core].astype(f32) + core_part[k, tap].astype(f32)).astype(bf16)

    def send_tile(k, index, slot, other):
        remote(
            own_part.at[k, :, tile(index)], section_part.at[k, slot, section], grad_send.at[1, k], grad_recv.at[1, k],
            at(other_section=other),
        ).start()

    def to_sections(k):
        sum_cores(k)
        block, diagonal, helper = roles(k)
        for step in range(1, sections):
            other = lax.rem(section + step, sections)

            @pl.when(other != diagonal)
            def _():
                send_tile(k, other, 0, other)

            @pl.when(other == helper)
            def _():
                send_tile(k, diagonal, 1, other)

        section_part[k, 0, section] = own_part[k, :, tile(section)]

        @pl.when(section == helper)
        def _():
            section_part[k, 1, section] = own_part[k, :, tile(diagonal)]

    def over_groups(slot, k, value, buffer, number):
        if groups == 1:
            return value
        mine_here = buffer.at[k, slot, group]
        mine_here[...] = value
        for step in range(1, groups):
            to = lax.rem(group + step, groups) * (2 * chips) + chip * 2 + core
            remote(
                mine_here, mine_here, group_send.at[slot, number], group_recv.at[slot, number], at(other=to)
            ).start()
        wait_for(buffer.at[k, slot, pl.ds(0, groups - 1)], group_recv.at[slot, number])
        return jnp.sum(buffer[k, slot].astype(f32), axis=0).astype(bf16)

    def reduce_tile(k, slot, index):
        piece = total_of(section_part[k, slot, number].astype(f32) for number in range(sections)).astype(bf16)
        place = whole.at[k, :, row_half, core, tile(index), lanes]
        place[...] = over_groups(slot, k, piece, group_part, k)
        for step in range(1, chips):
            remote(place, place, grad_send.at[2, k], grad_recv.at[2, k], at(other=chip_peer(step))).start()

    def to_column(k):
        block, diagonal, helper = roles(k)

        @pl.when(section == helper)
        def _():
            wait_for(section_part.at[k, :, pl.ds(0, sections - 1)], grad_recv.at[1, k])
            reduce_tile(k, 0, section)
            reduce_tile(k, 1, diagonal)

        @pl.when((section != helper) & (section != diagonal))
        def _():
            wait_for(section_part.at[k, 0, pl.ds(0, sections - 1)], grad_recv.at[1, k])
            reduce_tile(k, 0, section)

    def column_part(k, tiles):
        return whole.at[k, :, 0, 0, pl.ds(0, 16 * (chips - 1)), pl.ds(0, half * tiles)]

    def hand_over(k, index, block):
        place = whole.at[k, :, :, core, tile(index)]
        remote(place, place, grad_send.at[3, k], grad_recv.at[3, k], at(other_section=block)).start()

    def to_owner(k):
        block, diagonal, helper = roles(k)

        @pl.when(section == helper)
        def _():
            wait_for(column_part(k, 2), grad_recv.at[2, k])
            hand_over(k, section, block)
            hand_over(k, diagonal, block)

        @pl.when((section != helper) & (section != diagonal))
        def _():
            wait_for(column_part(k, 1), grad_recv.at[2, k])

            @pl.when(section != block)
            def _():
                hand_over(k, section, block)

    def to_sections_all(k):
        sum_cores(k)
        section_part[k, 0, section] = own_part[k, :, tile(section)]
        for step in range(1, sections):
            other = lax.rem(section + step, sections)
            send_tile(k, other, 0, other)

    def to_column_all(k):
        wait_for(section_part.at[k, 0, pl.ds(0, sections - 1)], grad_recv.at[1, k])
        reduce_tile(k, 0, section)

    def to_all(k):
        wait_for(column_part(k, 1), grad_recv.at[2, k])
        place = whole.at[k, :, :, core, tile(section)]
        for step in range(1, sections):
            other = lax.rem(section + step, sections)
            remote(place, place, grad_send.at[3, k], grad_recv.at[3, k], at(other_section=other)).start()

    def share(k):
        wait_for(whole.at[k, :, :, 0, pl.ds(0, 16 * (sections - 1))], grad_recv.at[3, k])
        place = whole.at[k, :, :, core]
        remote(place, place, grad_send.at[4, k], grad_recv.at[4, k], at(other=sibling)).start()

    def owner_share(k):
        @pl.when(section == block_of(k))
        def _():
            share(k)

    def shared(k):
        wait_for(whole.at[k, :, :, 0], grad_recv.at[4, k])

    def backwards(first, last, act):
        def step(number, unused):
            act(first - number)
            return 0

        lax.fori_loop(0, first - last + 1, step, 0)

    def when_due(k, act):
        @pl.when(k <= stages - 1)
        def _():
            act(k)

    def start_norm(stage, number, grads):
        value = halves[stage, number]
        grads = grads * twice_slope_of_half(value)
        held[number] = grads
        return jnp.sum(grads, axis=0, keepdims=True), jnp.sum(grads * value, axis=0, keepdims=True)

    def send_sums(stage, parts, gain, bias):
        firsts, seconds = zip(*parts)
        first = 0.5 * total_of(firsts)
        send_stats(stages - 1 + stage, first, (total_of(seconds) - bias * first) / gain)

    def norm_factors(stage, gain, bias):
        first, second = take_stats(stages - 1 + stage)
        first = jnp.sum(first, axis=0, keepdims=True)
        second = jnp.sum(second, axis=0, keepdims=True)
        totals[section, stage, 0:1] = first
        totals[section, stage, 1:2] = second
        first = first * (1.0 / count)
        second = second * (1.0 / count)
        scale = scales[stage]
        return 0.5 * gain * scale, 2.0 * scale * second, scale * (gain * first - bias * second)

    def end_norm(stage, number, factors):
        by_grads, by_halves, constant = factors
        put_shifted(
            shifted.at[number], held[number] * by_grads - halves[stage, number] * by_halves - constant, channels
        )

    def passed(number, index):
        return conv_transposed(
            shifted.at[number], lambda tap: weights[index, channels * tap : channels * (tap + 1), :], channels
        )

    def during(stage):
        when_due(stage + 2, to_sections)
        weight_grad(stage + 1, kept.at[stage])
        when_due(stage + column_lag, to_column)
        when_due(stage + owner_lag, to_owner)

    for step in range(1, chips):
        wait_for(upstream.at[0], cot_recv.at[step])
        wait_for(upstream.at[0], cot_send.at[step])
    def take_gains(s):
        @pl.when(s > 0)
        def _():
            gains[0:1] = vectors[jnp.maximum(s - 1, 0), 2:3]
            gains[1:2] = vectors[jnp.maximum(s - 1, 0), 3:4]

        @pl.when(s == 0)
        def _():
            gains[0:1] = unite_gain[...]
            gains[1:2] = unite_bias[...]

    take_gains(blocks)
    send_sums(
        stages - 1,
        [
            start_norm(stages - 1, number, upstream[number].astype(f32))
            for number in range(chips)
        ],
        gains[0:1], gains[1:2],
    )

    def block_back(back, unused):
        s = blocks - 1 - back
        stage = 2 * s + 1

        def vector(number):
            return vectors[s, number : number + 1]

        @pl.when(back > 0)
        def _():
            during(stage + 1)

        factors = norm_factors(stage + 1, vector(2), vector(3))
        parts = []
        for number in range(chips):
            end_norm(stage + 1, number, factors)
            parts.append(start_norm(stage, number, passed(number, 2 * s + 1)))
        send_sums(stage, parts, vector(0), vector(1))
        during(stage)
        take_gains(s)
        factors = norm_factors(stage, vector(0), vector(1))
        parts = []
        for number in range(chips):
            end_norm(stage, number, factors)
            grads = (upstream[number].astype(f32) + passed(number, 2 * s)).astype(bf16)
            upstream[number] = grads
            parts.append(start_norm(stage - 1, number, grads.astype(f32)))
        send_sums(stage - 1, parts, gains[0:1], gains[1:2])
        return 0

    lax.fori_loop(0, blocks, block_back, 0)

    during(0)
    for step in range(1, chips):
        wait_for(lidars.at[0], lidar_recv.at[step])
        wait_for(cameras.at[0], camera_recv.at[step])
    factors = norm_factors(0, unite_gain[...], unite_bias[...])
    for number in range(chips):
        end_norm(0, number, factors)
    weight_grad(0, lidars)
    to_sections(1)
    held_cameras = [cameras[number] for number in range(chips)]
    for i in range(3):
        for j in range(3):
            taps = total_of(
                lax.dot_general(
                    held_cameras[number],
                    shifted[number, side * (2 - i) : side * (2 - i) + cells, lateral(j)],
                    transposed_lhs,
                    preferred_element_type=f32,
                )
                for number in range(chips)
            ).astype(bf16)
            flat[cam * (3 * i + j) : cam * (3 * i + j + 1)] = taps[0:cam]
    quarter = flat_rows // 4
    kept_rows = pl.ds(pl.multiple_of(row_half * (2 * quarter) + core * quarter, 16), quarter)
    sent_rows = pl.ds(pl.multiple_of(row_half * (2 * quarter) + (1 - core) * quarter, 16), quarter)
    extra = stages
    remote(
        flat.at[sent_rows], flat_core, grad_send.at[0, extra], grad_recv.at[0, extra], at(other=sibling)
    ).start()
    to_sections_all(0)
    backwards(min(column_lag - 1, stages - 1), 2, to_column)
    for step in range(1, sections):
        remote(
            totals.at[section], totals.at[section], total_send, total_recv,
            at(other_section=lax.rem(section + step, sections)),
        ).start()
    own = shifted.at[chip]
    pooled_grad = conv_transposed(
        own, lambda tap: unite_weight[united_in * tap + channels : united_in * (tap + 1), :], channels
    ).astype(bf16)

    wait_for(flat_core, grad_recv.at[0, extra])
    flat_own[...] = (flat[kept_rows].astype(f32) + flat_core[...].astype(f32)).astype(bf16)
    flat_section[section] = flat_own[flat48]
    for step in range(1, sections):
        other = lax.rem(section + step, sections)
        remote(
            flat_own.at[pl.ds(pl.multiple_of(other * 48, 16), 48)], flat_section.at[section],
            grad_send.at[1, extra], grad_recv.at[1, extra], at(other_section=other),
        ).start()
    lidar_grad[...] = conv_transposed(
        own, lambda tap: unite_weight[united_in * tap : united_in * tap + channels, :], channels
    )
    to_column(1)

    context_grad[...] = lax.dot_general(pooled_grad, histogram[...], transposed_lhs, preferred_element_type=f32)
    table = lax.dot_general(
        context_ref[...], pooled_grad, (((0,), (1,)), ((), ())), preferred_element_type=f32
    )
    wanted = places[...].T.astype(jnp.int32)
    within = lax.rem(wanted, half)
    low = jnp.take_along_axis(table[:, 0:half], within, axis=1)
    high = jnp.take_along_axis(table[:, half : 2 * half], within, axis=1)
    chance_grad = jnp.where(wanted < half, low, high).T
    chance = probability[...]
    places[...] = chance * (chance_grad - jnp.sum(chance_grad * chance, axis=0, keepdims=True))

    def store_bin(number, unused):
        logit_grad[number] = places[pl.ds(number, 1)]
        return 0

    lax.fori_loop(0, bins, store_bin, 0)

    to_column_all(0)
    wait_for(flat_section.at[pl.ds(0, sections - 1)], grad_recv.at[1, extra])
    piece = total_of(flat_section[number].astype(f32) for number in range(sections)).astype(bf16)
    flat_place = flat_whole.at[row_half, core, flat48, lanes]
    flat_place[...] = over_groups(0, 0, piece, flat_group, extra)
    for step in range(1, chips):
        remote(
            flat_place, flat_place, grad_send.at[2, extra], grad_recv.at[2, extra], at(other=chip_peer(step))
        ).start()
    backwards(min(owner_lag - 1, stages - 1), 1, to_owner)
    to_all(0)
    wait_for(flat_whole.at[0, 0, pl.ds(0, 48 * (chips - 1)), pl.ds(0, half)], grad_recv.at[2, extra])
    flat_rows_place = flat_whole.at[:, core, flat48]
    for step in range(1, sections):
        other = lax.rem(section + step, sections)
        remote(
            flat_rows_place, flat_rows_place, grad_send.at[3, extra], grad_recv.at[3, extra],
            at(other_section=other),
        ).start()

    backwards(stages - 1, 1, owner_share)
    share(0)
    wait_for(flat_whole.at[:, 0, pl.ds(0, 48 * (sections - 1))], grad_recv.at[3, extra])
    flat_half = flat_whole.at[:, core]
    remote(flat_half, flat_half, grad_send.at[4, extra], grad_recv.at[4, extra], at(other=sibling)).start()

    wait_for(totals.at[pl.ds(0, sections - 1)], total_recv)
    def summed(stage, row):
        return total_of(totals[number, stage, row : row + 1] for number in range(sections))

    small_out[0] = summed(0, 1)
    small_out[1] = summed(0, 0)
    for number in range(2):
        small_out[2 + 2 * number] = summed(2 * section + 1 + number, 1)
        small_out[3 + 2 * number] = summed(2 * section + 1 + number, 0)
    shared(2 * section + 1)
    shared(2 * section + 2)
    first_copy = pltpu.make_async_copy(whole.at[2 * section + 1], first_out, local_sem.at[5])
    second_copy = pltpu.make_async_copy(whole.at[2 * section + 2], second_out, local_sem.at[6])
    first_copy.start()
    second_copy.start()
    shared(0)
    unite_done = pltpu.make_async_copy(whole.at[0], unite_out, local_sem.at[7])
    unite_done.start()
    wait_for(flat_whole.at[:, 0], grad_recv.at[4, extra])
    camera_done = pltpu.make_async_copy(flat_whole, camera_out, local_sem.at[8])
    camera_done.start()

    wait_for(unite_slots.at[pl.ds(0, peers - 1)], unite_send)
    for step in range(1, chips):
        wait_for(gathered.at[0], raw_send.at[step])
        wait_for(lidars.at[0], lidar_send.at[step])
        wait_for(cameras.at[0], camera_send.at[step])
    for number in range(4):
        wait_for(weights.at[0, part], weight_send.at[number])
    for number in range(2):
        wait_for(weights.at[0, part], relay_send.at[number])
    wait_for(vectors.at[pl.ds(0, sections - 1)], vector_send)
    wait_for(totals.at[pl.ds(0, sections - 1)], total_send)

    def drain_stats(event, unused):
        wait_for(slots.at[event, pl.ds(0, members - 1)], stat_send.at[event])
        return 0

    lax.fori_loop(0, 2 * stages - 1, drain_stats, 0)

    def drain_weights(index, unused):
        @pl.when(section != lax.div(index, 2))
        def _():
            wait_for(weights.at[index, part], pass_send.at[index])
        return 0

    lax.fori_loop(0, 2 * blocks, drain_weights, 0)

    def drain_grads(k, unused):
        block, diagonal, helper = roles(k)
        own_tiles = section_part.at[k, 0]
        column = whole.at[k, :, :, 0]
        wait_for(core_part.at[k], grad_send.at[0, k])

        @pl.when(section == diagonal)
        def _():
            wait_for(own_tiles.at[pl.ds(0, 4)], grad_send.at[1, k])

        @pl.when(section == helper)
        def _():
            wait_for(own_tiles.at[pl.ds(0, 2)], grad_send.at[1, k])
            wait_for(column_part(k, 2), grad_send.at[2, k])
            wait_for(column.at[:, :, pl.ds(0, 32)], grad_send.at[3, k])

        @pl.when((section != helper) & (section != diagonal))
        def _():
            wait_for(own_tiles.at[pl.ds(0, 3)], grad_send.at[1, k])
            wait_for(column_part(k, 1), grad_send.at[2, k])

            @pl.when(section != block)
            def _():
                wait_for(column.at[:, :, pl.ds(0, 16)], grad_send.at[3, k])

        @pl.when(section == block)
        def _():
            wait_for(column, grad_send.at[4, k])

        if groups > 1:
            @pl.when(section != diagonal)
            def _():
                wait_for(group_part.at[k, 0, pl.ds(0, groups - 1)], group_send.at[0, k])

            @pl.when(section == helper)
            def _():
                wait_for(group_part.at[k, 1, pl.ds(0, groups - 1)], group_send.at[1, k])
        return 0

    lax.fori_loop(1, stages, drain_grads, 0)
    wait_for(core_part.at[0], grad_send.at[0, 0])
    wait_for(section_part.at[0, 0, pl.ds(0, sections - 1)], grad_send.at[1, 0])
    wait_for(column_part(0, 1), grad_send.at[2, 0])
    if groups > 1:
        wait_for(group_part.at[0, 0, pl.ds(0, groups - 1)], group_send.at[0, 0])
    wait_for(whole.at[0, :, :, 0, pl.ds(0, 16 * (sections - 1))], grad_send.at[3, 0])
    wait_for(whole.at[0, :, :, 0], grad_send.at[4, 0])
    wait_for(flat_core, grad_send.at[0, extra])
    wait_for(flat_section.at[pl.ds(0, sections - 1)], grad_send.at[1, extra])
    wait_for(flat_whole.at[0, 0, pl.ds(0, 48 * (chips - 1)), pl.ds(0, half)], grad_send.at[2, extra])
    wait_for(flat_whole.at[:, 0, pl.ds(0, 48 * (sections - 1))], grad_send.at[3, extra])
    wait_for(flat_whole.at[:, 0], grad_send.at[4, extra])
    if groups > 1:
        wait_for(flat_group.at[0, 0, pl.ds(0, groups - 1)], group_send.at[0, extra])
    first_copy.wait()
    second_copy.wait()
    unite_done.wait()
    camera_done.wait()


def widen(cam, *refs):
    held_in, outs, narrow, full = refs[0:9], refs[9:22], refs[22:31], refs[31:34]
    in_sem, out_sem, plain_sem = refs[34:37]
    loads = [pltpu.make_async_copy(a, b, in_sem.at[n]) for n, (a, b) in enumerate(zip(held_in, narrow))]
    for load in loads:
        load.start()
    passed = []
    channels = full[1].shape[-1]

    def store(number, tap):
        return pltpu.make_async_copy(full[number].at[tap], outs[10 + number].at[tap], out_sem.at[number, tap])

    loads[0].wait()
    loads[1].wait()

    def unite_tap(tap, unused):
        full[0][tap, 0:channels] = narrow[0][tap].astype(f32)
        rows = pl.ds(pl.multiple_of(cam * tap, 16), cam)
        full[0][tap, channels : channels + cam] = narrow[1][rows].astype(f32)
        store(0, tap).start()
        return 0

    lax.fori_loop(0, 9, unite_tap, 0)
    for number in (1, 2):
        loads[number + 1].wait()

        def block_tap(tap, unused):
            full[number][tap] = narrow[number + 1][tap].astype(f32)
            store(number, tap).start()
            return 0

        lax.fori_loop(0, 9, block_tap, 0)
    for number in range(4, 9):
        loads[number].wait()
    for number in range(10):
        source = narrow[4 + number] if number < 4 else narrow[8].at[number - 4]
        passed.append(pltpu.make_async_copy(source, outs[number], plain_sem.at[number]))
        passed[-1].start()
    for number in range(3):
        for tap in range(9):
            store(number, tap).wait()
    for copy in passed:
        copy.wait()


def body(
    lidar, context, depth_logits, cell_index, unite_weight, unite_gain, unite_bias, first_weight, second_weight,
    first_gain, first_bias, second_gain, second_bias, cotangent,
):
    peers = lax.axis_size("dp")
    sections = lax.axis_size("section")
    section = lax.axis_index("section")
    channels = cotangent.shape[-1]
    pixels, bins = depth_logits.shape[2:]
    cam = context.shape[-1]
    united_in = unite_weight.shape[1]
    blocks = sections
    stages = 2 * blocks + 1
    events = 2 * stages - 1
    groups = peers // (2 * chips)
    taken = 9 * channels

    vmem = pl.BlockSpec(memory_space=pltpu.VMEM)
    hbm = pl.BlockSpec(memory_space=pltpu.HBM)
    shape = jax.ShapeDtypeStruct
    dma = pltpu.SemaphoreType.DMA
    results = pl.pallas_call(
        functools.partial(kernel, peers, sections),
        out_shape=(
            shape((cells, channels), f32),
            shape((cells, channels), f32),
            shape((cam, pixels), f32),
            shape((bins, 1, pixels), f32),
            shape((9, 2, 2, 64, channels), bf16),
            shape((2, 2, flat_rows // 4, channels), bf16),
            shape((9, 2, 2, 64, channels), bf16),
            shape((9, 2, 2, 64, channels), bf16),
            shape((6, 1, channels), f32),
        ),
        in_specs=[hbm, vmem, vmem, vmem, hbm, vmem, vmem, hbm, hbm, vmem, vmem, vmem, vmem, hbm],
        out_specs=[vmem, vmem, vmem, vmem, hbm, hbm, hbm, hbm, vmem],
        scratch_shapes=[
            pltpu.VMEM((2 * blocks, taken, channels), bf16),
            pltpu.VMEM((9 * united_in, channels), bf16),
            pltpu.VMEM((blocks, 4, channels), f32),
            pltpu.VMEM((cells + 2 * side, 3 * wide), bf16),
            pltpu.VMEM((chips, cells + 2 * side, 3 * channels), bf16),
            pltpu.VMEM((chips, cells, channels), bf16),
            pltpu.VMEM((2 * blocks, chips, cells, channels), bf16),
            pltpu.VMEM((stages, chips, cells, channels), f32),
            pltpu.VMEM((stages + 1, 1, channels), f32),
            pltpu.VMEM((chips, cells, channels), f32),
            pltpu.VMEM((chips, cells, channels), bf16),
            pltpu.VMEM((chips, cells, channels), bf16),
            pltpu.VMEM((chips, cells, channels), bf16),
            pltpu.VMEM((chips, cells, half), bf16),
            pltpu.VMEM((events, 2, channels), f32),
            pltpu.VMEM((events, 2 * groups, 2, channels), f32),
            pltpu.VMEM((2, channels), f32),
            pltpu.VMEM((peers, 2, channels), f32),
            pltpu.VMEM((half, pixels), f32),
            pltpu.VMEM((half, pixels), f32),
            pltpu.VMEM((cells, pixels), bf16),
            pltpu.VMEM((stages, 9, 2, 64, half), bf16),
            pltpu.VMEM((stages, 9, 64, half), bf16),
            pltpu.VMEM((stages, 9, 64, half), bf16),
            pltpu.VMEM((stages, 2, sections, 9, 16, half), bf16),
            pltpu.VMEM((stages, 9, 2, 2, 64, channels), bf16),
            pltpu.VMEM((flat_rows, half), bf16),
            pltpu.VMEM((flat_rows // 4, half), bf16),
            pltpu.VMEM((flat_rows // 4, half), bf16),
            pltpu.VMEM((sections, 48, half), bf16),
            pltpu.VMEM((2, 2, flat_rows // 4, channels), bf16),
            pltpu.VMEM((sections, stages, 2, channels), f32),
            pltpu.VMEM((2, channels), f32),
            pltpu.VMEM((stages if groups > 1 else 1, 2, groups, 9, 16, half), bf16),
            pltpu.VMEM((1, 1, groups, 48, half), bf16),
            dma((9,)), dma, dma, dma((events,)), dma((events,)), dma((chips,)), dma((chips,)), dma((chips,)),
            dma((chips,)), dma((chips,)), dma((chips,)), dma((chips,)), dma((chips,)), dma((4,)),
            dma((2 * blocks,)), dma((2,)), dma((2 * blocks,)), dma((2 * blocks,)), dma, dma,
            dma((5, stages + 1)), dma((5, stages + 1)), dma, dma, dma((2, stages + 1)), dma((2, stages + 1)),
        ],
        compiler_params=pltpu.CompilerParams(
            collective_id=0, has_side_effects=True, vmem_limit_bytes=60 << 20
        ),
    )(
        lidar.reshape(cells, channels), context.reshape(pixels, cam).T, depth_logits.reshape(pixels, bins).T,
        jnp.transpose(cell_index, (0, 3, 1, 2)).reshape(bins, 1, pixels), unite_weight.reshape(-1, channels),
        unite_gain[None], unite_bias[None], first_weight.reshape(taken, channels),
        second_weight.reshape(taken, channels), first_gain, first_bias, second_gain, second_bias,
        cotangent.reshape(-1, cells, channels),
    )

    act, lidar_grad, context_grad, logit_grad, *small, unite_whole, first_whole, second_whole = pl.pallas_call(
        functools.partial(widen, cam),
        out_shape=(
            shape((cells, channels), f32),
            shape((cells, channels), f32),
            shape((cam, pixels), f32),
            shape((bins, 1, pixels), f32),
            *[shape((1, channels), f32)] * 6,
            shape((9, united_in, channels), f32),
            shape((9, channels, channels), f32),
            shape((9, channels, channels), f32),
        ),
        in_specs=[hbm] * 9,
        out_specs=[hbm] * 13,
        scratch_shapes=[
            pltpu.VMEM((9, channels, channels), bf16),
            pltpu.VMEM((flat_rows, channels), bf16),
            pltpu.VMEM((9, channels, channels), bf16),
            pltpu.VMEM((9, channels, channels), bf16),
            pltpu.VMEM((cells, channels), f32),
            pltpu.VMEM((cells, channels), f32),
            pltpu.VMEM((cam, pixels), f32),
            pltpu.VMEM((bins, 1, pixels), f32),
            pltpu.VMEM((6, 1, channels), f32),
            pltpu.VMEM((9, united_in, channels), f32),
            pltpu.VMEM((9, channels, channels), f32),
            pltpu.VMEM((9, channels, channels), f32),
            dma((9,)), dma((3, 9)), dma((10,)),
        ],
        compiler_params=pltpu.CompilerParams(vmem_limit_bytes=60 << 20),
    )(
        results[4].reshape(9, channels, channels), results[5].reshape(flat_rows, channels),
        results[6].reshape(9, channels, channels), results[7].reshape(9, channels, channels), *results[0:4], results[8],
    )
    return (
        act.reshape(lidar.shape),
        lidar_grad.reshape(lidar.shape),
        context_grad.T.reshape(context.shape),
        jnp.transpose(logit_grad.reshape(1, bins, 1, pixels), (0, 2, 3, 1)),
        unite_whole,
        small[0].reshape(channels),
        small[1].reshape(channels),
        first_whole.reshape(first_weight.shape),
        second_whole.reshape(second_weight.shape),
        *small[2:6],
    )


def solution(mesh):
    split, by_dp = P("section"), P("section", "dp")
    in_specs = (by_dp, by_dp, by_dp, by_dp, P(), P(), P(), split, split, split, split, split, split, P(None, "dp"))
    out_specs = (by_dp, by_dp, by_dp, by_dp, P(), P(), P(), split, split, split, split, split, split)
    return jax.shard_map(body, mesh=mesh, in_specs=in_specs, out_specs=out_specs, check_vma=False)
```

```python
import functools

import jax
import jax.numpy as jnp
from jax import lax
from jax.experimental import pallas as pl
from jax.experimental.pallas import tpu as pltpu
from jax.sharding import PartitionSpec as P

eps = 1e-05
f32, bf16 = jnp.float32, jnp.bfloat16
MESH = pl.DeviceIdType.MESH
side = 16
cells = side * side
wide = 384
chips = 4
half = 128
column_lag = 3
owner_lag = 8
flat_rows = 768
transposed_rhs = (((1,), (1,)), ((), ()))
transposed_lhs = (((0,), (0,)), ((), ()))


def silu_of_half(half_value):
    return half_value + half_value * jnp.tanh(half_value)


def twice_slope_of_half(half_value):
    bent = jnp.tanh(half_value)
    return 1.0 + bent + half_value * (1.0 - bent * bent)


def put_shifted(buffer, value, stride, offset=0):
    width = value.shape[1]
    split = value.reshape(side, 2, 8, width)
    row = lax.broadcasted_iota(jnp.int32, (1, 8, width), 1)
    down = pltpu.roll(split, 1, 2)
    up = pltpu.roll(split, 7, 2)
    before = jnp.stack([jnp.where(row == 0, 0.0, down[:, 0]), jnp.where(row == 0, down[:, 0], down[:, 1])], axis=1)
    after = jnp.stack([jnp.where(row == 7, up[:, 1], up[:, 0]), jnp.where(row == 7, 0.0, up[:, 1])], axis=1)
    for group, shifted in enumerate((before, split, after)):
        start = group * stride + offset
        buffer[side : side + cells, start : start + width] = shifted.reshape(cells, width).astype(bf16)


def total_of(terms):
    total = None
    for term in terms:
        total = term if total is None else total + term
    return total


def conv(buffer, weight):
    return total_of(
        jnp.dot(buffer[side * i : side * i + cells, :], weight(i), preferred_element_type=f32) for i in range(3)
    )


def conv_transposed(buffer, weight, width):
    return total_of(
        lax.dot_general(
            buffer[side * (2 - i) : side * (2 - i) + cells, width * (2 - j) : width * (3 - j)],
            weight(3 * i + j),
            transposed_rhs,
            preferred_element_type=f32,
        )
        for i in range(3)
        for j in range(3)
    )


plan = {
    "start": [("offer", 0, "near", 2), ("offer", 0, "near", 0), ("offer", 0, "near", 1)],
    "lift1": [("offer", 0, "far", 3), ("offer", 1, "near", 1)],
    "united": [("offer", 1, "near", 0), ("relay", 0, 0), ("offer", 0, "near", 3)],
    "united2": [("offer", 1, "near", 2), ("offer", 1, "far", 0)],
    "merged": [("offer", 0, "far", 0)],
    "entered1": [("offer", 0, "far", 1)],
    "entered3": [("relay", 0, 1), ("relay", 1, 0), ("offer", 1, "near", 3)],
    "entered2": [("relay", 2, 0), ("offer", 1, "far", 1), ("relay", 2, 1)],
    "entered": [("relay", 3, 0), ("offer", 0, "far", 2), ("arrive", 0, 0)],
    ("first", 0): [("relay", 1, 1), ("offer", 1, "far", 2), ("offer", 1, "far", 3), ("arrive", 1, 0), ("arrive", 0, 1)],
    ("second", 0): [("relay", 3, 1)],
    ("first", 1): [("arrive", 2, 0), ("arrive", 1, 1)],
    ("second", 1): [("arrive", 3, 0), ("arrive", 2, 1)],
    ("second", 2): [("arrive", 3, 1)],
}


def kernel(
    peers, sections,
    lidar_ref, context_ref, logit_ref, cell_ref, unite_ref, unite_gain, unite_bias, first_ref, second_ref,
    first_gain, first_bias, second_gain, second_bias, cotangent_ref,
    act_ref, lidar_grad, context_grad, logit_grad, unite_out, camera_out, first_out, second_out, small_out,
    weights, unite_weight, vectors, joined, shifted, current, kept, halves, scales, held, gathered, upstream,
    lidars, cameras, mine, slots, unite_mine, unite_slots, probability, places, histogram,
    partial, core_part, own_part, section_part, whole, flat, flat_core, flat_own, flat_section, flat_whole,
    totals, gains, group_part, flat_group,
    local_sem, unite_send, unite_recv, stat_send, stat_recv, raw_send, raw_recv, cot_send, cot_recv,
    lidar_send, lidar_recv, camera_send, camera_recv, weight_send, weight_recv, relay_send, pass_send, pass_recv,
    vector_send, vector_recv, grad_send, grad_recv, total_send, total_recv, group_send, group_recv,
):
    me = lax.axis_index("dp")
    section = lax.axis_index("section")
    core = lax.rem(me, 2)
    chip = lax.rem(lax.div(me, 2), chips)
    group = lax.div(me, 2 * chips)
    groups = peers // (2 * chips)
    blocks = sections
    stages = 2 * blocks + 1
    channels = vectors.shape[-1]
    bins = logit_ref.shape[0]
    cam = context_ref.shape[0]
    united_in = channels + cam
    taken = 9 * channels
    row_half = lax.div(chip, 2)
    lane_half = lax.rem(chip, 2)
    count = float(peers * cells)

    def at(other_section=None, other=None):
        return (section if other_section is None else other_section, me if other is None else other)

    def chip_peer(step):
        return group * (2 * chips) + lax.rem(chip + step, chips) * 2 + core

    sibling = me + 1 - 2 * core

    def remote(source, target, send, recv, device):
        return pltpu.make_async_remote_copy(
            src_ref=source, dst_ref=target, send_sem=send, recv_sem=recv, device_id=device, device_id_type=MESH
        )

    def wait_for(part, semaphore):
        pltpu.make_async_copy(part, part, semaphore).wait()

    barrier = pltpu.get_barrier_semaphore()
    for step in range(1, sections):
        pl.semaphore_signal(
            barrier, inc=1, device_id=at(other_section=lax.rem(section + step, sections)), device_id_type=MESH
        )

    def greet(step, unused):
        pl.semaphore_signal(barrier, inc=1, device_id=at(other=lax.rem(me + step, peers)), device_id_type=MESH)
        return 0

    lax.fori_loop(1, peers, greet, 0)

    unite_copy = pltpu.make_async_copy(unite_ref, unite_weight, local_sem.at[0])
    own_first = pltpu.make_async_copy(first_ref, weights.at[2 * section], local_sem.at[1])
    own_second = pltpu.make_async_copy(second_ref, weights.at[2 * section + 1], local_sem.at[2])
    own_cot = pltpu.make_async_copy(cotangent_ref.at[section], upstream.at[chip], local_sem.at[3])
    own_lidar = pltpu.make_async_copy(lidar_ref, lidars.at[chip], local_sem.at[4])
    own_lidar.start()
    unite_copy.start()
    own_first.start()
    own_second.start()
    own_cot.start()
    for number, part in enumerate((first_gain, first_bias, second_gain, second_bias)):
        vectors[section, number : number + 1] = part[...]
    joined[...] = jnp.zeros_like(joined)
    probability[...] = jnp.zeros_like(probability)
    places[...] = jnp.zeros_like(places)
    cameras[chip] = jnp.zeros((cells, half), bf16)
    pl.semaphore_wait(barrier, peers - 1 + sections - 1)

    beside = section + 1 - 2 * lax.rem(section, 2)
    across = lax.rem(section + 2, sections)
    near = beside + core * (across - beside)
    far = across + core * (beside - across)
    part_rows = taken // 2
    part = pl.ds(pl.multiple_of(core * part_rows, part_rows), part_rows)
    sources = (first_ref, second_ref)

    def offer(which, target, number):
        index = 2 * section + which
        remote(
            sources[which].at[part], weights.at[index, part], weight_send.at[number], weight_recv.at[index],
            at(other_section=target),
        ).start()

    def arrived(index):
        wait_for(weights.at[index, part], weight_recv.at[index])

    def pass_on(index):
        remote(
            weights.at[index, part], weights.at[index, part], pass_send.at[index], pass_recv.at[index],
            at(other=sibling),
        ).start()

    def relay(block, which):
        index = 2 * block + which

        @pl.when(near == block)
        def _():
            arrived(index)
            remote(
                weights.at[index, part], weights.at[index, part], relay_send.at[which], weight_recv.at[index],
                at(other_section=far),
            ).start()
            pass_on(index)

    def arrive(block, which):
        index = 2 * block + which

        @pl.when((section != block) & (near != block))
        def _():
            arrived(index)
            pass_on(index)

    def ready(block, which):
        index = 2 * block + which
        rest = pl.ds(pl.multiple_of((1 - core) * part_rows, part_rows), part_rows)

        @pl.when(section != block)
        def _():
            wait_for(weights.at[index, rest], pass_recv.at[index])

        @pl.when(section == block)
        def _():
            (own_second if which else own_first).wait()

    def act_on(entry):
        name, one, two = entry[0:3]
        if name == "relay":
            relay(one, two)
        elif name == "arrive":
            arrive(one, two)
        else:
            @pl.when(section == entry[3])
            def _():
                offer(one, near if two == "near" else far, 2 * one + (two == "far"))

    def point(name, block=None):
        for key, entries in plan.items():
            if isinstance(key, tuple) and key[0] == name:
                @pl.when(block == key[1])
                def _():
                    for entry in entries:
                        act_on(entry)
            elif key == name:
                for entry in entries:
                    act_on(entry)

    point("start")
    for step in range(1, sections):
        remote(
            vectors.at[section], vectors.at[section], vector_send, vector_recv,
            at(other_section=lax.rem(section + step, sections)),
        ).start()

    logits = logit_ref[...].astype(f32)
    raised = jnp.exp(logits - jnp.max(logits, axis=0, keepdims=True))
    probability[0:bins] = raised / jnp.sum(raised, axis=0, keepdims=True)
    address = lax.broadcasted_iota(jnp.int32, (cells, half), 0)

    def add_bin(number, total):
        place = cell_ref[number]
        places[pl.ds(number, 1)] = place.astype(f32)
        return total + jnp.where(place == address, probability[pl.ds(number, 1)], 0.0)

    counted = jnp.zeros((cells, half), f32)
    for number in range(3):
        counted = lax.fori_loop(bins * number // 3, bins * (number + 1) // 3, add_bin, counted)
        if number < 2:
            point(f"lift{number + 1}")
    counted = counted.astype(bf16)
    histogram[...] = counted
    pooled = lax.dot_general(counted, context_ref[...], transposed_rhs, preferred_element_type=f32)
    cameras[chip, :, 0:cam] = pooled.astype(bf16)

    own_lidar.wait()
    put_shifted(joined, lidars[chip].astype(f32), wide)
    put_shifted(joined, pooled, wide, channels)
    unite_copy.wait()
    united = total_of(
        jnp.dot(
            joined[side * i : side * i + cells, wide * j : wide * j + united_in],
            unite_weight[united_in * (3 * i + j) : united_in * (3 * i + j + 1), :],
            preferred_element_type=f32,
        )
        for i in range(3)
        for j in range(3)
    )
    gathered[chip] = united.astype(bf16)
    for step in range(1, chips):
        remote(
            gathered.at[chip], gathered.at[chip], raw_send.at[step], raw_recv.at[step], at(other=chip_peer(step))
        ).start()
    center = jnp.sum(united, axis=0, keepdims=True) * (1.0 / cells)
    offsets = united - center
    unite_mine[0:1] = center
    unite_mine[1:2] = jnp.sum(offsets * offsets, axis=0, keepdims=True)
    unite_slots[me] = unite_mine[...]

    def send_unite(step, unused):
        remote(
            unite_mine, unite_slots.at[me], unite_send, unite_recv, at(other=lax.rem(me + step, peers))
        ).start()
        return 0

    lax.fori_loop(1, peers, send_unite, 0)

    point("united")
    shifted[...] = jnp.zeros_like(shifted)
    flat[9 * cam :, :] = jnp.zeros((flat_rows - 9 * cam, half), bf16)

    def merged(centers, squares, each):
        parts = centers.shape[0]
        center = jnp.sum(centers, axis=0, keepdims=True) * (1.0 / parts)
        apart = centers - center
        square = jnp.sum(squares, axis=0, keepdims=True) + each * jnp.sum(apart * apart, axis=0, keepdims=True)
        return center, square

    point("united2")
    wait_for(unite_slots.at[pl.ds(0, peers - 1)], unite_recv)
    center, square = merged(unite_slots[:, 0, :], unite_slots[:, 1, :], cells)
    scales[0] = lax.rsqrt(square * (1.0 / count) + eps)
    scales[stages] = center
    point("merged")

    def half_affine(center, scale, gain, bias):
        factor = 0.5 * gain * scale
        return factor, 0.5 * bias - center * factor

    factor, offset = half_affine(scales[stages], scales[0], unite_gain[...], unite_bias[...])

    def enter(number):
        value = gathered[number].astype(f32) * factor + offset
        halves[0, number] = value
        entering = silu_of_half(value)
        current[number] = entering.astype(bf16)
        kept[0, number] = entering.astype(bf16)
        put_shifted(shifted.at[number], entering, channels)

    enter(chip)
    for step in (1, 3, 2):
        wait_for(gathered.at[0], raw_recv.at[step])
        enter(lax.rem(chip - step + chips, chips))
        point(f"entered{step}")

    own_cot.wait()
    for step in range(1, chips):
        peer = at(other=chip_peer(step))
        remote(upstream.at[chip], upstream.at[chip], cot_send.at[step], cot_recv.at[step], peer).start()
    for step in range(1, chips):
        peer = at(other=chip_peer(step))
        remote(lidars.at[chip], lidars.at[chip], lidar_send.at[step], lidar_recv.at[step], peer).start()
        remote(cameras.at[chip], cameras.at[chip], camera_send.at[step], camera_recv.at[step], peer).start()

    point("entered")
    wait_for(vectors.at[pl.ds(0, sections - 1)], vector_recv)

    members = 2 * groups
    place = group * 2 + core

    def copy_stats(event, step):
        to = lax.rem(place + step, members)
        return remote(
            mine.at[event], slots.at[event, place], stat_send.at[event], stat_recv.at[event],
            at(other=lax.div(to, 2) * (2 * chips) + chip * 2 + lax.rem(to, 2)),
        )

    def send_stats(event, first, second):
        mine[event, 0:1] = first
        mine[event, 1:2] = second
        slots[event, place] = mine[event]
        for step in range(1, members):
            copy_stats(event, step).start()

    def take_stats(event):
        wait_for(slots.at[event, pl.ds(0, members - 1)], stat_recv.at[event])
        return slots[event, :, 0, :], slots[event, :, 1, :]

    def local_sums(parts):
        centers, squares = zip(*parts)
        return merged(jnp.concatenate(centers, axis=0), jnp.concatenate(squares, axis=0), cells)

    def start_conv(number, index):
        activ = conv(shifted.at[number], lambda i: weights[index, 3 * channels * i : 3 * channels * (i + 1), :])
        held[number] = activ
        center = jnp.sum(activ, axis=0, keepdims=True) * (1.0 / cells)
        offsets = activ - center
        return center, jnp.sum(offsets * offsets, axis=0, keepdims=True)

    def whole_sums(stage):
        centers, squares = take_stats(stage - 1)
        center, square = merged(centers, squares, chips * cells)
        scale = lax.rsqrt(square * (1.0 / count) + eps)
        scales[stage] = scale
        return center, scale

    def block(s, last):
        stage = 2 * s + 1

        def vector(number):
            return vectors[s, number : number + 1]

        point("first", s)
        ready(s, 1)
        factor, offset = half_affine(*whole_sums(stage), vector(0), vector(1))
        parts = []
        for number in range(chips):
            value = held[number] * factor + offset
            halves[stage, number] = value
            hidden = silu_of_half(value)
            kept[stage, number] = hidden.astype(bf16)
            put_shifted(shifted.at[number], hidden, channels)
            parts.append(start_conv(number, 2 * s + 1))
        send_stats(stage, *local_sums(parts))
        point("second", s)
        if not last:
            ready(s + 1, 0)
        factor, offset = half_affine(*whole_sums(stage + 1), vector(2), vector(3))
        parts = []
        for number in range(chips):
            value = held[number] * factor + offset
            halves[stage + 1, number] = value
            output = current[number].astype(f32) + silu_of_half(value)
            if last:
                held[number] = output
            else:
                current[number] = output.astype(bf16)
                kept[stage + 1, number] = output.astype(bf16)
                put_shifted(shifted.at[number], output, channels)
                parts.append(start_conv(number, 2 * s + 2))
        if not last:
            send_stats(stage + 1, *local_sums(parts))

    def block_step(s, unused):
        block(s, False)
        return 0

    ready(0, 0)
    send_stats(0, *local_sums([start_conv(number, 0) for number in range(chips)]))
    lax.fori_loop(0, blocks - 1, block_step, 0)
    block(blocks - 1, True)
    act_ref[...] = held[chip]

    lanes = pl.ds(pl.multiple_of(lane_half * half, half), half)
    flat48 = pl.ds(pl.multiple_of(section * 48, 16), 48)

    def lateral(j):
        return pl.ds(pl.multiple_of(channels * (2 - j) + lane_half * half, half), half)

    def weight_grad(stage, inputs):
        columns = pl.ds(pl.multiple_of(row_half * half, half), half)
        values = [inputs[number, :, columns] for number in range(chips)]
        for i in range(3):
            for j in range(3):
                taps = total_of(
                    lax.dot_general(
                        values[number],
                        shifted[number, side * (2 - i) : side * (2 - i) + cells, lateral(j)],
                        transposed_lhs,
                        preferred_element_type=f32,
                    )
                    for number in range(chips)
                ).astype(bf16)
                partial[stage, 3 * i + j, 0] = taps[0:64]
                partial[stage, 3 * i + j, 1] = taps[64:128]
        to_sibling(stage)

    def to_sibling(k):
        remote(
            partial.at[k, :, 1 - core], core_part.at[k], grad_send.at[0, k], grad_recv.at[0, k], at(other=sibling)
        ).start()

    def block_of(k):
        return lax.div(k - 1, 2)

    def roles(k):
        block = block_of(k)
        across_x = block + 1 - 2 * lax.rem(block, 2)
        across_y = lax.rem(block + 2, sections)
        return block, sections - 1 - block, across_x + core * (across_y - across_x)

    def tile(index):
        return pl.ds(pl.multiple_of(index * 16, 16), 16)

    def sum_cores(k):
        wait_for(core_part.at[k], grad_recv.at[0, k])
        for tap in range(9):
            own_part[k, tap] = (partial[k, tap, core].astype(f32) + core_part[k, tap].astype(f32)).astype(bf16)

    def send_tile(k, index, slot, other):
        remote(
            own_part.at[k, :, tile(index)], section_part.at[k, slot, section], grad_send.at[1, k], grad_recv.at[1, k],
            at(other_section=other),
        ).start()

    def to_sections(k):
        sum_cores(k)
        block, diagonal, helper = roles(k)
        for step in range(1, sections):
            other = lax.rem(section + step, sections)

            @pl.when(other != diagonal)
            def _():
                send_tile(k, other, 0, other)

            @pl.when(other == helper)
            def _():
                send_tile(k, diagonal, 1, other)

        section_part[k, 0, section] = own_part[k, :, tile(section)]

        @pl.when(section == helper)
        def _():
            section_part[k, 1, section] = own_part[k, :, tile(diagonal)]

    def over_groups(slot, k, value, buffer, number):
        if groups == 1:
            return value
        mine_here = buffer.at[k, slot, group]
        mine_here[...] = value
        for step in range(1, groups):
            to = lax.rem(group + step, groups) * (2 * chips) + chip * 2 + core
            remote(
                mine_here, mine_here, group_send.at[slot, number], group_recv.at[slot, number], at(other=to)
            ).start()
        wait_for(buffer.at[k, slot, pl.ds(0, groups - 1)], group_recv.at[slot, number])
        return jnp.sum(buffer[k, slot].astype(f32), axis=0).astype(bf16)

    def reduce_tile(k, slot, index):
        piece = total_of(section_part[k, slot, number].astype(f32) for number in range(sections)).astype(bf16)
        place = whole.at[k, :, row_half, core, tile(index), lanes]
        place[...] = over_groups(slot, k, piece, group_part, k)
        for step in range(1, chips):
            remote(place, place, grad_send.at[2, k], grad_recv.at[2, k], at(other=chip_peer(step))).start()

    def to_column(k):
        block, diagonal, helper = roles(k)

        @pl.when(section == helper)
        def _():
            wait_for(section_part.at[k, :, pl.ds(0, sections - 1)], grad_recv.at[1, k])
            reduce_tile(k, 0, section)
            reduce_tile(k, 1, diagonal)

        @pl.when((section != helper) & (section != diagonal))
        def _():
            wait_for(section_part.at[k, 0, pl.ds(0, sections - 1)], grad_recv.at[1, k])
            reduce_tile(k, 0, section)

    def column_part(k, tiles):
        return whole.at[k, :, 0, 0, pl.ds(0, 16 * (chips - 1)), pl.ds(0, half * tiles)]

    def hand_over(k, index, block):
        place = whole.at[k, :, :, core, tile(index)]
        remote(place, place, grad_send.at[3, k], grad_recv.at[3, k], at(other_section=block)).start()

    def to_owner(k):
        block, diagonal, helper = roles(k)

        @pl.when(section == helper)
        def _():
            wait_for(column_part(k, 2), grad_recv.at[2, k])
            hand_over(k, section, block)
            hand_over(k, diagonal, block)

        @pl.when((section != helper) & (section != diagonal))
        def _():
            wait_for(column_part(k, 1), grad_recv.at[2, k])

            @pl.when(section != block)
            def _():
                hand_over(k, section, block)

    def to_sections_all(k):
        sum_cores(k)
        section_part[k, 0, section] = own_part[k, :, tile(section)]
        for step in range(1, sections):
            other = lax.rem(section + step, sections)
            send_tile(k, other, 0, other)

    def to_column_all(k):
        wait_for(section_part.at[k, 0, pl.ds(0, sections - 1)], grad_recv.at[1, k])
        reduce_tile(k, 0, section)

    def to_all(k):
        wait_for(column_part(k, 1), grad_recv.at[2, k])
        place = whole.at[k, :, :, core, tile(section)]
        for step in range(1, sections):
            other = lax.rem(section + step, sections)
            remote(place, place, grad_send.at[3, k], grad_recv.at[3, k], at(other_section=other)).start()

    def share(k):
        wait_for(whole.at[k, :, :, 0, pl.ds(0, 16 * (sections - 1))], grad_recv.at[3, k])
        place = whole.at[k, :, :, core]
        remote(place, place, grad_send.at[4, k], grad_recv.at[4, k], at(other=sibling)).start()

    def owner_share(k):
        @pl.when(section == block_of(k))
        def _():
            share(k)

    def shared(k):
        wait_for(whole.at[k, :, :, 0], grad_recv.at[4, k])

    def backwards(first, last, act):
        def step(number, unused):
            act(first - number)
            return 0

        lax.fori_loop(0, first - last + 1, step, 0)

    def when_due(k, act):
        @pl.when(k <= stages - 1)
        def _():
            act(k)

    def start_norm(stage, number, grads):
        value = halves[stage, number]
        grads = grads * twice_slope_of_half(value)
        held[number] = grads
        return jnp.sum(grads, axis=0, keepdims=True), jnp.sum(grads * value, axis=0, keepdims=True)

    def send_sums(stage, parts, gain, bias):
        firsts, seconds = zip(*parts)
        first = 0.5 * total_of(firsts)
        send_stats(stages - 1 + stage, first, (total_of(seconds) - bias * first) / gain)

    def norm_factors(stage, gain, bias):
        first, second = take_stats(stages - 1 + stage)
        first = jnp.sum(first, axis=0, keepdims=True)
        second = jnp.sum(second, axis=0, keepdims=True)
        totals[section, stage, 0:1] = first
        totals[section, stage, 1:2] = second
        first = first * (1.0 / count)
        second = second * (1.0 / count)
        scale = scales[stage]
        return 0.5 * gain * scale, 2.0 * scale * second, scale * (gain * first - bias * second)

    def end_norm(stage, number, factors):
        by_grads, by_halves, constant = factors
        put_shifted(
            shifted.at[number], held[number] * by_grads - halves[stage, number] * by_halves - constant, channels
        )

    def passed(number, index):
        return conv_transposed(
            shifted.at[number], lambda tap: weights[index, channels * tap : channels * (tap + 1), :], channels
        )

    def during(stage):
        when_due(stage + 2, to_sections)
        weight_grad(stage + 1, kept.at[stage])
        when_due(stage + column_lag, to_column)
        when_due(stage + owner_lag, to_owner)

    for step in range(1, chips):
        wait_for(upstream.at[0], cot_recv.at[step])
        wait_for(upstream.at[0], cot_send.at[step])
    def take_gains(s):
        @pl.when(s > 0)
        def _():
            gains[0:1] = vectors[jnp.maximum(s - 1, 0), 2:3]
            gains[1:2] = vectors[jnp.maximum(s - 1, 0), 3:4]

        @pl.when(s == 0)
        def _():
            gains[0:1] = unite_gain[...]
            gains[1:2] = unite_bias[...]

    take_gains(blocks)
    send_sums(
        stages - 1,
        [
            start_norm(stages - 1, number, upstream[number].astype(f32))
            for number in range(chips)
        ],
        gains[0:1], gains[1:2],
    )

    def block_back(back, unused):
        s = blocks - 1 - back
        stage = 2 * s + 1

        def vector(number):
            return vectors[s, number : number + 1]

        @pl.when(back > 0)
        def _():
            during(stage + 1)

        factors = norm_factors(stage + 1, vector(2), vector(3))
        parts = []
        for number in range(chips):
            end_norm(stage + 1, number, factors)
            parts.append(start_norm(stage, number, passed(number, 2 * s + 1)))
        send_sums(stage, parts, vector(0), vector(1))
        during(stage)
        take_gains(s)
        factors = norm_factors(stage, vector(0), vector(1))
        parts = []
        for number in range(chips):
            end_norm(stage, number, factors)
            grads = (upstream[number].astype(f32) + passed(number, 2 * s)).astype(bf16)
            upstream[number] = grads
            parts.append(start_norm(stage - 1, number, grads.astype(f32)))
        send_sums(stage - 1, parts, gains[0:1], gains[1:2])
        return 0

    lax.fori_loop(0, blocks, block_back, 0)

    during(0)
    for step in range(1, chips):
        wait_for(lidars.at[0], lidar_recv.at[step])
        wait_for(cameras.at[0], camera_recv.at[step])
    factors = norm_factors(0, unite_gain[...], unite_bias[...])
    for number in range(chips):
        end_norm(0, number, factors)
    weight_grad(0, lidars)
    to_sections(1)
    held_cameras = [cameras[number] for number in range(chips)]
    for i in range(3):
        for j in range(3):
            taps = total_of(
                lax.dot_general(
                    held_cameras[number],
                    shifted[number, side * (2 - i) : side * (2 - i) + cells, lateral(j)],
                    transposed_lhs,
                    preferred_element_type=f32,
                )
                for number in range(chips)
            ).astype(bf16)
            flat[cam * (3 * i + j) : cam * (3 * i + j + 1)] = taps[0:cam]
    quarter = flat_rows // 4
    kept_rows = pl.ds(pl.multiple_of(row_half * (2 * quarter) + core * quarter, 16), quarter)
    sent_rows = pl.ds(pl.multiple_of(row_half * (2 * quarter) + (1 - core) * quarter, 16), quarter)
    extra = stages
    remote(
        flat.at[sent_rows], flat_core, grad_send.at[0, extra], grad_recv.at[0, extra], at(other=sibling)
    ).start()
    to_sections_all(0)
    backwards(min(column_lag - 1, stages - 1), 2, to_column)
    for step in range(1, sections):
        remote(
            totals.at[section], totals.at[section], total_send, total_recv,
            at(other_section=lax.rem(section + step, sections)),
        ).start()
    own = shifted.at[chip]
    pooled_grad = conv_transposed(
        own, lambda tap: unite_weight[united_in * tap + channels : united_in * (tap + 1), :], channels
    ).astype(bf16)

    wait_for(flat_core, grad_recv.at[0, extra])
    flat_own[...] = (flat[kept_rows].astype(f32) + flat_core[...].astype(f32)).astype(bf16)
    flat_section[section] = flat_own[flat48]
    for step in range(1, sections):
        other = lax.rem(section + step, sections)
        remote(
            flat_own.at[pl.ds(pl.multiple_of(other * 48, 16), 48)], flat_section.at[section],
            grad_send.at[1, extra], grad_recv.at[1, extra], at(other_section=other),
        ).start()
    lidar_grad[...] = conv_transposed(
        own, lambda tap: unite_weight[united_in * tap : united_in * tap + channels, :], channels
    )
    to_column(1)

    context_grad[...] = lax.dot_general(pooled_grad, histogram[...], transposed_lhs, preferred_element_type=f32)
    table = lax.dot_general(
        context_ref[...], pooled_grad, (((0,), (1,)), ((), ())), preferred_element_type=f32
    )
    wanted = places[...].T.astype(jnp.int32)
    within = lax.rem(wanted, half)
    low = jnp.take_along_axis(table[:, 0:half], within, axis=1)
    high = jnp.take_along_axis(table[:, half : 2 * half], within, axis=1)
    chance_grad = jnp.where(wanted < half, low, high).T
    chance = probability[...]
    places[...] = chance * (chance_grad - jnp.sum(chance_grad * chance, axis=0, keepdims=True))

    def store_bin(number, unused):
        logit_grad[number] = places[pl.ds(number, 1)]
        return 0

    lax.fori_loop(0, bins, store_bin, 0)

    to_column_all(0)
    wait_for(flat_section.at[pl.ds(0, sections - 1)], grad_recv.at[1, extra])
    piece = total_of(flat_section[number].astype(f32) for number in range(sections)).astype(bf16)
    flat_place = flat_whole.at[row_half, core, flat48, lanes]
    flat_place[...] = over_groups(0, 0, piece, flat_group, extra)
    for step in range(1, chips):
        remote(
            flat_place, flat_place, grad_send.at[2, extra], grad_recv.at[2, extra], at(other=chip_peer(step))
        ).start()
    backwards(min(owner_lag - 1, stages - 1), 1, to_owner)
    to_all(0)
    wait_for(flat_whole.at[0, 0, pl.ds(0, 48 * (chips - 1)), pl.ds(0, half)], grad_recv.at[2, extra])
    flat_rows_place = flat_whole.at[:, core, flat48]
    for step in range(1, sections):
        other = lax.rem(section + step, sections)
        remote(
            flat_rows_place, flat_rows_place, grad_send.at[3, extra], grad_recv.at[3, extra],
            at(other_section=other),
        ).start()

    backwards(stages - 1, 1, owner_share)
    share(0)
    wait_for(flat_whole.at[:, 0, pl.ds(0, 48 * (sections - 1))], grad_recv.at[3, extra])
    flat_half = flat_whole.at[:, core]
    remote(flat_half, flat_half, grad_send.at[4, extra], grad_recv.at[4, extra], at(other=sibling)).start()

    wait_for(totals.at[pl.ds(0, sections - 1)], total_recv)
    def summed(stage, row):
        return total_of(totals[number, stage, row : row + 1] for number in range(sections))

    small_out[0] = summed(0, 1)
    small_out[1] = summed(0, 0)
    for number in range(2):
        small_out[2 + 2 * number] = summed(2 * section + 1 + number, 1)
        small_out[3 + 2 * number] = summed(2 * section + 1 + number, 0)
    shared(2 * section + 1)
    shared(2 * section + 2)
    first_copy = pltpu.make_async_copy(whole.at[2 * section + 1], first_out, local_sem.at[5])
    second_copy = pltpu.make_async_copy(whole.at[2 * section + 2], second_out, local_sem.at[6])
    first_copy.start()
    second_copy.start()
    shared(0)
    unite_done = pltpu.make_async_copy(whole.at[0], unite_out, local_sem.at[7])
    unite_done.start()
    wait_for(flat_whole.at[:, 0], grad_recv.at[4, extra])
    camera_done = pltpu.make_async_copy(flat_whole, camera_out, local_sem.at[8])
    camera_done.start()

    wait_for(unite_slots.at[pl.ds(0, peers - 1)], unite_send)
    for step in range(1, chips):
        wait_for(gathered.at[0], raw_send.at[step])
        wait_for(lidars.at[0], lidar_send.at[step])
        wait_for(cameras.at[0], camera_send.at[step])
    for number in range(4):
        wait_for(weights.at[0, part], weight_send.at[number])
    for number in range(2):
        wait_for(weights.at[0, part], relay_send.at[number])
    wait_for(vectors.at[pl.ds(0, sections - 1)], vector_send)
    wait_for(totals.at[pl.ds(0, sections - 1)], total_send)

    def drain_stats(event, unused):
        wait_for(slots.at[event, pl.ds(0, members - 1)], stat_send.at[event])
        return 0

    lax.fori_loop(0, 2 * stages - 1, drain_stats, 0)

    def drain_weights(index, unused):
        @pl.when(section != lax.div(index, 2))
        def _():
            wait_for(weights.at[index, part], pass_send.at[index])
        return 0

    lax.fori_loop(0, 2 * blocks, drain_weights, 0)

    def drain_grads(k, unused):
        block, diagonal, helper = roles(k)
        own_tiles = section_part.at[k, 0]
        column = whole.at[k, :, :, 0]
        wait_for(core_part.at[k], grad_send.at[0, k])

        @pl.when(section == diagonal)
        def _():
            wait_for(own_tiles.at[pl.ds(0, 4)], grad_send.at[1, k])

        @pl.when(section == helper)
        def _():
            wait_for(own_tiles.at[pl.ds(0, 2)], grad_send.at[1, k])
            wait_for(column_part(k, 2), grad_send.at[2, k])
            wait_for(column.at[:, :, pl.ds(0, 32)], grad_send.at[3, k])

        @pl.when((section != helper) & (section != diagonal))
        def _():
            wait_for(own_tiles.at[pl.ds(0, 3)], grad_send.at[1, k])
            wait_for(column_part(k, 1), grad_send.at[2, k])

            @pl.when(section != block)
            def _():
                wait_for(column.at[:, :, pl.ds(0, 16)], grad_send.at[3, k])

        @pl.when(section == block)
        def _():
            wait_for(column, grad_send.at[4, k])

        if groups > 1:
            @pl.when(section != diagonal)
            def _():
                wait_for(group_part.at[k, 0, pl.ds(0, groups - 1)], group_send.at[0, k])

            @pl.when(section == helper)
            def _():
                wait_for(group_part.at[k, 1, pl.ds(0, groups - 1)], group_send.at[1, k])
        return 0

    lax.fori_loop(1, stages, drain_grads, 0)
    wait_for(core_part.at[0], grad_send.at[0, 0])
    wait_for(section_part.at[0, 0, pl.ds(0, sections - 1)], grad_send.at[1, 0])
    wait_for(column_part(0, 1), grad_send.at[2, 0])
    if groups > 1:
        wait_for(group_part.at[0, 0, pl.ds(0, groups - 1)], group_send.at[0, 0])
    wait_for(whole.at[0, :, :, 0, pl.ds(0, 16 * (sections - 1))], grad_send.at[3, 0])
    wait_for(whole.at[0, :, :, 0], grad_send.at[4, 0])
    wait_for(flat_core, grad_send.at[0, extra])
    wait_for(flat_section.at[pl.ds(0, sections - 1)], grad_send.at[1, extra])
    wait_for(flat_whole.at[0, 0, pl.ds(0, 48 * (chips - 1)), pl.ds(0, half)], grad_send.at[2, extra])
    wait_for(flat_whole.at[:, 0, pl.ds(0, 48 * (sections - 1))], grad_send.at[3, extra])
    wait_for(flat_whole.at[:, 0], grad_send.at[4, extra])
    if groups > 1:
        wait_for(flat_group.at[0, 0, pl.ds(0, groups - 1)], group_send.at[0, extra])
    first_copy.wait()
    second_copy.wait()
    unite_done.wait()
    camera_done.wait()


def widen(cam, *refs):
    held_in, outs, narrow, full = refs[0:9], refs[9:22], refs[22:31], refs[31:34]
    in_sem, out_sem, plain_sem = refs[34:37]
    loads = [pltpu.make_async_copy(a, b, in_sem.at[n]) for n, (a, b) in enumerate(zip(held_in, narrow))]
    for load in loads:
        load.start()
    passed = []
    channels = full[1].shape[-1]

    def store(number, row):
        taps = pl.ds(3 * row, 3)
        return pltpu.make_async_copy(full[number].at[taps], outs[10 + number].at[taps], out_sem.at[number, row])

    loads[0].wait()
    loads[1].wait()

    def unite_tap(tap, unused):
        full[0][tap, 0:channels] = narrow[0][tap].astype(f32)
        rows = pl.ds(pl.multiple_of(cam * tap, 16), cam)
        full[0][tap, channels : channels + cam] = narrow[1][rows].astype(f32)
        return 0

    for row in range(3):
        lax.fori_loop(3 * row, 3 * row + 3, unite_tap, 0)
        store(0, row).start()
    for number in (1, 2):
        loads[number + 1].wait()

        def block_tap(tap, unused):
            full[number][tap] = narrow[number + 1][tap].astype(f32)
            return 0

        for row in range(3):
            lax.fori_loop(3 * row, 3 * row + 3, block_tap, 0)
            store(number, row).start()
    for number in range(4, 9):
        loads[number].wait()
    for number in range(10):
        source = narrow[4 + number] if number < 4 else narrow[8].at[number - 4]
        passed.append(pltpu.make_async_copy(source, outs[number], plain_sem.at[number]))
        passed[-1].start()
    for number in range(3):
        for row in range(3):
            store(number, row).wait()
    for copy in passed:
        copy.wait()


def body(
    lidar, context, depth_logits, cell_index, unite_weight, unite_gain, unite_bias, first_weight, second_weight,
    first_gain, first_bias, second_gain, second_bias, cotangent,
):
    peers = lax.axis_size("dp")
    sections = lax.axis_size("section")
    section = lax.axis_index("section")
    channels = cotangent.shape[-1]
    pixels, bins = depth_logits.shape[2:]
    cam = context.shape[-1]
    united_in = unite_weight.shape[1]
    blocks = sections
    stages = 2 * blocks + 1
    events = 2 * stages - 1
    groups = peers // (2 * chips)
    taken = 9 * channels

    vmem = pl.BlockSpec(memory_space=pltpu.VMEM)
    hbm = pl.BlockSpec(memory_space=pltpu.HBM)
    shape = jax.ShapeDtypeStruct
    dma = pltpu.SemaphoreType.DMA
    results = pl.pallas_call(
        functools.partial(kernel, peers, sections),
        out_shape=(
            shape((cells, channels), f32),
            shape((cells, channels), f32),
            shape((cam, pixels), f32),
            shape((bins, 1, pixels), f32),
            shape((9, 2, 2, 64, channels), bf16),
            shape((2, 2, flat_rows // 4, channels), bf16),
            shape((9, 2, 2, 64, channels), bf16),
            shape((9, 2, 2, 64, channels), bf16),
            shape((6, 1, channels), f32),
        ),
        in_specs=[hbm, vmem, vmem, vmem, hbm, vmem, vmem, hbm, hbm, vmem, vmem, vmem, vmem, hbm],
        out_specs=[vmem, vmem, vmem, vmem, hbm, hbm, hbm, hbm, vmem],
        scratch_shapes=[
            pltpu.VMEM((2 * blocks, taken, channels), bf16),
            pltpu.VMEM((9 * united_in, channels), bf16),
            pltpu.VMEM((blocks, 4, channels), f32),
            pltpu.VMEM((cells + 2 * side, 3 * wide), bf16),
            pltpu.VMEM((chips, cells + 2 * side, 3 * channels), bf16),
            pltpu.VMEM((chips, cells, channels), bf16),
            pltpu.VMEM((2 * blocks, chips, cells, channels), bf16),
            pltpu.VMEM((stages, chips, cells, channels), f32),
            pltpu.VMEM((stages + 1, 1, channels), f32),
            pltpu.VMEM((chips, cells, channels), f32),
            pltpu.VMEM((chips, cells, channels), bf16),
            pltpu.VMEM((chips, cells, channels), bf16),
            pltpu.VMEM((chips, cells, channels), bf16),
            pltpu.VMEM((chips, cells, half), bf16),
            pltpu.VMEM((events, 2, channels), f32),
            pltpu.VMEM((events, 2 * groups, 2, channels), f32),
            pltpu.VMEM((2, channels), f32),
            pltpu.VMEM((peers, 2, channels), f32),
            pltpu.VMEM((half, pixels), f32),
            pltpu.VMEM((half, pixels), f32),
            pltpu.VMEM((cells, pixels), bf16),
            pltpu.VMEM((stages, 9, 2, 64, half), bf16),
            pltpu.VMEM((stages, 9, 64, half), bf16),
            pltpu.VMEM((stages, 9, 64, half), bf16),
            pltpu.VMEM((stages, 2, sections, 9, 16, half), bf16),
            pltpu.VMEM((stages, 9, 2, 2, 64, channels), bf16),
            pltpu.VMEM((flat_rows, half), bf16),
            pltpu.VMEM((flat_rows // 4, half), bf16),
            pltpu.VMEM((flat_rows // 4, half), bf16),
            pltpu.VMEM((sections, 48, half), bf16),
            pltpu.VMEM((2, 2, flat_rows // 4, channels), bf16),
            pltpu.VMEM((sections, stages, 2, channels), f32),
            pltpu.VMEM((2, channels), f32),
            pltpu.VMEM((stages if groups > 1 else 1, 2, groups, 9, 16, half), bf16),
            pltpu.VMEM((1, 1, groups, 48, half), bf16),
            dma((9,)), dma, dma, dma((events,)), dma((events,)), dma((chips,)), dma((chips,)), dma((chips,)),
            dma((chips,)), dma((chips,)), dma((chips,)), dma((chips,)), dma((chips,)), dma((4,)),
            dma((2 * blocks,)), dma((2,)), dma((2 * blocks,)), dma((2 * blocks,)), dma, dma,
            dma((5, stages + 1)), dma((5, stages + 1)), dma, dma, dma((2, stages + 1)), dma((2, stages + 1)),
        ],
        compiler_params=pltpu.CompilerParams(
            collective_id=0, has_side_effects=True, vmem_limit_bytes=60 << 20
        ),
    )(
        lidar.reshape(cells, channels), context.reshape(pixels, cam).T, depth_logits.reshape(pixels, bins).T,
        jnp.transpose(cell_index, (0, 3, 1, 2)).reshape(bins, 1, pixels), unite_weight.reshape(-1, channels),
        unite_gain[None], unite_bias[None], first_weight.reshape(taken, channels),
        second_weight.reshape(taken, channels), first_gain, first_bias, second_gain, second_bias,
        cotangent.reshape(-1, cells, channels),
    )

    act, lidar_grad, context_grad, logit_grad, *small, unite_whole, first_whole, second_whole = pl.pallas_call(
        functools.partial(widen, cam),
        out_shape=(
            shape((cells, channels), f32),
            shape((cells, channels), f32),
            shape((cam, pixels), f32),
            shape((bins, 1, pixels), f32),
            *[shape((1, channels), f32)] * 6,
            shape((9, united_in, channels), f32),
            shape((9, channels, channels), f32),
            shape((9, channels, channels), f32),
        ),
        in_specs=[hbm] * 9,
        out_specs=[hbm] * 13,
        scratch_shapes=[
            pltpu.VMEM((9, channels, channels), bf16),
            pltpu.VMEM((flat_rows, channels), bf16),
            pltpu.VMEM((9, channels, channels), bf16),
            pltpu.VMEM((9, channels, channels), bf16),
            pltpu.VMEM((cells, channels), f32),
            pltpu.VMEM((cells, channels), f32),
            pltpu.VMEM((cam, pixels), f32),
            pltpu.VMEM((bins, 1, pixels), f32),
            pltpu.VMEM((6, 1, channels), f32),
            pltpu.VMEM((9, united_in, channels), f32),
            pltpu.VMEM((9, channels, channels), f32),
            pltpu.VMEM((9, channels, channels), f32),
            dma((9,)), dma((3, 3)), dma((10,)),
        ],
        compiler_params=pltpu.CompilerParams(vmem_limit_bytes=60 << 20),
    )(
        results[4].reshape(9, channels, channels), results[5].reshape(flat_rows, channels),
        results[6].reshape(9, channels, channels), results[7].reshape(9, channels, channels), *results[0:4], results[8],
    )
    return (
        act.reshape(lidar.shape),
        lidar_grad.reshape(lidar.shape),
        context_grad.T.reshape(context.shape),
        jnp.transpose(logit_grad.reshape(1, bins, 1, pixels), (0, 2, 3, 1)),
        unite_whole,
        small[0].reshape(channels),
        small[1].reshape(channels),
        first_whole.reshape(first_weight.shape),
        second_whole.reshape(second_weight.shape),
        *small[2:6],
    )


def solution(mesh):
    split, by_dp = P("section"), P("section", "dp")
    in_specs = (by_dp, by_dp, by_dp, by_dp, P(), P(), P(), split, split, split, split, split, split, P(None, "dp"))
    out_specs = (by_dp, by_dp, by_dp, by_dp, P(), P(), P(), split, split, split, split, split, split)
    return jax.shard_map(body, mesh=mesh, in_specs=in_specs, out_specs=out_specs, check_vma=False)
```
